32 devices in a mesh: dp: 8 (over z, y), tensor: 4 (over x, core).
Axes of the slice: x: 2, y: 2, z: 4, core: 2. Of those that a mesh axis runs over, the one named last changes fastest.
Arguments:
- patch_tokens: bfloat16 [64, 196, 768], P('dp', 'tensor'), may hold values from -6 to 6
- class_tokens: bfloat16 [24, 768], P('dp'), may hold values from -6 to 6
- frame_counts: int32 [8, 3], P('dp'), may hold values from 1 to 4, 8 in all within a row
- patch_cotangent: bfloat16 [64, 196, 768], P('dp', 'tensor'), may hold values from -6 to 6
- class_cotangent: bfloat16 [24, 768], P('dp'), may hold values from -6 to 6
- temporal_in: bfloat16 [2, 768, 2304], replicated, may hold values from -0.21875 to 0.21875
- temporal_out: bfloat16 [2, 768, 768], replicated, may hold values from -0.3125 to 0.3125
- temporal_mix: bfloat16 [2, 768, 768], replicated, may hold values from -0.21875 to 0.21875
- spatial_in: bfloat16 [2, 768, 2304], replicated, may hold values from -0.21875 to 0.21875
- spatial_out: bfloat16 [2, 768, 768], replicated, may hold values from -1.75 to 1.75
- hidden_up: bfloat16 [2, 768, 3072], P(None, None, 'tensor'), may hold values from -0.21875 to 0.21875
- hidden_down: bfloat16 [2, 3072, 768], P(None, 'tensor'), may hold values from -0.3125 to 0.3125
- norm_gain: float32 [2, 3, 768], replicated, may hold values from 0.5 to 1.5
- norm_shift: float32 [2, 3, 768], replicated, may hold values from -3 to 3
Outputs:
- patch_output: bfloat16 [64, 196, 768], P('dp', 'tensor')
- class_output: bfloat16 [24, 768], P('dp')
- patch_grad: float32 [64, 196, 768], P('dp', 'tensor')
- class_grad: float32 [24, 768], P('dp')
- grad_temporal_in: float32 [2, 768, 2304], P(None, 'dp')
- grad_temporal_out: float32 [2, 768, 768], P(None, 'dp')
- grad_temporal_mix: float32 [2, 768, 768], P(None, 'dp')
- grad_spatial_in: float32 [2, 768, 2304], P(None, 'dp')
- grad_spatial_out: float32 [2, 768, 768], P(None, 'dp')
- grad_hidden_up: float32 [2, 768, 3072], P(None, 'dp', 'tensor')
- grad_hidden_down: float32 [2, 3072, 768], P(None, 'tensor', 'dp')
- grad_norm_gain: float32 [2, 3, 768], P(None, None, 'dp')
- grad_norm_shift: float32 [2, 3, 768], P(None, None, 'dp')
The draws below stay inside these ranges and needn't reach their ends.
Inputs may be any that keep to these rules, and one draw needn't show every extreme that they name: `frame_counts`: each row sums to 8, and in each row the longest clip has exactly 4 frames.
All inputs are finite; a program needn't handle non-finite values.
Results may differ from the reference program's by a relative error of at most 0.02.
Values may be sent and summed in bfloat16 or wider, within the bound.
No kernel may reach another device: no remote copies, remote signals or barrier semaphores. Data moves between devices by JAX's collectives and lax.ppermute only.
A program may use at most 320 MiB of HBM per device.

```python
import math
import jax
import jax.numpy as jnp
import numpy as np
from jax import lax

D = 768
HEADS = 12
FF = 3072
PATCHES = 196
LAYERS = 2
FR_DEV = 8
CLIP_MOST = 4
CLIPS_DEV = 3
FRAMES = 64
CLIPS = 24
N_DP = 8


def levels(stream_key, dims, shards, least, high):
    loudness, own = 1.0, jax.random.fold_in(stream_key, 6)
    for dim, blocks in shards:
        steps = jnp.exp(jax.random.uniform(jax.random.fold_in(own, dim), (blocks,), jnp.float32, least / len(shards), high / len(shards)))
        loudness = loudness * jnp.repeat(steps, dims[dim] // blocks).reshape([-1 if axis == dim else 1 for axis in range(len(dims))])
    return loudness


def split_up(count, total, reach, skew):
    weights = [(1 << 20) // math.isqrt(standing ** skew) + 1 for standing in range(2, count + 1)]
    rest, holding = total - reach - (count - 1), [1] * (count - 1)
    while rest > 0:
        movable = [i for i in range(count - 1) if holding[i] < reach]
        whole, left = sum([weights[i] for i in movable]), rest
        for i in movable:
            extra = min(reach - holding[i], max(1, left * weights[i] // whole), rest)
            holding[i] = holding[i] + extra
            rest = rest - extra
    return np.array([reach] + holding)


def uneven_parts(stream_key, amount, total, most, slope):
    if amount == 2:
        one = jax.random.randint(stream_key, (), max(1, total - most), min(most, total - 1) + 1)
        return jnp.stack([one, total - one])
    lengths = jnp.asarray(split_up(amount, total, most, slope), jnp.int32)
    pairs = (amount - 1) // 2
    source_of, receiver = lengths[1:1 + 2 * pairs:2], lengths[2:2 + 2 * pairs:2]
    slack = jnp.minimum(source_of - 1, most - receiver)
    passed = jax.random.randint(jax.random.fold_in(stream_key, 1), (pairs,), 0, 1 << 20) % (slack + 1)
    lengths = lengths.at[1:1 + 2 * pairs:2].set(source_of - passed).at[2:2 + 2 * pairs:2].set(receiver + passed)
    return lengths[jax.random.permutation(jax.random.fold_in(stream_key, 2), amount)]


def scatter_about(key, dims, deviation, bound, pieces=(), kind=jnp.bfloat16):
    drawn = deviation * jax.random.normal(key, dims, jnp.float32)
    if pieces:
        drawn = drawn * levels(key, dims, pieces, -0.22, 0.18)
    return jnp.clip(drawn, -bound, bound).astype(kind)


def setup_inputs(seed: int = 0) -> dict:
    keys = jax.random.split(jax.random.key(seed), 15)
    return {
        "patch_tokens": scatter_about(keys[0], (FRAMES, PATCHES, D), 1.0, 6.0, ((0, 8), (1, 4))),
        "class_tokens": scatter_about(keys[1], (CLIPS, D), 1.0, 6.0, ((0, 8),)),
        "frame_counts": jax.vmap(lambda own: uneven_parts(own, CLIPS_DEV, FR_DEV, CLIP_MOST, 2))(jax.random.split(keys[2], N_DP)).reshape((N_DP, CLIPS_DEV)).astype(jnp.int32),
        "patch_cotangent": scatter_about(keys[3], (FRAMES, PATCHES, D), 1.0, 6.0, ((0, 8), (1, 4))),
        "class_cotangent": scatter_about(keys[4], (CLIPS, D), 1.0, 6.0, ((0, 8),)),
        "temporal_in": scatter_about(keys[5], (LAYERS, D, 3 * D), D ** -0.5, 0.21875),
        "temporal_out": scatter_about(keys[6], (LAYERS, D, D), (D // 2) ** -0.5, 0.3125),
        "temporal_mix": scatter_about(keys[7], (LAYERS, D, D), D ** -0.5, 0.21875),
        "spatial_in": scatter_about(keys[8], (LAYERS, D, 3 * D), D ** -0.5, 0.21875),
        "spatial_out": scatter_about(keys[9], (LAYERS, D, D), (D // 64) ** -0.5, 1.75),
        "hidden_up": scatter_about(keys[10], (LAYERS, D, FF), D ** -0.5, 0.21875, ((2, 4),)),
        "hidden_down": scatter_about(keys[11], (LAYERS, FF, D), (FF // 8) ** -0.5, 0.3125, ((1, 4),)),
        "norm_gain": jnp.clip(1.0 + 0.1 * jax.random.normal(keys[12], (LAYERS, 3, D), jnp.float32), 0.5, 1.5),
        "norm_shift": scatter_about(keys[13], (LAYERS, 3, D), 0.5, 3.0, (), jnp.float32),
    }


EPS = 1e-06
HIGH = lax.Precision.HIGHEST

@jax.custom_vjp
def low(v):
    return lax.optimization_barrier(v.astype(jnp.bfloat16)).astype(jnp.float32)

@jax.custom_vjp
def low_back(v):
    return v

def low_keep(v):
    return (low(v), None)

def low_pass(kept, grad):
    return (grad,)

def back_keep(v):
    return (v, None)

def back_low(kept, grad):
    return (low(grad),)
low.defvjp(low_keep, low_pass)
low_back.defvjp(back_keep, back_low)

def both(values):
    return low(low_back(values))

def matmul(left, right):
    return jnp.matmul(left, right, precision=HIGH)

def layer_norm(values, gain, shift):
    mean = lax.optimization_barrier(jnp.mean(values, -1, keepdims=True))
    centred = values - mean
    spread = lax.optimization_barrier(jnp.mean(centred * centred, -1, keepdims=True))
    return centred * lax.rsqrt(spread + EPS) * gain + shift

def softmax_rows(scores):
    top = lax.optimization_barrier(jnp.max(scores, -1, keepdims=True))
    raised = jnp.exp(scores - top)
    return raised / lax.optimization_barrier(jnp.sum(raised, -1, keepdims=True))

def block(weights, patch_rows, class_rows, member, same, counts):
    temporal_in, temporal_out, temporal_mix, spatial_in, spatial_out, hidden_up, hidden_down, gains, shifts = weights
    frames = patch_rows.shape[0]
    width = patch_rows.shape[2]
    head_size = width // HEADS
    scale = head_size ** (-0.5)
    normed = low(layer_norm(patch_rows, gains[0], shifts[0]))
    triple = both(matmul(normed, temporal_in)).reshape(frames, PATCHES, 3, HEADS, head_size)
    scores = low_back(jnp.einsum('fphd,gphd->phfg', triple[:, :, 0], triple[:, :, 1], precision=HIGH) * scale)
    scores = jnp.where(same, scores, -1e+30)
    attend = low(softmax_rows(scores))
    mixed = jnp.einsum('phfg,gphd->fphd', attend, triple[:, :, 2], precision=HIGH)
    mixed = both(mixed.reshape(frames, PATCHES, width))
    projected = both(matmul(mixed, temporal_out))
    after_time = patch_rows + low_back(matmul(projected, temporal_mix))
    normed_patch = low(layer_norm(after_time, gains[1], shifts[1]))
    normed_class = low(layer_norm(class_rows, gains[1], shifts[1]))
    triple_patch = both(matmul(normed_patch, spatial_in)).reshape(frames, PATCHES, 3, HEADS, head_size)
    triple_class = both(matmul(normed_class, spatial_in))
    triple_frame = matmul(member, triple_class).reshape(frames, 1, 3, HEADS, head_size)
    joined = jnp.concatenate([triple_frame, triple_patch], 1)
    scores = low_back(jnp.einsum('fqhd,fkhd->fhqk', joined[:, :, 0], joined[:, :, 1], precision=HIGH) * scale)
    attend = low(softmax_rows(scores))
    mixed = jnp.einsum('fhqk,fkhd->fqhd', attend, joined[:, :, 2], precision=HIGH)
    mixed = mixed.reshape(frames, PATCHES + 1, width)
    patch_mixed = both(mixed[:, 1:])
    class_frames = low_back(mixed[:, 0])
    class_mean = low(matmul(member.T, class_frames) / counts[:, None])
    after_space = after_time + low_back(matmul(patch_mixed, spatial_out))
    class_space = class_rows + low_back(matmul(class_mean, spatial_out))
    rows = jnp.concatenate([after_space.reshape(frames * PATCHES, width), class_space], 0)
    normed_rows = low(layer_norm(rows, gains[2], shifts[2]))
    hidden = low_back(matmul(normed_rows, hidden_up))
    active = low(jax.nn.gelu(hidden, approximate=False))
    rows = rows + low_back(matmul(active, hidden_down))
    return (rows[:frames * PATCHES].reshape(frames, PATCHES, width), rows[frames * PATCHES:])

def reference(patch_tokens, class_tokens, frame_counts, patch_cotangent, class_cotangent, temporal_in, temporal_out, temporal_mix, spatial_in, spatial_out, hidden_up, hidden_down, norm_gain, norm_shift):
    groups = frame_counts.shape[0]
    clips = frame_counts.shape[1]
    frames = patch_tokens.shape[0] // groups
    width = patch_tokens.shape[2]
    ends = jnp.cumsum(frame_counts, 1).astype(jnp.int32)
    frame_index = jnp.arange(frames, dtype=jnp.int32)
    clip_of = lax.optimization_barrier(jnp.sum((frame_index[None, :, None] >= ends[:, None, :]).astype(jnp.int32), 2)).astype(jnp.int32)
    member = (clip_of[:, :, None] == jnp.arange(clips, dtype=jnp.int32)[None, None, :]).astype(jnp.float32)
    same = clip_of[:, :, None] == clip_of[:, None, :]
    counts = frame_counts.astype(jnp.float32)
    patch_in = patch_tokens.astype(jnp.float32).reshape(groups, frames, PATCHES, width)
    class_in = class_tokens.astype(jnp.float32).reshape(groups, clips, width)
    weights = tuple((matrix.astype(jnp.float32) for matrix in (temporal_in, temporal_out, temporal_mix, spatial_in, spatial_out, hidden_up, hidden_down, norm_gain, norm_shift)))

    def forward(patch_start, class_start, layer_weights):

        def group(item):
            patch_rows, class_rows, member_group, same_group, counts_group = item
            for layer in range(LAYERS):
                chosen = tuple((matrix[layer] for matrix in layer_weights))
                patch_rows, class_rows = block(chosen, patch_rows, class_rows, member_group, same_group, counts_group)
            return (patch_rows, class_rows)
        return lax.map(jax.checkpoint(group), (patch_start, class_start, member, same, counts))
    outputs, pull = jax.vjp(forward, patch_in, class_in, weights)
    cotangents = (patch_cotangent.astype(jnp.float32).reshape(groups, frames, PATCHES, width), class_cotangent.astype(jnp.float32).reshape(groups, clips, width))
    grad_patch, grad_class, grad_weights = pull(cotangents)
    patch_output = outputs[0].reshape(groups * frames, PATCHES, width).astype(jnp.bfloat16)
    class_output = outputs[1].reshape(groups * clips, width).astype(jnp.bfloat16)
    return (patch_output, class_output, grad_patch.reshape(groups * frames, PATCHES, width), grad_class.reshape(groups * clips, width), grad_weights[0], grad_weights[1], grad_weights[2], grad_weights[3], grad_weights[4], grad_weights[5], grad_weights[6], grad_weights[7], grad_weights[8])
```

```python
from functools import partial
from types import SimpleNamespace

import jax
import jax.numpy as jnp
from jax import lax
from jax.sharding import PartitionSpec as P

HEADS = 12


EPS = 1e-06
HIGH = lax.Precision.HIGHEST
HALF = jnp.bfloat16
FULL = jnp.float32
NEAR = 4
TENSOR = "tensor"
DP = "dp"


def matmul(left, right):
    return jnp.dot(left, right, preferred_element_type=jnp.float32)


def matmul_back(left, right):
    return lax.dot_general(
        left, right, (((left.ndim - 1,), (1,)), ((), ())), preferred_element_type=jnp.float32
    )


def outer_sum(left, right):
    return lax.dot_general(
        left, right, (((0,), (0,)), ((), ())), preferred_element_type=jnp.float32
    )


def norm_forward(values, gain, shift):
    mean = jnp.mean(values, -1, keepdims=True)
    centred = values - mean
    inverse = lax.rsqrt(jnp.mean(centred * centred, -1, keepdims=True) + EPS)
    unit = centred * inverse
    return (unit * gain + shift, unit, inverse)


def norm_backward(grad, unit, inverse, gain):
    scaled = grad * gain
    inner = (
        scaled
        - jnp.mean(scaled, -1, keepdims=True)
        - unit * jnp.mean(scaled * unit, -1, keepdims=True)
    )
    return inner * inverse


def gelu_backward(hidden, grad):
    unused, pull = jax.vjp(partial(jax.nn.gelu, approximate=False), hidden)
    return pull(grad)[0]


def temporal_logits(queries, keys, same, scale):
    scores = jnp.einsum("fphd,gphd->phfg", queries, keys, preferred_element_type=FULL) * scale
    return jnp.where(same, scores, -1e30)


def temporal_forward(queries, keys, values, same, scale):
    scores = temporal_logits(queries, keys, same, scale)
    top = jnp.max(scores, -1, keepdims=True)
    log_total = top + jnp.log(jnp.sum(jnp.exp(scores - top), -1, keepdims=True))
    attend = jnp.exp(scores - log_total).astype(HALF)
    mixed = jnp.einsum("phfg,gphd->fphd", attend, values, preferred_element_type=FULL)
    return (mixed, log_total)


def temporal_backward(grad_mixed, queries, keys, values, log_total, same, scale):
    scores = temporal_logits(queries, keys, same, scale)
    attend = jnp.exp(scores - log_total)
    grad_attend = jnp.einsum("fphd,gphd->phfg", grad_mixed, values, preferred_element_type=FULL)
    delta = jnp.sum(attend * grad_attend, -1, keepdims=True)
    grad_score = (attend * (grad_attend - delta)).astype(HALF)
    grad_query = (
        jnp.einsum("phfg,gphd->fphd", grad_score, keys, preferred_element_type=FULL) * scale
    )
    grad_key = (
        jnp.einsum("phfg,fphd->gphd", grad_score, queries, preferred_element_type=FULL) * scale
    )
    grad_value = jnp.einsum(
        "phfg,fphd->gphd", attend.astype(HALF), grad_mixed, preferred_element_type=FULL
    )
    return (grad_query, grad_key, grad_value)


def spatial_logits(queries, keys_all, key_class, scale):
    main = jnp.einsum("fqhd,fkhd->fhqk", queries, keys_all, preferred_element_type=FULL) * scale
    side = jnp.einsum("fqhd,fhd->fhq", queries, key_class, preferred_element_type=FULL) * scale
    return (main, side)


def spatial_forward(queries, keys_all, key_class, values_all, value_class, scale):
    main, side = spatial_logits(queries, keys_all, key_class, scale)
    top = jnp.maximum(jnp.max(main, -1), side)
    total = jnp.sum(jnp.exp(main - top[..., None]), -1) + jnp.exp(side - top)
    log_total = top + jnp.log(total)
    main_prob = jnp.exp(main - log_total[..., None]).astype(HALF)
    side_prob = jnp.exp(side - log_total).astype(HALF)
    mixed = jnp.einsum("fhqk,fkhd->fqhd", main_prob, values_all, preferred_element_type=FULL)
    mixed = mixed + jnp.einsum("fhq,fhd->fqhd", side_prob, value_class, preferred_element_type=FULL)
    return (mixed, log_total)


def spatial_backward(
    grad_mixed, queries, keys_all, key_class, values_all, value_class, log_total, scale
):
    main, side = spatial_logits(queries, keys_all, key_class, scale)
    main_prob = jnp.exp(main - log_total[..., None])
    side_prob = jnp.exp(side - log_total)
    grad_main = jnp.einsum("fqhd,fkhd->fhqk", grad_mixed, values_all, preferred_element_type=FULL)
    grad_side = jnp.einsum("fqhd,fhd->fhq", grad_mixed, value_class, preferred_element_type=FULL)
    delta = jnp.sum(main_prob * grad_main, -1) + side_prob * grad_side
    score_main = (main_prob * (grad_main - delta[..., None])).astype(HALF)
    score_side = (side_prob * (grad_side - delta)).astype(HALF)
    grad_query = jnp.einsum("fhqk,fkhd->fqhd", score_main, keys_all, preferred_element_type=FULL)
    grad_query = (
        grad_query + jnp.einsum("fhq,fhd->fqhd", score_side, key_class, preferred_element_type=FULL)
    ) * scale
    grad_keys = (
        jnp.einsum("fhqk,fqhd->fkhd", score_main, queries, preferred_element_type=FULL) * scale
    )
    grad_values = jnp.einsum(
        "fhqk,fqhd->fkhd", main_prob.astype(HALF), grad_mixed, preferred_element_type=FULL
    )
    grad_key_class = (
        jnp.einsum("fhq,fqhd->fhd", score_side, queries, preferred_element_type=FULL) * scale
    )
    grad_value_class = jnp.einsum(
        "fhq,fqhd->fhd", side_prob.astype(HALF), grad_mixed, preferred_element_type=FULL
    )
    return (grad_query, grad_keys, grad_values, grad_key_class, grad_value_class)


def swap(values, axis, bit):
    size = lax.axis_size(axis)
    return lax.ppermute(values, axis, [(index, index ^ bit) for index in range(size)])


def halve(values, axis, bit, dim):
    mine = lax.axis_index(axis) // bit % 2
    keep = lax.dynamic_index_in_dim(values, mine, dim, False)
    send = lax.dynamic_index_in_dim(values, 1 - mine, dim, False)
    return keep + swap(send, axis, bit)


def join(values, axis, bit, dim):
    other = swap(values, axis, bit)
    first = lax.axis_index(axis) // bit % 2 == 0
    return jnp.where(
        first,
        jnp.concatenate([values, other], dim),
        jnp.concatenate([other, values], dim),
    )


def scatter_dp(values):
    far = values.shape[0]
    if far > NEAR:
        values = values.reshape((-1,) + values.shape[3:])
        return lax.psum_scatter(values, DP, scatter_dimension=0, tiled=True).astype(FULL)
    values = halve(values, DP, 1, 1)
    place = lax.axis_index(DP) // 2
    total = lax.dynamic_index_in_dim(values, place, 0, False).astype(FULL)
    for step in range(1, far):
        send = lax.dynamic_index_in_dim(values, (place + step) % far, 0, False)
        ring = [
            (far_from * 2 + near, (far_from + step) % far * 2 + near)
            for far_from in range(far)
            for near in range(2)
        ]
        total = total + lax.ppermute(send, DP, ring).astype(FULL)
    return total


def scatter_tensor(grad):
    rows, columns = grad.shape
    blocks = lax.axis_size(DP)
    half = columns // 2
    mine = lax.axis_index(TENSOR) % 2
    grad = grad.astype(HALF)
    keep = lax.dynamic_slice_in_dim(grad, mine * half, half, 1)
    send = lax.dynamic_slice_in_dim(grad, (1 - mine) * half, half, 1)
    grad = keep + swap(send, TENSOR, 1)
    grad = grad.reshape(blocks // 2, 2, 2, rows // blocks // 2, half)
    return halve(grad, TENSOR, 2, 2)


def gather_tensor(values):
    values = join(values.astype(HALF), TENSOR, 2, 0)
    return join(values, TENSOR, 1, 1).astype(FULL)


def sum_everywhere(values):
    blocks = lax.axis_size(DP)
    far = blocks // 2
    if far > NEAR:
        values = lax.psum(values, TENSOR)
        return lax.psum_scatter(values, DP, scatter_dimension=1, tiled=True)
    for bit in (1, 2):
        values = values + swap(values, TENSOR, bit)
    values = values + swap(values, DP, 1)
    total = values
    for step in range(1, far):
        ring = [
            (far_from * 2 + near, (far_from + step) % far * 2 + near)
            for far_from in range(far)
            for near in range(2)
        ]
        total = total + lax.ppermute(values, DP, ring)
    lanes = values.shape[1] // blocks
    return lax.dynamic_slice_in_dim(total, lax.axis_index(DP) * lanes, lanes, 1)


def body(
    patch_tokens,
    class_tokens,
    frame_counts,
    patch_cotangent,
    class_cotangent,
    temporal_in,
    temporal_out,
    temporal_mix,
    spatial_in,
    spatial_out,
    hidden_up,
    hidden_down,
    norm_gain,
    norm_shift,
):
    frames, local_patches, width = patch_tokens.shape
    clips = class_tokens.shape[0]
    layers = temporal_in.shape[0]
    heads = HEADS
    head_size = width // heads
    scale = head_size ** (-0.5)
    groups = lax.axis_size(TENSOR)
    position = lax.axis_index(TENSOR)
    patch_count = frames * local_patches
    row_count = patch_count + clips
    ends = jnp.cumsum(frame_counts[0])
    frame_index = jnp.arange(frames, dtype=jnp.int32)
    clip_of = jnp.sum((frame_index[:, None] >= ends[None, :]).astype(jnp.int32), 1)
    member = (clip_of[:, None] == jnp.arange(clips, dtype=jnp.int32)[None, :]).astype(FULL)
    member_half = member.astype(HALF)
    same = clip_of[:, None] == clip_of[None, :]
    counts = frame_counts[0].astype(FULL)
    owned = (frame_index % groups == position).astype(FULL)
    leader = (position == 0).astype(FULL)
    row_index = jnp.arange(row_count, dtype=jnp.int32)
    keep_local = jnp.logical_or(row_index < patch_count, position == 0)
    patch_rows = patch_tokens.astype(FULL)
    class_rows = class_tokens.astype(FULL)
    lane_count = width // lax.axis_size(DP)
    saved = []
    for layer in range(layers):
        gains = norm_gain[layer]
        shifts = norm_shift[layer]
        normed_time, unit_time, inverse_time = norm_forward(patch_rows, gains[0], shifts[0])
        normed_time = normed_time.astype(HALF)
        triple = (
            matmul(normed_time, temporal_in[layer])
            .astype(HALF)
            .reshape(frames, local_patches, 3, heads, head_size)
        )
        query_time = triple[:, :, 0]
        key_time = triple[:, :, 1]
        value_time = triple[:, :, 2]
        mixed_time, total_time = temporal_forward(query_time, key_time, value_time, same, scale)
        mixed_time = mixed_time.reshape(frames, local_patches, width).astype(HALF)
        projected = matmul(mixed_time, temporal_out[layer]).astype(HALF)
        after_time = patch_rows + matmul(projected, temporal_mix[layer])
        normed_patch, unit_patch, inverse_patch = norm_forward(after_time, gains[1], shifts[1])
        normed_class, unit_class, inverse_class = norm_forward(class_rows, gains[1], shifts[1])
        normed_patch = normed_patch.astype(HALF)
        normed_class = normed_class.astype(HALF)
        space_weight = spatial_in[layer]
        triple_class = matmul(normed_class, space_weight).astype(HALF)
        query_patch = (
            matmul(normed_patch, space_weight[:, :width])
            .astype(HALF)
            .reshape(frames, local_patches, heads, head_size)
        )
        pair_patch = matmul(normed_patch, space_weight[:, width:]).astype(HALF)
        pair_all = lax.all_gather(pair_patch, TENSOR, axis=1, tiled=True)
        keys_all = pair_all[..., :width].reshape(frames, -1, heads, head_size)
        values_all = pair_all[..., width:].reshape(frames, -1, heads, head_size)
        triple_frame = matmul(member_half, triple_class).astype(HALF)
        query_frame = triple_frame[:, :width].reshape(frames, 1, heads, head_size)
        key_frame = triple_frame[:, width : 2 * width].reshape(frames, heads, head_size)
        value_frame = triple_frame[:, 2 * width :].reshape(frames, heads, head_size)
        mixed_patch, total_patch = spatial_forward(
            query_patch, keys_all, key_frame, values_all, value_frame, scale
        )
        mixed_patch = mixed_patch.reshape(frames, local_patches, width).astype(HALF)
        mixed_frame, total_frame = spatial_forward(
            query_frame, keys_all, key_frame, values_all, value_frame, scale
        )
        mixed_frame = mixed_frame.reshape(frames, width) * owned[:, None]
        class_part = jnp.dot(member.T, mixed_frame, precision=HIGH)
        class_sum = lax.psum(class_part, TENSOR)
        class_mean = (class_sum / counts[:, None]).astype(HALF)
        after_space = after_time + matmul(mixed_patch, spatial_out[layer])
        class_space = class_rows + matmul(class_mean, spatial_out[layer])
        rows = jnp.concatenate([after_space.reshape(patch_count, width), class_space], 0)
        normed_feed, unit_feed, inverse_feed = norm_forward(rows, gains[2], shifts[2])
        normed_feed = normed_feed.astype(HALF)
        up_all = hidden_up[layer]
        down_all = hidden_down[layer]
        feed_inputs = lax.all_gather(normed_feed, TENSOR, axis=0, tiled=True)
        hidden = matmul(feed_inputs, up_all)
        active = jax.nn.gelu(hidden, approximate=False).astype(HALF)
        update = lax.psum_scatter(
            matmul(active, down_all).astype(jnp.bfloat16), TENSOR, scatter_dimension=0, tiled=True
        ).astype(jnp.float32)
        rows = rows + update
        saved.append(
            SimpleNamespace(
                normed_time=normed_time,
                unit_time=unit_time,
                inverse_time=inverse_time,
                query_time=query_time,
                key_time=key_time,
                value_time=value_time,
                total_time=total_time,
                mixed_time=mixed_time,
                projected=projected,
                normed_patch=normed_patch,
                normed_frames=normed_patch,
                unit_patch=unit_patch,
                inverse_patch=inverse_patch,
                normed_class=normed_class,
                unit_class=unit_class,
                inverse_class=inverse_class,
                query_patch=query_patch,
                keys_all=keys_all,
                values_all=values_all,
                query_frame=query_frame,
                key_frame=key_frame,
                value_frame=value_frame,
                total_patch=total_patch,
                total_frame=total_frame,
                mixed_patch=mixed_patch,
                class_mean=class_mean,
                unit_feed=unit_feed,
                inverse_feed=inverse_feed,
                feed_inputs=feed_inputs,
                hidden=hidden,
                active=active,
                up_all=up_all,
                down_all=down_all,
            )
        )
        patch_rows = rows[:patch_count].reshape(frames, local_patches, width)
        class_rows = rows[patch_count:]
    patch_output = patch_rows.astype(HALF)
    class_output = class_rows.astype(HALF)
    grad_rows = jnp.concatenate(
        [patch_cotangent.reshape(patch_count, width), class_cotangent], 0
    ).astype(FULL)
    collected = [None] * layers
    for layer in reversed(range(layers)):
        kept = saved[layer]
        gains = norm_gain[layer]
        grad_update = grad_rows.astype(HALF)
        grad_all = lax.all_gather(grad_update, TENSOR, axis=0, tiled=True)
        grad_active = matmul_back(grad_all, kept.down_all)
        grad_hidden = gelu_backward(kept.hidden, grad_active).astype(HALF)
        grad_normed = lax.psum_scatter(
            matmul_back(grad_hidden, kept.up_all).astype(jnp.bfloat16),
            TENSOR,
            scatter_dimension=0,
            tiled=True,
        ).astype(jnp.float32)
        spread_index = jnp.arange(groups * row_count, dtype=jnp.int32)
        keep_spread = jnp.logical_or(
            spread_index % row_count < patch_count, spread_index < row_count
        )
        inputs_kept = jnp.where(keep_spread[:, None], kept.feed_inputs, 0)
        active_kept = jnp.where(keep_spread[:, None], kept.active, 0)
        grad_up = outer_sum(inputs_kept, grad_hidden)
        grad_down = outer_sum(active_kept, grad_all)
        gain_feed = jnp.sum(jnp.where(keep_local[:, None], grad_normed * kept.unit_feed, 0.0), 0)
        shift_feed = jnp.sum(jnp.where(keep_local[:, None], grad_normed, 0.0), 0)
        grad_rows = grad_rows + norm_backward(
            grad_normed, kept.unit_feed, kept.inverse_feed, gains[2]
        )
        grad_space = grad_rows[:patch_count].reshape(frames, local_patches, width)
        grad_class = grad_rows[patch_count:]
        branch_patch = grad_space.astype(HALF)
        branch_class = grad_class.astype(HALF)
        grad_spatial_out = outer_sum(
            kept.mixed_patch.reshape(patch_count, width),
            branch_patch.reshape(patch_count, width),
        )
        grad_spatial_out = grad_spatial_out + leader * outer_sum(kept.class_mean, branch_class)
        grad_mixed_rows = matmul_back(branch_patch, spatial_out[layer]).astype(HALF)
        grad_mean = matmul_back(branch_class, spatial_out[layer])
        grad_mixed_patch = grad_mixed_rows.reshape(frames, local_patches, heads, head_size)
        grad_mixed_frame = jnp.dot(member, grad_mean / counts[:, None], precision=HIGH).astype(HALF)
        grad_mixed_frame = (grad_mixed_frame * owned[:, None].astype(HALF)).reshape(
            frames, 1, heads, head_size
        )
        patch_query, patch_keys, patch_values, patch_side_key, patch_side_value = spatial_backward(
            grad_mixed_patch,
            kept.query_patch,
            kept.keys_all,
            kept.key_frame,
            kept.values_all,
            kept.value_frame,
            kept.total_patch,
            scale,
        )
        frame_query, frame_keys, frame_values, frame_side_key, frame_side_value = spatial_backward(
            grad_mixed_frame,
            kept.query_frame,
            kept.keys_all,
            kept.key_frame,
            kept.values_all,
            kept.value_frame,
            kept.total_frame,
            scale,
        )
        pair_grad = jnp.concatenate(
            [
                (patch_keys + frame_keys).reshape(frames, -1, width),
                (patch_values + frame_values).reshape(frames, -1, width),
            ],
            -1,
        )
        pair_local = (
            lax.psum_scatter(
                pair_grad.astype(jnp.bfloat16), TENSOR, scatter_dimension=1, tiled=True
            )
            .astype(jnp.float32)
            .astype(HALF)
        )
        class_terms = jnp.concatenate(
            [
                frame_query.reshape(frames, width),
                (patch_side_key + frame_side_key).reshape(frames, width),
                (patch_side_value + frame_side_value).reshape(frames, width),
            ],
            -1,
        )
        class_local = jnp.dot(member.T, class_terms, precision=HIGH)
        grad_triple_patch = jnp.concatenate(
            [patch_query.reshape(frames, local_patches, width).astype(HALF), pair_local], -1
        )
        grad_normed_patch = matmul_back(grad_triple_patch, spatial_in[layer])
        patch_in_grad = outer_sum(
            kept.normed_patch.reshape(patch_count, width),
            grad_triple_patch.reshape(patch_count, 3 * width),
        )
        class_triple = lax.psum(class_local, TENSOR).astype(HALF)
        grad_normed_class = matmul_back(class_triple, spatial_in[layer])
        grad_spatial_in = patch_in_grad + leader * outer_sum(kept.normed_class, class_triple)
        gain_space = jnp.sum(grad_normed_patch * kept.unit_patch, (0, 1)) + leader * jnp.sum(
            grad_normed_class * kept.unit_class, 0
        )
        shift_space = jnp.sum(grad_normed_patch, (0, 1)) + leader * jnp.sum(grad_normed_class, 0)
        grad_time = grad_space + norm_backward(
            grad_normed_patch, kept.unit_patch, kept.inverse_patch, gains[1]
        )
        grad_class = grad_class + norm_backward(
            grad_normed_class, kept.unit_class, kept.inverse_class, gains[1]
        )
        branch_time = grad_time.astype(HALF)
        grad_temporal_mix = outer_sum(
            kept.projected.reshape(patch_count, width), branch_time.reshape(patch_count, width)
        )
        grad_projected = matmul_back(branch_time, temporal_mix[layer]).astype(HALF)
        grad_temporal_out = outer_sum(
            kept.mixed_time.reshape(patch_count, width),
            grad_projected.reshape(patch_count, width),
        )
        grad_mixed_time = (
            matmul_back(grad_projected, temporal_out[layer])
            .astype(HALF)
            .reshape(frames, local_patches, heads, head_size)
        )
        time_query, time_key, time_value = temporal_backward(
            grad_mixed_time,
            kept.query_time,
            kept.key_time,
            kept.value_time,
            kept.total_time,
            same,
            scale,
        )
        grad_triple_time = (
            jnp.stack([time_query, time_key, time_value], 2)
            .astype(HALF)
            .reshape(frames, local_patches, 3 * width)
        )
        grad_normed_time = matmul_back(grad_triple_time, temporal_in[layer])
        grad_temporal_in = outer_sum(
            kept.normed_time.reshape(patch_count, width),
            grad_triple_time.reshape(patch_count, 3 * width),
        )
        gain_time = jnp.sum(grad_normed_time * kept.unit_time, (0, 1))
        shift_time = jnp.sum(grad_normed_time, (0, 1))
        grad_patch = grad_time + norm_backward(
            grad_normed_time, kept.unit_time, kept.inverse_time, gains[0]
        )
        grad_rows = jnp.concatenate([grad_patch.reshape(patch_count, width), grad_class], 0)
        gain_grads = jnp.stack([gain_time, gain_space, gain_feed])
        shift_grads = jnp.stack([shift_time, shift_space, shift_feed])
        shared = [
            gather_tensor(scatter_dp(scatter_tensor(grad)))
            for grad in (
                grad_temporal_in,
                grad_temporal_out,
                grad_temporal_mix,
                grad_spatial_in,
                grad_spatial_out,
            )
        ]
        norms = sum_everywhere(jnp.concatenate([gain_grads, shift_grads], 0))
        feeds = [
            scatter_dp(grad.astype(HALF).reshape(-1, 2, lane_count, width)).astype(FULL)
            for grad in (grad_up, grad_down.T)
        ]
        shared += [norms[:3], norms[3:], feeds[0], feeds[1].T]
        collected[layer] = tuple(shared)
    patch_grad = grad_rows[:patch_count].reshape(frames, local_patches, width)
    class_grad = grad_rows[patch_count:]
    stacked = [
        jnp.stack([collected[layer][member_index] for layer in range(layers)])
        for member_index in range(9)
    ]
    return (
        patch_output,
        class_output,
        patch_grad,
        class_grad,
        stacked[0],
        stacked[1],
        stacked[2],
        stacked[3],
        stacked[4],
        stacked[7],
        stacked[8],
        stacked[5],
        stacked[6],
    )


def solution(mesh):
    placed = (
        P(DP, TENSOR, None),
        P(DP, None),
        P(DP, None),
        P(DP, TENSOR, None),
        P(DP, None),
        P(),
        P(),
        P(),
        P(),
        P(),
        P(None, None, TENSOR),
        P(None, TENSOR, None),
        P(),
        P(),
    )
    return jax.shard_map(
        body,
        mesh=mesh,
        in_specs=placed,
        out_specs=(
            P(DP, TENSOR, None),
            P(DP, None),
            P(DP, TENSOR, None),
            P(DP, None),
            P(None, DP, None),
            P(None, DP, None),
            P(None, DP, None),
            P(None, DP, None),
            P(None, DP, None),
            P(None, DP, TENSOR),
            P(None, TENSOR, DP),
            P(None, None, DP),
            P(None, None, DP),
        ),
        check_vma=False,
    )
```

```python
from functools import partial

import jax
import jax.numpy as jnp
from jax import lax
from jax.experimental import pallas as pl
from jax.experimental.pallas import tpu as pltpu
from jax.sharding import PartitionSpec as P

HEADS = 12
EPS = 1e-06
HIGH = lax.Precision.HIGHEST
HALF = jnp.bfloat16
FULL = jnp.float32
NEAR = 4
TENSOR = "tensor"
DP = "dp"
TILE = 256
VMEM_BYTES = 56 << 20
SMEM = pl.BlockSpec(memory_space=pltpu.SMEM)
VMEM = pl.BlockSpec(memory_space=pltpu.VMEM)
ANY = pl.BlockSpec(memory_space=pl.ANY)
ROOT_HALF = 0.5**0.5
DENSITY = (2.0 * 3.141592653589793) ** -0.5


def up_to(value, step):
    return -(-value // step) * step


def dot(left, right):
    return jnp.dot(left, right, preferred_element_type=FULL)


def dot_back(left, right):
    return lax.dot_general(left, right, (((1,), (1,)), ((), ())), preferred_element_type=FULL)


def dot_outer(left, right):
    return lax.dot_general(left, right, (((0,), (0,)), ((), ())), preferred_element_type=FULL)


def unit_of(values):
    centred = values - jnp.mean(values, -1, keepdims=True)
    inverse = lax.rsqrt(jnp.mean(centred * centred, -1, keepdims=True) + EPS)
    return centred * inverse, inverse


def unit_back(grad, unit, inverse, gain):
    scaled = grad * gain
    inner = (
        scaled
        - jnp.mean(scaled, -1, keepdims=True)
        - unit * jnp.mean(scaled * unit, -1, keepdims=True)
    )
    return inner * inverse


def head_lanes(head_size, half):
    lane = lax.broadcasted_iota(jnp.int32, (1, 2 * head_size), 1)
    return (lane // head_size) == half


def row_chunk(rows):
    return next(step for step in (80, 104, 64, 48, 32, 16, 8) if rows % step == 0)


def over_rows(rows, step, run):
    def one(index, carry):
        run(pl.ds(pl.multiple_of(index * step, step), step))
        return carry

    lax.fori_loop(0, rows // step, one, 0)


def interleave(order, frame, frames, values):
    for group in range(order.shape[0]):
        part = values[:, group * 128 : (group + 1) * 128]
        order[group, pl.ds(frame, values.shape[0], stride=frames), :] = part


def pick(order, frame, frames, patches):
    own = pl.ds(frame, patches, stride=frames)
    return jnp.concatenate([order[group, own, :] for group in range(order.shape[0])], 1)


def shard_copies(place_ref, refs, target):
    own, core, far_first, far_second, core_first, core_second = refs
    half = far_first.shape[0]
    first = pl.multiple_of(place_ref[1] * half, half)
    second = pl.multiple_of((1 - place_ref[1]) * half, half)
    return [
        [(own, target.at[0])],
        [(core, target.at[1])],
        [
            (far_first, target.at[2, pl.ds(first, half)]),
            (far_second, target.at[2, pl.ds(second, half)]),
        ],
        [
            (core_first, target.at[3, pl.ds(first, half)]),
            (core_second, target.at[3, pl.ds(second, half)]),
        ],
    ]


def start_shards(place_ref, ups, downs, up_ref, down_ref, sems):
    waits = []
    index = 0
    for pairs in zip(
        shard_copies(place_ref, ups, up_ref), shard_copies(place_ref, downs, down_ref)
    ):
        group = []
        for source, target in pairs[0] + pairs[1]:
            copy = pltpu.make_async_copy(source, target, sems.at[index])
            copy.start()
            group.append(copy)
            index += 1
        waits.append(group)
    return waits


def fetch(sources, targets, sems):
    copies = [
        pltpu.make_async_copy(source, target, sems.at[index])
        for index, (source, target) in enumerate(zip(sources, targets))
    ]
    for copy in copies:
        copy.start()
    return copies


def attend_forward(load, store, store_total, heads, head_size, bias):
    scale = head_size**-0.5
    totals = None
    lanes = None
    for pair in range(heads // 2):
        query, key, value = (load(part, pair) for part in range(3))
        sides = []
        for half in range(2):
            mine = head_lanes(head_size, half)
            scores = dot_back(jnp.where(mine, query, 0), key) * scale + bias
            top = jnp.max(scores, -1, keepdims=True)
            raised = jnp.exp(scores - top)
            total = jnp.sum(raised, -1, keepdims=True)
            sides.append(dot(raised.astype(HALF), value) * (1.0 / total))
            log_total = top + jnp.log(total)
            if totals is None:
                lanes = lax.broadcasted_iota(jnp.int32, (query.shape[0], 128), 1)
                totals = jnp.zeros(lanes.shape, FULL)
            totals = jnp.where(lanes == pair * 2 + half, log_total, totals)
        store(pair, jnp.where(head_lanes(head_size, 0), sides[0], sides[1]))
    store_total(totals)


def attend_backward(load, load_grad, totals, store, heads, head_size, bias):
    scale = head_size**-0.5
    for pair in range(heads // 2):
        query, key, value = (load(part, pair) for part in range(3))
        grad = load_grad(pair)
        sides = []
        for half in range(2):
            mine = head_lanes(head_size, half)
            head = pair * 2 + half
            scores = dot_back(jnp.where(mine, query, 0), key) * scale + bias
            prob = jnp.exp(scores - totals[:, head : head + 1])
            grad_prob = dot_back(jnp.where(mine, grad, 0), value)
            delta = jnp.sum(prob * grad_prob, -1, keepdims=True)
            grad_score = (prob * (grad_prob - delta)).astype(HALF)
            sides.append(
                (
                    dot(grad_score, key) * scale,
                    dot_outer(grad_score, query) * scale,
                    dot_outer(prob.astype(HALF), grad),
                )
            )
        for part in range(3):
            first = head_lanes(head_size, 0)
            store(part, pair, jnp.where(first, sides[0][part], sides[1][part]))


def time_forward(dims, layer, place_ref, x_ref, bias_ref, gain_ref, shift_ref, in_hbm, out_hbm, mix_hbm,
                 normed_ref, triple_ref, total_ref, mixed_ref, projected_ref, after_ref,
                 send0, send1, send2, send3, class_ref,
                 in_ref, out_ref, mix_ref, order, plain, blocks, sems):
    frames, patches, width, heads, groups = dims
    count = frames * patches
    rows = x_ref.shape[0]
    step = bias_ref.shape[0]
    copies = fetch(
        (in_hbm.at[layer], out_hbm.at[layer], mix_hbm.at[layer]), (in_ref, out_ref, mix_ref), sems
    )
    gain = gain_ref[layer, 0:1, :]
    shift = shift_ref[layer, 0:1, :]
    for frame in range(frames):
        unit, unused = unit_of(x_ref[frame * patches : (frame + 1) * patches, :])
        interleave(order, frame, frames, unit * gain + shift)
    for group in range(width // 128):
        order[group, count:, :] = jnp.zeros((rows - count, 128), FULL)
        normed_ref[:, group * 128 : (group + 1) * 128] = order[group].astype(HALF)
    copies[0].wait()
    for column in range(0, 3 * width, TILE):
        part = slice(column, column + TILE)
        triple_ref[:, part] = dot(normed_ref[...], in_ref[:, part]).astype(HALF)

    def block(index, carry):
        own = pl.ds(pl.multiple_of(index * step, step), step)

        def load(part, pair):
            start = part * width + pair * 128
            return triple_ref[own, start : start + 128]

        def store(pair, mixed):
            order[pair, own, :] = mixed

        def store_total(totals):
            total_ref[own, :] = totals

        attend_forward(load, store, store_total, heads, width // heads, bias_ref[...])
        return carry

    lax.fori_loop(0, rows // step, block, 0)
    for frame in range(frames):
        plain[frame * patches : (frame + 1) * patches, :] = pick(order, frame, frames, patches)
    plain[count:, :] = jnp.zeros((rows - count, width), FULL)
    mixed_ref[...] = plain[...].astype(HALF)
    copies[1].wait()
    for column in range(0, width, TILE):
        part = slice(column, column + TILE)
        projected_ref[:, part] = dot(mixed_ref[...], out_ref[:, part]).astype(HALF)
    copies[2].wait()
    for column in range(0, width, TILE):
        part = slice(column, column + TILE)
        after_ref[:, part] = x_ref[:, part] + dot(projected_ref[...], mix_ref[:, part])
    gain = gain_ref[layer, 1:2, :]
    shift = shift_ref[layer, 1:2, :]

    def norm(own):
        unit, unused = unit_of(after_ref[own, :])
        plain[own, :] = unit * gain + shift

    over_rows(rows, row_chunk(rows), norm)
    send_blocks(plain, blocks, (send0, send1, send2, send3), place_ref[0], count // groups)
    class_ref[...] = plain[count:, :]


def send_blocks(plain, blocks, sends, place, size):
    groups = len(sends)
    for group in range(groups):
        blocks[group, 0:size, :] = plain[group * size : (group + 1) * size, :]
    for away in range(groups):
        sends[away][...] = blocks[place ^ away][0:size].astype(HALF)


def space_forward(dims, layer, place_ref, clip_ref, class_ref, piece0, piece1, piece2, piece3, in_hbm,
                  normed_ref, triple_ref, total_ref, send0, send1, send2, send3,
                  in_ref, plain, sems):
    frames, patches, width, heads, groups = dims
    own_frames = frames // groups
    seq = groups * patches
    rows = normed_ref.shape[0] // own_frames
    copies = fetch((in_hbm.at[layer],), (in_ref,), sems)
    pieces = [piece0, piece1, piece2, piece3]
    for away, piece in enumerate(pieces):
        values = piece[...].astype(FULL)
        for frame in range(own_frames):
            start = frame * rows + away * patches
            plain[start : start + patches, :] = values[frame * patches : (frame + 1) * patches]
    for frame in range(own_frames):
        start = frame * rows + seq
        plain[start : start + rows - seq, :] = jnp.zeros((rows - seq, width), FULL)
        clip = clip_ref[place_ref[0] * own_frames + frame]
        plain[start : start + 1, :] = class_ref[pl.ds(clip, 1), :]
    normed_ref[...] = plain[...].astype(HALF)
    copies[0].wait()
    for column in range(0, 3 * width, TILE):
        part = slice(column, column + TILE)
        triple_ref[:, part] = dot(normed_ref[...], in_ref[:, part]).astype(HALF)
    keys = lax.broadcasted_iota(jnp.int32, (1, rows), 1)
    bias = jnp.where(keys <= seq, 0.0, -1e30)

    def block(index, carry):
        own = pl.ds(pl.multiple_of(index * rows, rows), rows)

        def load(part, pair):
            start = part * width + pair * 128
            return triple_ref[own, start : start + 128]

        def store(pair, mixed):
            plain[own, pair * 128 : (pair + 1) * 128] = mixed

        def store_total(totals):
            total_ref[own, :] = totals

        attend_forward(load, store, store_total, heads, width // heads, bias)
        return carry

    lax.fori_loop(0, own_frames, block, 0)
    return_pieces(plain, (send0, send1, send2, send3), own_frames, patches, rows)


def return_pieces(plain, sends, own_frames, patches, rows):
    seq = len(sends) * patches
    tail = []
    for frame in range(own_frames):
        row = plain[frame * rows + seq : frame * rows + seq + 1, :]
        high = row.astype(HALF).astype(FULL)
        tail += [high, row - high]
    size = own_frames * patches
    spare = sends[0].shape[0] - size - len(tail)
    tail.append(jnp.zeros((spare, plain.shape[1]), FULL))
    for away, send in enumerate(sends):
        kept = [
            plain[frame * rows + away * patches : frame * rows + (away + 1) * patches, :]
            for frame in range(own_frames)
        ]
        send[...] = jnp.concatenate(kept + tail, 0).astype(HALF)


def take_pieces(pieces, blocks, plain, frame_rows, place, size, own_frames):
    for away, piece in enumerate(pieces):
        blocks[place ^ away] = piece[...].astype(FULL)
    for group in range(len(pieces)):
        plain[group * size : (group + 1) * size, :] = blocks[group, 0:size, :]
        for frame in range(own_frames):
            start = size + 2 * frame
            frame_rows[group * own_frames + frame : group * own_frames + frame + 1, :] = (
                blocks[group, start : start + 1, :] + blocks[group, start + 1 : start + 2, :]
            )


def feed_forward(dims, layer, place_ref, piece0, piece1, piece2, piece3, share_ref, after_ref,
                 gain_ref, shift_ref, out_hbm,
                 up0, up1, up2, up3, up4, up5, down0, down1, down2, down3, down4, down5,
                 mixed_ref, rows_ref, normed_ref, active_ref, slope_ref, next_ref,
                 out_ref, up_ref, down_ref, plain, blocks, frame_rows, whole, out_sem, sems):
    frames, patches, width, heads, groups = dims
    count = frames * patches
    rows = after_ref.shape[0]
    size = count // groups
    place = place_ref[0]
    copies = fetch((out_hbm.at[layer],), (out_ref,), out_sem)
    ups, downs = (up0, up1, up2, up3, up4, up5), (down0, down1, down2, down3, down4, down5)
    shards = start_shards(place_ref, ups, downs, up_ref, down_ref, sems)
    take_pieces(
        (piece0, piece1, piece2, piece3), blocks, plain, frame_rows, place, size, frames // groups
    )
    plain[count:, :] = jnp.dot(
        share_ref[...], frame_rows[...], precision=HIGH, preferred_element_type=FULL
    )
    whole[...] = plain[...].astype(HALF)
    leader = jnp.where(place == 0, 1.0, 0.0).astype(FULL)
    kept = lax.broadcasted_iota(jnp.int32, (rows, 1), 0) < count
    kept = jnp.where(kept, 1.0, leader)
    mixed_ref[...] = (plain[...] * kept).astype(HALF)
    copies[0].wait()
    for column in range(0, width, TILE):
        part = slice(column, column + TILE)
        rows_ref[:, part] = after_ref[:, part] + dot(whole[...], out_ref[:, part])
    gain = gain_ref[layer, 2:3, :]
    shift = shift_ref[layer, 2:3, :]

    def norm(own):
        unit, unused = unit_of(rows_ref[own, :])
        plain[own, :] = unit * gain + shift

    over_rows(rows, row_chunk(rows), norm)
    whole[...] = plain[...].astype(HALF)
    normed_ref[...] = (plain[...] * kept).astype(HALF)
    next_ref[...] = rows_ref[...]
    for away in range(groups):
        for copy in shards[away]:
            copy.wait()
        for column in range(0, width, TILE):
            part = slice(column, column + TILE)
            hidden = dot(whole[...], up_ref[away, :, part])
            below = 0.5 + 0.5 * lax.erf(hidden * ROOT_HALF)
            active = (hidden * below).astype(HALF)
            slope = below + hidden * (jnp.exp(hidden * hidden * -0.5) * DENSITY)
            start = away * width + column
            active_ref[:, start : start + TILE] = active
            slope_ref[:, start : start + TILE] = slope.astype(HALF)
            next_ref[...] += dot(active, down_ref[away, part, :])
    start = count // 16 * 16
    active_ref[start:, :] = (active_ref[start:, :].astype(FULL) * kept[start:]).astype(HALF)


def feed_backward(dims, layer, place_ref, clip_ref, grad_ref, slope_ref, rows_ref, share_ref, gain_ref,
                  out_hbm, up0, up1, up2, up3, up4, up5, down0, down1, down2, down3, down4, down5,
                  update_ref, hidden_ref, branch_ref, back_ref, norms_ref,
                  send0, send1, send2, send3, class_ref,
                  out_ref, up_ref, down_ref, total, plain, blocks, out_sem, sems):
    frames, patches, width, heads, groups = dims
    count = frames * patches
    rows = grad_ref.shape[0]
    place = place_ref[0]
    own_frames = frames // groups
    ups, downs = (up0, up1, up2, up3, up4, up5), (down0, down1, down2, down3, down4, down5)
    shards = start_shards(place_ref, ups, downs, up_ref, down_ref, sems)
    copies = fetch((out_hbm.at[layer],), (out_ref,), out_sem)
    update_ref[...] = grad_ref[...].astype(HALF)
    for away in range(groups):
        for copy in shards[away]:
            copy.wait()
        for column in range(0, width, TILE):
            part = slice(column, column + TILE)
            start = away * width + column
            grad_active = dot_back(update_ref[...], down_ref[away, part, :])
            slope = slope_ref[:, start : start + TILE].astype(FULL)
            grad_hidden = (grad_active * slope).astype(HALF)
            hidden_ref[:, start : start + TILE] = grad_hidden
            term = dot_back(grad_hidden, up_ref[away, :, part])
            if start == 0:
                total[...] = term
            else:
                total[...] += term
    gain = gain_ref[layer, 2:3, :]
    leader = jnp.where(place == 0, 1.0, 0.0).astype(FULL)
    norms_ref[...] = jnp.zeros(norms_ref.shape, FULL)
    step = row_chunk(rows)

    def norm(own):
        unit, inverse = unit_of(rows_ref[own, :])
        grad = total[own, :]
        back = grad_ref[own, :] + unit_back(grad, unit, inverse, gain)
        back_ref[own, :] = back
        branch_ref[own, :] = back.astype(HALF)
        kept = lax.broadcasted_iota(jnp.int32, (step, 1), 0) + own.start < count
        grad = jnp.where(kept, grad, grad * leader)
        norms_ref[0:1, :] += jnp.sum(grad * unit, 0, keepdims=True)
        norms_ref[1:2, :] += jnp.sum(grad, 0, keepdims=True)

    over_rows(rows, step, norm)
    copies[-1].wait()
    for column in range(0, width, TILE):
        part = slice(column, column + TILE)
        plain[:, part] = dot_back(branch_ref[...], out_ref[part, :])
    send_blocks(plain, blocks, (send0, send1, send2, send3), place, count // groups)
    for frame in range(own_frames):
        clip = clip_ref[place * own_frames + frame]
        class_ref[frame : frame + 1, :] = (
            plain[pl.ds(count + clip, 1), :] * share_ref[pl.ds(clip, 1), 0:1]
        )


def space_backward(dims, layer, piece0, piece1, piece2, piece3, class_ref, triple_ref, total_ref, in_hbm,
                   grad_ref, send0, send1, send2, send3,
                   in_ref, plain, mixed, sems):
    frames, patches, width, heads, groups = dims
    own_frames = frames // groups
    seq = groups * patches
    rows = triple_ref.shape[0] // own_frames
    copies = fetch((in_hbm.at[layer],), (in_ref,), sems)
    for away, piece in enumerate((piece0, piece1, piece2, piece3)):
        values = piece[...].astype(FULL)
        for frame in range(own_frames):
            start = frame * rows + away * patches
            plain[start : start + patches, :] = values[frame * patches : (frame + 1) * patches]
    for frame in range(own_frames):
        start = frame * rows + seq
        plain[start : start + rows - seq, :] = jnp.zeros((rows - seq, width), FULL)
        plain[start : start + 1, :] = class_ref[frame : frame + 1, :]
    mixed[...] = plain[...].astype(HALF)
    keys = lax.broadcasted_iota(jnp.int32, (1, rows), 1)
    bias = jnp.where(keys <= seq, 0.0, -1e30)

    def block(index, carry):
        own = pl.ds(pl.multiple_of(index * rows, rows), rows)

        def load(part, pair):
            start = part * width + pair * 128
            return triple_ref[own, start : start + 128]

        def load_grad(pair):
            return mixed[own, pair * 128 : (pair + 1) * 128]

        def store(part, pair, grad):
            start = part * width + pair * 128
            grad_ref[own, start : start + 128] = grad.astype(HALF)

        attend_backward(load, load_grad, total_ref[own, :], store, heads, width // heads, bias)
        return carry

    lax.fori_loop(0, own_frames, block, 0)
    copies[0].wait()
    for column in range(0, width, TILE):
        part = slice(column, column + TILE)
        plain[:, part] = dot_back(grad_ref[...], in_ref[part, :])
    return_pieces(plain, (send0, send1, send2, send3), own_frames, patches, rows)


def time_backward(dims, layer, place_ref, piece0, piece1, piece2, piece3, member_ref, back_ref, after_ref, x_ref,
                  triple_ref, total_ref, bias_ref, gain_ref, in_hbm, out_hbm, mix_hbm,
                  branch_ref, projected_ref, grad_ref, next_ref, norms_ref,
                  in_ref, out_ref, mix_ref, order, plain, blocks, frame_rows, mixed, sems):
    frames, patches, width, heads, groups = dims
    count = frames * patches
    rows = x_ref.shape[0]
    step = bias_ref.shape[0]
    place = place_ref[0]
    copies = fetch(
        (mix_hbm.at[layer], out_hbm.at[layer], in_hbm.at[layer]), (mix_ref, out_ref, in_ref), sems
    )
    take_pieces(
        (piece0, piece1, piece2, piece3),
        blocks,
        plain,
        frame_rows,
        place,
        count // groups,
        frames // groups,
    )
    plain[count:, :] = jnp.dot(
        member_ref[...], frame_rows[...], precision=HIGH, preferred_element_type=FULL
    )
    leader = jnp.where(place == 0, 1.0, 0.0).astype(FULL)
    norms_ref[...] = jnp.zeros(norms_ref.shape, FULL)
    gain = gain_ref[layer, 1:2, :]
    chunk = row_chunk(rows)

    def space_norm(own):
        unit, inverse = unit_of(after_ref[own, :])
        grad = plain[own, :]
        back = back_ref[own, :] + unit_back(grad, unit, inverse, gain)
        next_ref[own, :] = back
        kept = lax.broadcasted_iota(jnp.int32, (chunk, 1), 0) + own.start < count
        branch_ref[own, :] = jnp.where(kept, back, 0.0).astype(HALF)
        grad = jnp.where(kept, grad, grad * leader)
        norms_ref[0:1, :] += jnp.sum(grad * unit, 0, keepdims=True)
        norms_ref[1:2, :] += jnp.sum(grad, 0, keepdims=True)

    over_rows(rows, chunk, space_norm)
    copies[0].wait()
    for column in range(0, width, TILE):
        part = slice(column, column + TILE)
        projected_ref[:, part] = dot_back(branch_ref[...], mix_ref[part, :]).astype(HALF)
    copies[1].wait()
    for column in range(0, width, TILE):
        part = slice(column, column + TILE)
        plain[:, part] = dot_back(projected_ref[...], out_ref[part, :])
    for frame in range(frames):
        interleave(order, frame, frames, plain[frame * patches : (frame + 1) * patches, :])
    for group in range(width // 128):
        order[group, count:, :] = jnp.zeros((rows - count, 128), FULL)
        mixed[:, group * 128 : (group + 1) * 128] = order[group].astype(HALF)

    def block(index, carry):
        own = pl.ds(pl.multiple_of(index * step, step), step)

        def load(part, pair):
            start = part * width + pair * 128
            return triple_ref[own, start : start + 128]

        def load_grad(pair):
            return mixed[own, pair * 128 : (pair + 1) * 128]

        def store(part, pair, grad):
            start = part * width + pair * 128
            grad_ref[own, start : start + 128] = grad.astype(HALF)

        attend_backward(
            load, load_grad, total_ref[own, :], store, heads, width // heads, bias_ref[...]
        )
        return carry

    lax.fori_loop(0, rows // step, block, 0)
    copies[2].wait()
    for column in range(0, width, TILE):
        part = slice(column, column + TILE)
        grad = dot_back(grad_ref[...], in_ref[part, :])
        for group in range(TILE // 128):
            order[column // 128 + group] = grad[:, group * 128 : (group + 1) * 128]
    gain = gain_ref[layer, 0:1, :]
    for frame in range(frames):
        own = slice(frame * patches, (frame + 1) * patches)
        grad = pick(order, frame, frames, patches)
        unit, inverse = unit_of(x_ref[own, :])
        next_ref[own, :] += unit_back(grad, unit, inverse, gain)
        norms_ref[2:3, :] += jnp.sum(grad * unit, 0, keepdims=True)
        norms_ref[3:4, :] += jnp.sum(grad, 0, keepdims=True)


def cost(micros):
    return pl.CostEstimate(flops=micros * 10**9, bytes_accessed=micros * 10**6, transcendentals=0)


def call(kernel, outs, scratch, specs, micros):
    return pl.pallas_call(
        kernel,
        out_shape=[jax.ShapeDtypeStruct(shape, kind) for shape, kind in outs],
        in_specs=specs,
        out_specs=[VMEM] * len(outs),
        scratch_shapes=scratch,
        compiler_params=pltpu.CompilerParams(vmem_limit_bytes=VMEM_BYTES),
        cost_estimate=cost(micros),
    )


def outer_kernel(split, steps, place_ref, *refs):
    count = len(steps)
    lefts, rights, send_ref, keep_ref, turned = (
        refs[:count],
        refs[count : 2 * count],
        refs[2 * count],
        refs[2 * count + 1],
        refs[2 * count + 2 :],
    )
    step = pl.program_id(0)
    half = pl.num_programs(0) // 2

    def store(target, terms):
        if split:
            blocks, rows = target.shape[1], target.shape[2]
            far = place_ref[0] // 2 % 2
            for index in range(blocks):
                for side in range(2):
                    start = (index * 2 + side) * rows
                    target[far ^ side, index] = terms[start : start + rows]
        else:
            target[0] = terms

    for index, (first, last) in enumerate(steps):

        @pl.when(step == first)
        def _():
            turned[index][...] = lefts[index][...].astype(FULL).T.astype(HALF)

        @pl.when(jnp.logical_and(step >= first, step < last))
        def _():
            store(send_ref, dot(turned[index][...], rights[index][...]).astype(HALF))

        @pl.when(jnp.logical_and(step >= first + half, step < last + half))
        def _():
            store(keep_ref, dot(turned[index][...], rights[index][...]).astype(HALF))


def outer_group(place, pairs, groups, blocks, split, micros):
    rows = pairs[0][0].shape[1]
    parts = 2 if split else groups
    sizes = [right.shape[1] // parts for left, right in pairs]
    tile = 384 if all(size % 384 == 0 for size in sizes) else 128
    tiles = [size // tile for size in sizes]
    inner = 1 if split else 2
    total = sum(tiles)
    half = inner * total
    starts = [inner * sum(tiles[:index]) for index in range(len(tiles))]
    steps = [(start, start + inner * own) for start, own in zip(starts, tiles)]

    def right_map(start, own, step, place_ref):
        keep = step >= half
        local = jnp.clip(jnp.where(keep, step - half, step) - start, 0, inner * own - 1)
        if split:
            side = place_ref[0] % 2
            return (0, jnp.where(keep, side, 1 - side) * own + local)
        shard = local // own * 2 + jnp.where(keep, 0, 1)
        return (0, shard * own + local % own)

    def out_map(step):
        if split:
            return (0, 0, 0, step)
        shard = step * 0
        column = step * 0
        for start, own, base in zip(starts, tiles, [s // inner for s in starts]):
            here = jnp.logical_and(step >= start, step < start + inner * own)
            shard = jnp.where(here, (step - start) // own, shard)
            column = jnp.where(here, base + (step - start) % own, column)
        return (shard, 0, column)

    if split:
        size = rows // blocks // 2
        shape, block = (2, blocks, size, total * tile), (2, blocks, size, tile)
    else:
        shape, block = (2, rows, total * tile), (1, rows, tile)
    shape = jax.ShapeDtypeStruct(shape, HALF)
    lefts, rights = zip(*pairs)
    send, keep = pl.pallas_call(
        partial(outer_kernel, split, steps),
        out_shape=[shape, shape],
        grid_spec=pltpu.PrefetchScalarGridSpec(
            num_scalar_prefetch=1,
            grid=(2 * half,),
            in_specs=[pl.BlockSpec(left.shape, lambda step, place_ref: (0, 0)) for left in lefts]
            + [
                pl.BlockSpec((right.shape[0], tile), partial(right_map, start, own))
                for right, start, own in zip(rights, starts, tiles)
            ],
            out_specs=[
                pl.BlockSpec(block, lambda step, place_ref: out_map(jnp.minimum(step, half - 1))),
                pl.BlockSpec(block, lambda step, place_ref: out_map(jnp.maximum(step - half, 0))),
            ],
            scratch_shapes=[pltpu.VMEM((rows, left.shape[0]), HALF) for left in lefts],
        ),
        compiler_params=pltpu.CompilerParams(vmem_limit_bytes=VMEM_BYTES),
        cost_estimate=cost(micros),
    )(place, *lefts, *rights)
    if split:
        return send, keep
    shape = (2, blocks, rows // blocks, total * tile)
    return send.reshape(shape), keep.reshape(shape)


def swap(values, axis, bit):
    size = lax.axis_size(axis)
    return lax.ppermute(values, axis, [(index, index ^ bit) for index in range(size)])


def ring(values, far, step):
    return lax.ppermute(
        values,
        DP,
        [
            (start * 2 + near, (start + step) % far * 2 + near)
            for start in range(far)
            for near in range(2)
        ],
    )


def reduce_group(parts, order):
    send, keep = parts
    other = yield swap(send, TENSOR, 1)
    values = keep + other
    blocks, rows, columns = values.shape[1:]
    far = blocks // 2
    near_index = lax.axis_index(DP) % 2
    far_index = lax.axis_index(DP) // 2
    values = values.reshape(2, far, 2, rows, columns)
    dims = [0, 1, 2]
    for axis in order:
        dim = dims.index(axis)
        if axis == 0:
            keep = lax.index_in_dim(values, 0, dim, False)
            other = yield swap(lax.index_in_dim(values, 1, dim, False), TENSOR, 2)
            values = keep + other
        elif axis == 2:
            keep = lax.dynamic_index_in_dim(values, near_index, dim, False)
            send = lax.dynamic_index_in_dim(values, 1 - near_index, dim, False)
            other = yield swap(send, DP, 1)
            values = keep + other
        else:
            keep = lax.dynamic_index_in_dim(values, far_index, dim, False).astype(FULL)
            others = yield [
                ring(
                    lax.dynamic_index_in_dim(values, (far_index + step) % far, dim, False),
                    far,
                    step,
                )
                for step in range(1, far)
            ]
            for other in others:
                keep = keep + other.astype(FULL)
            values = keep.astype(HALF) if axis != order[-1] else keep
        dims.remove(axis)
    return values.astype(FULL)


def reduce_attention(parts, order, sizes):
    values = (yield from reduce_group(parts, order)).astype(HALF)
    other = yield swap(values, TENSOR, 2)
    values = in_order(values, other, 2, 0)
    other = yield swap(values, TENSOR, 1)
    matrices = []
    begin = 0
    for size in sizes:
        end = begin + size // 2
        matrices.append(in_order(values[:, begin:end], other[:, begin:end], 1, 1).astype(FULL))
        begin = end
    return matrices


def in_order(values, other, bit, dim):
    first = lax.axis_index(TENSOR) // bit % 2 == 0
    return jnp.where(
        first,
        jnp.concatenate([values, other], dim),
        jnp.concatenate([other, values], dim),
    )


def reduce_far(parts):
    send, keep = parts
    other = yield swap(send, TENSOR, 1)
    values = keep + other
    values = values[0] + swap(values[1], TENSOR, 2)
    values = values.reshape(-1, values.shape[-1])
    return lax.psum_scatter(values, DP, scatter_dimension=0, tiled=True).astype(FULL)


def reduce_whole(pairs):
    totals = yield [lax.psum(dot_outer(*pair).astype(HALF), TENSOR) for pair in pairs]
    return [
        lax.psum_scatter(total, DP, scatter_dimension=0, tiled=True).astype(FULL)
        for total in totals
    ]


class Flights:
    def __init__(self):
        self.running = {}
        self.results = {}

    def start(self, name, steps):
        self.running[name] = (steps, next(steps))

    def land(self, names, values):
        names = [name for name in names if name in self.running]
        held = [self.running[name][1] for name in names]
        values, held = lax.optimization_barrier((values, held))
        for name, arrived in zip(names, held):
            steps = self.running.pop(name)[0]
            try:
                self.running[name] = (steps, steps.send(arrived))
            except StopIteration as stop:
                self.results[name] = stop.value
        return values

    def finish(self):
        while self.running:
            for name in list(self.running):
                steps, arrived = self.running.pop(name)
                try:
                    self.running[name] = (steps, steps.send(arrived))
                except StopIteration as stop:
                    self.results[name] = stop.value


def reduce_norms(values):
    count = lax.axis_size(DP)
    far = count // 2
    if count > 2 * NEAR:
        values = yield lax.psum(values, TENSOR)
        return lax.psum_scatter(values, DP, scatter_dimension=1, tiled=True)
    for axis, bit in ((TENSOR, 1), (TENSOR, 2), (DP, 1)):
        other = yield swap(values, axis, bit)
        values = values + other
    others = yield [ring(values, far, step) for step in range(1, far)]
    for other in others:
        values = values + other
    lanes = values.shape[1] // count
    return lax.dynamic_slice_in_dim(values, lax.axis_index(DP) * lanes, lanes, 1)


def spread(pieces):
    return [pieces[0]] + [swap(piece, TENSOR, away) for away, piece in enumerate(pieces) if away]


def gather_shards(values):
    half = values.shape[0] // 2
    near = lax.axis_index(DP) % 2
    first = swap(lax.dynamic_slice_in_dim(values, near * half, half, 0), TENSOR, 2)
    second = swap(first, DP, 1)
    return [
        values,
        swap(values, TENSOR, 1),
        first,
        second,
        swap(first, TENSOR, 1),
        swap(second, TENSOR, 1),
    ]


def body(
    patch_tokens,
    class_tokens,
    frame_counts,
    patch_cotangent,
    class_cotangent,
    temporal_in,
    temporal_out,
    temporal_mix,
    spatial_in,
    spatial_out,
    hidden_up,
    hidden_down,
    norm_gain,
    norm_shift,
):
    frames, patches, width = patch_tokens.shape
    clips = class_tokens.shape[0]
    layers = temporal_in.shape[0]
    groups = lax.axis_size(TENSOR)
    place = jnp.stack([lax.axis_index(TENSOR), lax.axis_index(DP) % 2]).astype(jnp.int32)
    blocks_dp = lax.axis_size(DP)
    dims = (frames, patches, width, HEADS, groups)
    count = frames * patches
    rows = up_to(count + up_to(clips, 8), 80)
    spare = rows - count
    own_frames = frames // groups
    seq = groups * patches
    frame_span = up_to(seq + 1, 16)
    span = own_frames * frame_span
    hidden = groups * hidden_up.shape[2]
    piece_rows = own_frames * patches
    back_rows = up_to(piece_rows + 2 * own_frames, 8)

    ends = jnp.cumsum(frame_counts[0])
    frame_index = jnp.arange(frames, dtype=jnp.int32)
    clip_of = jnp.sum((frame_index[:, None] >= ends[None, :]).astype(jnp.int32), 1)
    clip_index = jnp.arange(spare, dtype=jnp.int32)
    member = (clip_index[:, None] == clip_of[None, :]).astype(FULL)
    counts = jnp.concatenate([frame_counts[0].astype(FULL), jnp.ones((spare - clips,), FULL)])
    share = member / counts[:, None]
    inverse_counts = 1.0 / counts
    row_index = jnp.arange(80, dtype=jnp.int32)
    row_clip = jnp.sum(
        jnp.where(row_index[:, None] % frames == frame_index[None, :], clip_of[None, :], 0), 1
    )
    same = jnp.logical_and(
        row_index[:, None] // frames == row_index[None, :] // frames,
        row_clip[:, None] == row_clip[None, :],
    )
    bias = jnp.where(same, 0.0, -1e30)

    def rows_of(patch, per_clip):
        return jnp.concatenate(
            [
                patch.reshape(count, width),
                per_clip,
                jnp.zeros((spare - clips, width), patch.dtype),
            ],
            0,
        ).astype(FULL)

    ups = [gather_shards(hidden_up[0])]
    downs = [gather_shards(hidden_down[0])]
    patch_rows = rows_of(patch_tokens, class_tokens)
    pieces_out = [((piece_rows, width), HALF)] * groups
    backs_out = [((back_rows, width), HALF)] * groups
    lane_buffer = pltpu.VMEM((width // 128, rows, 128), FULL)
    row_buffer = pltpu.VMEM((rows, width), FULL)
    square = pltpu.VMEM((width, width), HALF)
    wide = pltpu.VMEM((width, 3 * width), HALF)
    shards = pltpu.VMEM((groups, width, width), HALF)
    blocks = pltpu.VMEM((groups, back_rows, width), FULL)
    frame_rows = pltpu.VMEM((frames, width), FULL)
    saved = []
    for layer in range(layers):
        time = call(
            partial(time_forward, dims, layer),
            [
                ((rows, width), HALF),
                ((rows, 3 * width), HALF),
                ((rows, 128), FULL),
                ((rows, width), HALF),
                ((rows, width), HALF),
                ((rows, width), FULL),
            ]
            + pieces_out
            + [((spare, width), FULL)],
            [wide, square, square, lane_buffer, row_buffer, blocks, pltpu.SemaphoreType.DMA((3,))],
            [SMEM, VMEM, VMEM, VMEM, VMEM, ANY, ANY, ANY],
            14,
        )(place, patch_rows, bias, norm_gain, norm_shift, temporal_in, temporal_out, temporal_mix)
        space = call(
            partial(space_forward, dims, layer),
            [((span, width), HALF), ((span, 3 * width), HALF), ((span, 128), FULL)] + backs_out,
            [wide, pltpu.VMEM((span, width), FULL), pltpu.SemaphoreType.DMA((1,))],
            [SMEM, SMEM, VMEM] + [VMEM] * groups + [ANY],
            9,
        )(place, clip_of, time[10], *spread(time[6:10]), spatial_in)
        if layer + 1 < layers:
            later = lax.optimization_barrier((hidden_up[layer + 1], hidden_down[layer + 1], *space))
            ups.append(gather_shards(later[0]))
            downs.append(gather_shards(later[1]))
            space = later[2:]
        feed = call(
            partial(feed_forward, dims, layer),
            [
                ((rows, width), HALF),
                ((rows, width), FULL),
                ((rows, width), HALF),
                ((rows, hidden), HALF),
                ((rows, hidden), HALF),
                ((rows, width), FULL),
            ],
            [
                square,
                shards,
                shards,
                row_buffer,
                blocks,
                frame_rows,
                pltpu.VMEM((rows, width), HALF),
                pltpu.SemaphoreType.DMA((1,)),
                pltpu.SemaphoreType.DMA((12,)),
            ],
            [SMEM] + [VMEM] * groups + [VMEM] * 4 + [ANY] * 13,
            15,
        )(
            place, *spread(space[3:]), share, time[5], norm_gain, norm_shift, spatial_out,
            *ups[layer], *downs[layer],
        )
        saved.append((patch_rows, time, space, feed))
        patch_rows = feed[5]
    patch_output = patch_rows[:count].reshape(frames, patches, width).astype(HALF)
    class_output = patch_rows[count : count + clips].astype(HALF)

    grad_rows = rows_of(patch_cotangent, class_cotangent)
    near = blocks_dp <= 2 * NEAR
    flights = Flights()
    norms = [None] * layers

    def start(name, pairs, order, split, micros):
        if split and not near:
            flights.start(name, reduce_whole(pairs))
            return
        parts = outer_group(place, pairs, groups, blocks_dp, split, micros)
        if split:
            flights.start(name, reduce_attention(parts, order, [right.shape[1] for left, right in pairs]))
        elif near:
            flights.start(name, reduce_group(parts, order))
        else:
            flights.start(name, reduce_far(parts))

    for layer in reversed(range(layers)):
        first, time, space, feed = saved[layer]
        last = layer == 0
        feed_back = call(
            partial(feed_backward, dims, layer),
            [
                ((rows, width), HALF),
                ((rows, hidden), HALF),
                ((rows, width), HALF),
                ((rows, width), FULL),
                ((8, width), FULL),
            ]
            + pieces_out
            + [((8, width), FULL)],
            [
                square,
                shards,
                shards,
                row_buffer,
                row_buffer,
                blocks,
                pltpu.SemaphoreType.DMA((1,)),
                pltpu.SemaphoreType.DMA((12,)),
            ],
            [SMEM, SMEM] + [VMEM] * 5 + [ANY] * 13,
            23,
        )(
            place, clip_of, grad_rows, feed[4], feed[1],
            jnp.broadcast_to(inverse_counts[:, None], (spare, 128)), norm_gain, spatial_out,
            *ups[layer], *downs[layer],
        )
        update, grad_hidden, branch, back, feed_norms = feed_back[:5]
        arrived = spread(feed_back[5:9])
        pairs = ((feed[2], grad_hidden), (update, feed[3]))
        if last:
            pairs = flights.land(("feed1", "space1"), pairs)
            start("up0", pairs[:1], (0, 2, 1), False, 10)
            start("down0", pairs[1:], (2, 0, 1), False, 10)
            arrived = flights.land(("space1", "time1"), arrived)
        else:
            start("feed1", pairs, (2, 1, 0), False, 19)
        space_back = call(
            partial(space_backward, dims, layer),
            [((span, 3 * width), HALF)] + backs_out,
            [
                wide,
                pltpu.VMEM((span, width), FULL),
                pltpu.VMEM((span, width), HALF),
                pltpu.SemaphoreType.DMA((1,)),
            ],
            [VMEM] * groups + [VMEM] * 3 + [ANY],
            29,
        )(*arrived, feed_back[9], space[1], space[2], spatial_in)
        arrived = spread(space_back[1:])
        pairs = ((space[0], space_back[0]), (feed[0], branch))
        if last:
            pairs = flights.land(("up0", "down0"), pairs)
            start("space0", pairs, (2, 0, 1), True, 11)
            arrived = flights.land(("feed1", "space1", "time1"), arrived)
        else:
            pairs = flights.land(("feed1",), pairs)
            start("space1", pairs, (0, 2, 1), True, 11)
        time_back = call(
            partial(time_backward, dims, layer),
            [
                ((rows, width), HALF),
                ((rows, width), HALF),
                ((rows, 3 * width), HALF),
                ((rows, width), FULL),
                ((8, width), FULL),
            ],
            [
                wide,
                square,
                square,
                lane_buffer,
                row_buffer,
                blocks,
                frame_rows,
                pltpu.VMEM((rows, width), HALF),
                pltpu.SemaphoreType.DMA((3,)),
            ],
            [SMEM] + [VMEM] * groups + [VMEM] * 8 + [ANY] * 3,
            14,
        )(
            place, *arrived, member, back, time[5], first, time[1], time[2], bias,
            norm_gain, temporal_in, temporal_out, temporal_mix,
        )
        grad_rows = time_back[3]
        norms[layer] = (time_back[4], feed_norms)
        pairs = ((time[0], time_back[2]), (time[3], time_back[1]), (time[4], time_back[0]))
        if last:
            pairs = flights.land(("feed1", "space1", "space0", "up0", "down0"), pairs)
            ordered = [
                entry[at : at + 1]
                for part, at in ((0, 2), (0, 0), (1, 0), (0, 3), (0, 1), (1, 1))
                for entry in [norms[index][part] for index in range(layers)]
            ]
            flights.start("norms", reduce_norms(jnp.concatenate(ordered, 0)))
            start("others0", pairs[1:], (2, 0, 1), True, 8)
            start("time0", pairs[:1], (0, 2, 1), True, 8)
        else:
            start("time1", pairs, (0, 2, 1), True, 15)
            grad_rows = flights.land(("space1",), grad_rows)
    flights.finish()
    results = flights.results
    lanes = width // blocks_dp

    norm_sums = results["norms"].reshape(2, 3, layers, lanes).transpose(0, 2, 1, 3)
    time_sums = (results["time0"] + results["others0"], results["time1"])
    space_sums = (results["space0"], results["space1"])
    gradients = (
        *[jnp.stack([sums[index] for sums in time_sums]) for index in range(3)],
        *[jnp.stack([sums[index] for sums in space_sums]) for index in range(2)],
        jnp.stack([results["up0"], results["feed1"][:, :width]]),
        jnp.stack([results["down0"].T, results["feed1"][:, width:].T]),
        norm_sums[0],
        norm_sums[1],
    )
    patch_grad = grad_rows[:count].reshape(frames, patches, width)
    class_grad = grad_rows[count : count + clips]
    return (patch_output, class_output, patch_grad, class_grad, *gradients)


def solution(mesh):
    placed = (
        P(DP, TENSOR, None),
        P(DP, None),
        P(DP, None),
        P(DP, TENSOR, None),
        P(DP, None),
        P(),
        P(),
        P(),
        P(),
        P(),
        P(None, None, TENSOR),
        P(None, TENSOR, None),
        P(),
        P(),
    )
    return jax.shard_map(
        body,
        mesh=mesh,
        in_specs=placed,
        out_specs=(
            P(DP, TENSOR, None),
            P(DP, None),
            P(DP, TENSOR, None),
            P(DP, None),
            P(None, DP, None),
            P(None, DP, None),
            P(None, DP, None),
            P(None, DP, None),
            P(None, DP, None),
            P(None, DP, TENSOR),
            P(None, TENSOR, DP),
            P(None, None, DP),
            P(None, None, DP),
        ),
        check_vma=False,
    )
```

```python
from functools import partial

import jax
import jax.numpy as jnp
from jax import lax
from jax.experimental import pallas as pl
from jax.experimental.pallas import tpu as pltpu
from jax.sharding import PartitionSpec as P

HEADS = 12
EPS = 1e-06
HIGH = lax.Precision.HIGHEST
HALF = jnp.bfloat16
FULL = jnp.float32
NEAR = 4
TENSOR = "tensor"
DP = "dp"
TILE = 256
VMEM_BYTES = 58 << 20
SMEM = pl.BlockSpec(memory_space=pltpu.SMEM)
SMALL, ROWS, FAR = range(3)
HBM = pl.BlockSpec(memory_space=pltpu.HBM)
ROOT_HALF = 0.5**0.5
DENSITY = (2.0 * 3.141592653589793) ** -0.5


def up_to(value, step):
    return -(-value // step) * step


def dot(left, right):
    return jnp.dot(left, right, preferred_element_type=FULL)


def dot_back(left, right):
    return lax.dot_general(left, right, (((1,), (1,)), ((), ())), preferred_element_type=FULL)


def dot_outer(left, right):
    return lax.dot_general(left, right, (((0,), (0,)), ((), ())), preferred_element_type=FULL)


def unit_of(values):
    centred = values - jnp.mean(values, -1, keepdims=True)
    inverse = lax.rsqrt(jnp.mean(centred * centred, -1, keepdims=True) + EPS)
    return centred * inverse, inverse


def unit_back(grad, unit, inverse, gain):
    scaled = grad * gain
    inner = (
        scaled
        - jnp.mean(scaled, -1, keepdims=True)
        - unit * jnp.mean(scaled * unit, -1, keepdims=True)
    )
    return inner * inverse


def head_lanes(head_size, half):
    lane = lax.broadcasted_iota(jnp.int32, (1, 2 * head_size), 1)
    return (lane // head_size) == half


def over_rows(rows, step, run):
    for start in range(0, rows, step):
        run(start, min(step, rows - start))


def two_heads(values, head_size):
    return jnp.concatenate(
        [jnp.where(head_lanes(head_size, half), values, 0) for half in range(2)], 0
    )


def one_of_two(values, head_size):
    rows = values.shape[0] // 2
    return jnp.where(head_lanes(head_size, 0), values[:rows], values[rows:])


def interleave(order, frame, frames, values):
    for group in range(order.shape[0]):
        part = values[:, group * 128 : (group + 1) * 128]
        order[group, pl.ds(frame, values.shape[0], stride=frames), :] = part


def pick(order, frame, frames, patches):
    own = pl.ds(frame, patches, stride=frames)
    return jnp.concatenate([order[group, own, :] for group in range(order.shape[0])], 1)


def shard_copies(place_ref, refs, target, which):
    own, core, far_first, far_second, core_first, core_second = refs
    half = far_first.shape[1]
    first = pl.multiple_of(place_ref[1] * half, half)
    second = pl.multiple_of((1 - place_ref[1]) * half, half)
    return [
        [(own, target.at[0])],
        [(core.at[which], target.at[1])],
        [
            (far_first.at[which], target.at[2, pl.ds(first, half)]),
            (far_second.at[which], target.at[2, pl.ds(second, half)]),
        ],
        [
            (core_first.at[which], target.at[3, pl.ds(first, half)]),
            (core_second.at[which], target.at[3, pl.ds(second, half)]),
        ],
    ]


def start_shards(place_ref, own, peers, up_ref, down_ref, sems):
    waits = []
    index = 0
    for pairs in zip(
        shard_copies(place_ref, (own[0],) + peers, up_ref, 0),
        shard_copies(place_ref, (own[1],) + peers, down_ref, 1),
    ):
        group = []
        for source, target in pairs[0] + pairs[1]:
            copy = pltpu.make_async_copy(source, target, sems.at[index])
            copy.start()
            group.append(copy)
            index += 1
        waits.append(group)
    return waits


def fetch(sources, targets, sems):
    copies = [
        pltpu.make_async_copy(source, target, sems.at[index])
        for index, (source, target) in enumerate(zip(sources, targets))
    ]
    for copy in copies:
        copy.start()
    return copies


def attend_forward(load, store, store_total, heads, head_size, bias):
    scale = head_size**-0.5
    totals = None
    if bias.shape[0] > 1:
        bias = jnp.concatenate([bias, bias], 0)
    for pair in range(heads // 2):
        query, key, value = (load(part, pair) for part in range(3))
        rows = query.shape[0]
        scores = dot_back(two_heads(query, head_size), key) * scale + bias
        top = jnp.max(scores, -1, keepdims=True)
        raised = jnp.exp(scores - top)
        total = jnp.sum(raised, -1, keepdims=True)
        mixed = dot(raised.astype(HALF), value) * (1.0 / total)
        log_total = top + jnp.log(total)
        if totals is None:
            lanes = lax.broadcasted_iota(jnp.int32, (rows, 128), 1)
            totals = jnp.zeros(lanes.shape, FULL)
        totals = jnp.where(lanes == pair * 2, log_total[:rows], totals)
        totals = jnp.where(lanes == pair * 2 + 1, log_total[rows:], totals)
        store(pair, one_of_two(mixed, head_size))
    store_total(totals)


def attend_backward(load, load_grad, totals, store, heads, head_size, bias):
    scale = head_size**-0.5
    totals = totals.T
    if bias.shape[1] > 1:
        bias = jnp.concatenate([bias, bias], 1)
    for pair in range(heads // 2):
        query, key, value = (load(part, pair) for part in range(3))
        query = two_heads(query, head_size)
        grad = two_heads(load_grad(pair), head_size)
        total = jnp.concatenate([totals[2 * pair + half : 2 * pair + half + 1] for half in range(2)], 1)
        prob = jnp.exp(dot_back(key, query) * scale + (bias - total))
        grad_prob = dot_back(value, grad)
        delta = jnp.sum(prob * grad_prob, 0, keepdims=True)
        grad_score = (prob * (grad_prob - delta)).astype(HALF)
        store(0, pair, one_of_two(dot_outer(grad_score, key), head_size) * scale)
        store(1, pair, dot(grad_score, query) * scale)
        store(2, pair, dot(prob.astype(HALF), grad))


def row_blocks(rows, step):
    return [(start, min(step, rows - start)) for start in range(0, rows, step)]


def time_forward(dims, layer, place_ref, x_ref, bias_ref, gain_ref, shift_ref, in_hbm, out_hbm, mix_hbm,
                 normed_ref, triple_ref, total_ref, mixed_ref, projected_ref, after_ref,
                 send0, send1, send2, send3, class_ref,
                 in_ref, out_ref, mix_ref, order, plain, blocks, sems):
    frames, patches, width, heads, groups = dims
    count = frames * patches
    rows = x_ref.shape[0]
    step = bias_ref.shape[0]
    copies = fetch(
        (in_hbm.at[layer], out_hbm.at[layer], mix_hbm.at[layer]), (in_ref, out_ref, mix_ref), sems
    )
    gain = gain_ref[layer, 0:1, :]
    shift = shift_ref[layer, 0:1, :]
    for frame in range(frames):
        unit, unused = unit_of(x_ref[frame * patches : (frame + 1) * patches, :])
        interleave(order, frame, frames, unit * gain + shift)
    for group in range(width // 128):
        order[group, count:, :] = jnp.zeros((rows - count, 128), FULL)
        normed_ref[:, group * 128 : (group + 1) * 128] = order[group].astype(HALF)
    normed_ref.flush()
    copies[0].wait()
    for column in range(0, 3 * width, TILE):
        part = slice(column, column + TILE)
        triple_ref[:, part] = dot(normed_ref[...], in_ref[:, part]).astype(HALF)
    triple_ref.flush()
    for begin, size in row_blocks(rows, step):
        own = slice(begin, begin + size)

        def load(part, pair):
            start = part * width + pair * 128
            return triple_ref[own, start : start + 128]

        def store(pair, mixed):
            order[pair, own, :] = mixed

        def store_total(totals):
            total_ref[own, :] = totals

        attend_forward(
            load, store, store_total, heads, width // heads, bias_ref[0:size, 0:size]
        )
    for frame in range(frames):
        plain[frame * patches : (frame + 1) * patches, :] = pick(order, frame, frames, patches)
    plain[count:, :] = jnp.zeros((rows - count, width), FULL)
    mixed_ref[...] = plain[...].astype(HALF)
    mixed_ref.flush()
    copies[1].wait()
    for column in range(0, width, TILE):
        part = slice(column, column + TILE)
        projected_ref[:, part] = dot(mixed_ref[...], out_ref[:, part]).astype(HALF)
    projected_ref.flush()
    copies[2].wait()
    for column in range(0, width, TILE):
        part = slice(column, column + TILE)
        after_ref[:, part] = x_ref[:, part] + dot(projected_ref[...], mix_ref[:, part])
    after_ref.flush()
    gain = gain_ref[layer, 1:2, :]
    shift = shift_ref[layer, 1:2, :]

    def norm(start, size):
        own = slice(start, start + size)
        unit, unused = unit_of(after_ref[own, :])
        plain[own, :] = unit * gain + shift

    over_rows(rows, 80, norm)
    send_blocks(plain, blocks, (send0, send1, send2, send3), place_ref[0], count // groups)
    class_ref[...] = plain[count:, :]


def send_blocks(plain, blocks, sends, place, size):
    groups = len(sends)
    for group in range(groups):
        blocks[group, 0:size, :] = plain[group * size : (group + 1) * size, :]
    for away in range(groups):
        sends[away][...] = blocks[place ^ away][0:size].astype(HALF)


def space_forward(dims, layer, place_ref, clip_ref, class_ref, piece0, piece1, piece2, piece3, in_hbm,
                  normed_ref, triple_ref, total_ref, send0, send1, send2, send3,
                  in_ref, plain, sems):
    frames, patches, width, heads, groups = dims
    own_frames = frames // groups
    seq = groups * patches
    rows = normed_ref.shape[0] // own_frames
    copies = fetch((in_hbm.at[layer],), (in_ref,), sems)
    pieces = [piece0, piece1, piece2, piece3]
    for away, piece in enumerate(pieces):
        values = piece[...].astype(FULL)
        for frame in range(own_frames):
            start = frame * rows + away * patches
            plain[start : start + patches, :] = values[frame * patches : (frame + 1) * patches]
    for frame in range(own_frames):
        start = frame * rows + seq
        plain[start : start + rows - seq, :] = jnp.zeros((rows - seq, width), FULL)
        clip = clip_ref[place_ref[0] * own_frames + frame]
        plain[start : start + 1, :] = class_ref[pl.ds(clip, 1), :]
    normed_ref[...] = plain[...].astype(HALF)
    normed_ref.flush()
    copies[0].wait()
    for column in range(0, 3 * width, TILE):
        part = slice(column, column + TILE)
        triple_ref[:, part] = dot(normed_ref[...], in_ref[:, part]).astype(HALF)
    triple_ref.flush()
    keys = lax.broadcasted_iota(jnp.int32, (1, rows), 1)
    bias = jnp.where(keys <= seq, 0.0, -1e30)

    for frame in range(own_frames):
        own = slice(frame * rows, (frame + 1) * rows)

        def load(part, pair):
            start = part * width + pair * 128
            return triple_ref[own, start : start + 128]

        def store(pair, mixed):
            plain[own, pair * 128 : (pair + 1) * 128] = mixed

        def store_total(totals):
            total_ref[own, :] = totals

        attend_forward(load, store, store_total, heads, width // heads, bias)
    return_pieces(plain, (send0, send1, send2, send3), own_frames, patches, rows)


def return_pieces(plain, sends, own_frames, patches, rows):
    seq = len(sends) * patches
    tail = []
    for frame in range(own_frames):
        row = plain[frame * rows + seq : frame * rows + seq + 1, :]
        high = row.astype(HALF).astype(FULL)
        tail += [high, row - high]
    size = own_frames * patches
    spare = sends[0].shape[0] - size - len(tail)
    tail.append(jnp.zeros((spare, plain.shape[1]), FULL))
    for away, send in enumerate(sends):
        kept = [
            plain[frame * rows + away * patches : frame * rows + (away + 1) * patches, :]
            for frame in range(own_frames)
        ]
        send[...] = jnp.concatenate(kept + tail, 0).astype(HALF)


def take_pieces(pieces, blocks, plain, frame_rows, place, size, own_frames):
    for away, piece in enumerate(pieces):
        blocks[place ^ away] = piece[...].astype(FULL)
    for group in range(len(pieces)):
        plain[group * size : (group + 1) * size, :] = blocks[group, 0:size, :]
        for frame in range(own_frames):
            start = size + 2 * frame
            frame_rows[group * own_frames + frame : group * own_frames + frame + 1, :] = (
                blocks[group, start : start + 1, :] + blocks[group, start + 1 : start + 2, :]
            )


def feed_forward(dims, layer, place_ref, piece0, piece1, piece2, piece3, share_ref, after_ref,
                 gain_ref, shift_ref, out_hbm,
                 up_hbm, down_hbm, peer1, peer2, peer3, peer4, peer5,
                 mixed_ref, rows_ref, normed_ref, active_ref, slope_ref, next_ref,
                 out_ref, up_ref, down_ref, plain, blocks, frame_rows, whole, out_sem, sems):
    frames, patches, width, heads, groups = dims
    count = frames * patches
    rows = after_ref.shape[0]
    size = count // groups
    place = place_ref[0]
    copies = fetch((out_hbm.at[layer],), (out_ref,), out_sem)
    own = (up_hbm.at[layer], down_hbm.at[layer])
    peers = (peer1, peer2, peer3, peer4, peer5)
    shards = start_shards(place_ref, own, peers, up_ref, down_ref, sems)
    take_pieces(
        (piece0, piece1, piece2, piece3), blocks, plain, frame_rows, place, size, frames // groups
    )
    plain[count:, :] = jnp.dot(
        share_ref[...], frame_rows[...], precision=HIGH, preferred_element_type=FULL
    )
    whole[...] = plain[...].astype(HALF)
    leader = jnp.where(place == 0, 1.0, 0.0).astype(FULL)
    kept = lax.broadcasted_iota(jnp.int32, (rows, 1), 0) < count
    kept = jnp.where(kept, 1.0, leader)
    mixed_ref[...] = (plain[...] * kept).astype(HALF)
    mixed_ref.flush()
    copies[0].wait()
    for column in range(0, width, TILE):
        part = slice(column, column + TILE)
        rows_ref[:, part] = after_ref[:, part] + dot(whole[...], out_ref[:, part])
    rows_ref.flush()
    gain = gain_ref[layer, 2:3, :]
    shift = shift_ref[layer, 2:3, :]

    def norm(start, size):
        own = slice(start, start + size)
        unit, unused = unit_of(rows_ref[own, :])
        plain[own, :] = unit * gain + shift

    over_rows(rows, 80, norm)
    whole[...] = plain[...].astype(HALF)
    normed_ref[...] = (plain[...] * kept).astype(HALF)
    normed_ref.flush()
    next_ref[...] = rows_ref[...]
    for away in range(groups):
        for copy in shards[away]:
            copy.wait()
        for column in range(0, width, TILE):
            part = slice(column, column + TILE)
            hidden = dot(whole[...], up_ref[away, :, part])
            below = 0.5 + 0.5 * lax.erf(hidden * ROOT_HALF)
            active = (hidden * below).astype(HALF)
            slope = below + hidden * (jnp.exp(hidden * hidden * -0.5) * DENSITY)
            start = away * width + column
            active_ref[:, start : start + TILE] = active
            slope_ref[:, start : start + TILE] = slope.astype(HALF)
        own = slice(away * width, (away + 1) * width)
        for column in range(0, width, TILE):
            part = slice(column, column + TILE)
            next_ref[:, part] += dot(active_ref[:, own], down_ref[away, :, part])
        end = count // 16 * 16
        active_ref[end:, own] = (active_ref[end:, own].astype(FULL) * kept[end:]).astype(HALF)
        active_ref.flush(own)
        slope_ref.flush(own)


def feed_backward(dims, layer, place_ref, clip_ref, grad_ref, slope_ref, rows_ref, share_ref, gain_ref,
                  out_hbm, up_hbm, down_hbm, peer1, peer2, peer3, peer4, peer5,
                  update_ref, hidden_ref, branch_ref, back_ref, norms_ref,
                  send0, send1, send2, send3, class_ref,
                  out_ref, up_ref, down_ref, total, plain, blocks, out_sem, sems):
    frames, patches, width, heads, groups = dims
    count = frames * patches
    rows = grad_ref.shape[0]
    place = place_ref[0]
    own_frames = frames // groups
    own = (up_hbm.at[layer], down_hbm.at[layer])
    peers = (peer1, peer2, peer3, peer4, peer5)
    shards = start_shards(place_ref, own, peers, up_ref, down_ref, sems)
    copies = fetch((out_hbm.at[layer],), (out_ref,), out_sem)
    update_ref[...] = grad_ref[...].astype(HALF)
    update_ref.flush()
    for away in range(groups):
        for copy in shards[away]:
            copy.wait()
        for column in range(0, width, TILE):
            part = slice(column, column + TILE)
            start = away * width + column
            grad_active = dot_back(update_ref[...], down_ref[away, part, :])
            slope = slope_ref[:, start : start + TILE].astype(FULL)
            grad_hidden = (grad_active * slope).astype(HALF)
            hidden_ref[:, start : start + TILE] = grad_hidden
        own = slice(away * width, (away + 1) * width)
        for column in range(0, width, TILE):
            part = slice(column, column + TILE)
            term = dot_back(hidden_ref[:, own], up_ref[away, part, :])
            if away == 0:
                total[:, part] = term
            else:
                total[:, part] += term
        hidden_ref.flush(own)
    gain = gain_ref[layer, 2:3, :]
    leader = jnp.where(place == 0, 1.0, 0.0).astype(FULL)
    norms_ref[...] = jnp.zeros(norms_ref.shape, FULL)
    def norm(start, size):
        own = slice(start, start + size)
        unit, inverse = unit_of(rows_ref[own, :])
        grad = total[own, :]
        back = grad_ref[own, :] + unit_back(grad, unit, inverse, gain)
        back_ref[own, :] = back
        branch_ref[own, :] = back.astype(HALF)
        kept = lax.broadcasted_iota(jnp.int32, (size, 1), 0) + start < count
        grad = jnp.where(kept, grad, grad * leader)
        norms_ref[0:1, :] += jnp.sum(grad * unit, 0, keepdims=True)
        norms_ref[1:2, :] += jnp.sum(grad, 0, keepdims=True)

    over_rows(rows, 80, norm)
    back_ref.flush()
    branch_ref.flush()
    copies[-1].wait()
    for column in range(0, width, TILE):
        part = slice(column, column + TILE)
        plain[:, part] = dot_back(branch_ref[...], out_ref[part, :])
    send_blocks(plain, blocks, (send0, send1, send2, send3), place, count // groups)
    for frame in range(own_frames):
        clip = clip_ref[place * own_frames + frame]
        class_ref[frame : frame + 1, :] = (
            plain[pl.ds(count + clip, 1), :] * share_ref[pl.ds(clip, 1), 0:1]
        )


def space_backward(dims, layer, piece0, piece1, piece2, piece3, class_ref, triple_ref, total_ref, in_hbm,
                   grad_ref, send0, send1, send2, send3,
                   in_ref, plain, mixed, sems):
    frames, patches, width, heads, groups = dims
    own_frames = frames // groups
    seq = groups * patches
    rows = triple_ref.shape[0] // own_frames
    copies = fetch((in_hbm.at[layer],), (in_ref,), sems)
    for away, piece in enumerate((piece0, piece1, piece2, piece3)):
        values = piece[...].astype(FULL)
        for frame in range(own_frames):
            start = frame * rows + away * patches
            plain[start : start + patches, :] = values[frame * patches : (frame + 1) * patches]
    for frame in range(own_frames):
        start = frame * rows + seq
        plain[start : start + rows - seq, :] = jnp.zeros((rows - seq, width), FULL)
        plain[start : start + 1, :] = class_ref[frame : frame + 1, :]
    mixed[...] = plain[...].astype(HALF)
    keys = lax.broadcasted_iota(jnp.int32, (rows, 1), 0)
    bias = jnp.where(keys <= seq, 0.0, -1e30)
    for frame in range(own_frames):
        own = slice(frame * rows, (frame + 1) * rows)

        def load(part, pair):
            start = part * width + pair * 128
            return triple_ref[own, start : start + 128]

        def load_grad(pair):
            return mixed[own, pair * 128 : (pair + 1) * 128]

        def store(part, pair, grad):
            start = part * width + pair * 128
            grad_ref[own, start : start + 128] = grad.astype(HALF)

        attend_backward(load, load_grad, total_ref[own, :], store, heads, width // heads, bias)
    grad_ref.flush()
    copies[0].wait()
    for column in range(0, width, TILE):
        part = slice(column, column + TILE)
        plain[:, part] = dot_back(grad_ref[...], in_ref[part, :])
    return_pieces(plain, (send0, send1, send2, send3), own_frames, patches, rows)


def time_backward(dims, layer, place_ref, piece0, piece1, piece2, piece3, member_ref, back_ref, after_ref, x_ref,
                  triple_ref, total_ref, bias_ref, gain_ref, in_hbm, out_hbm, mix_hbm,
                  branch_ref, projected_ref, grad_ref, next_ref, norms_ref,
                  in_ref, out_ref, mix_ref, order, plain, blocks, frame_rows, mixed, sems):
    frames, patches, width, heads, groups = dims
    count = frames * patches
    rows = x_ref.shape[0]
    step = bias_ref.shape[0]
    place = place_ref[0]
    copies = fetch(
        (mix_hbm.at[layer], out_hbm.at[layer], in_hbm.at[layer]), (mix_ref, out_ref, in_ref), sems
    )
    take_pieces(
        (piece0, piece1, piece2, piece3),
        blocks,
        plain,
        frame_rows,
        place,
        count // groups,
        frames // groups,
    )
    plain[count:, :] = jnp.dot(
        member_ref[...], frame_rows[...], precision=HIGH, preferred_element_type=FULL
    )
    leader = jnp.where(place == 0, 1.0, 0.0).astype(FULL)
    norms_ref[...] = jnp.zeros(norms_ref.shape, FULL)
    gain = gain_ref[layer, 1:2, :]

    def space_norm(start, size):
        own = slice(start, start + size)
        unit, inverse = unit_of(after_ref[own, :])
        grad = plain[own, :]
        back = back_ref[own, :] + unit_back(grad, unit, inverse, gain)
        next_ref[own, :] = back
        kept = lax.broadcasted_iota(jnp.int32, (size, 1), 0) + start < count
        branch_ref[own, :] = jnp.where(kept, back, 0.0).astype(HALF)
        grad = jnp.where(kept, grad, grad * leader)
        norms_ref[0:1, :] += jnp.sum(grad * unit, 0, keepdims=True)
        norms_ref[1:2, :] += jnp.sum(grad, 0, keepdims=True)

    over_rows(rows, 80, space_norm)
    branch_ref.flush()
    copies[0].wait()
    for column in range(0, width, TILE):
        part = slice(column, column + TILE)
        projected_ref[:, part] = dot_back(branch_ref[...], mix_ref[part, :]).astype(HALF)
    projected_ref.flush()
    copies[1].wait()
    for column in range(0, width, TILE):
        part = slice(column, column + TILE)
        plain[:, part] = dot_back(projected_ref[...], out_ref[part, :])
    for frame in range(frames):
        interleave(order, frame, frames, plain[frame * patches : (frame + 1) * patches, :])
    for group in range(width // 128):
        order[group, count:, :] = jnp.zeros((rows - count, 128), FULL)
        mixed[:, group * 128 : (group + 1) * 128] = order[group].astype(HALF)

    for begin, size in row_blocks(rows, step):
        own = slice(begin, begin + size)

        def load(part, pair):
            start = part * width + pair * 128
            return triple_ref[own, start : start + 128]

        def load_grad(pair):
            return mixed[own, pair * 128 : (pair + 1) * 128]

        def store(part, pair, grad):
            start = part * width + pair * 128
            grad_ref[own, start : start + 128] = grad.astype(HALF)

        attend_backward(
            load,
            load_grad,
            total_ref[own, :],
            store,
            heads,
            width // heads,
            bias_ref[0:size, 0:size],
        )
    grad_ref.flush()
    copies[2].wait()
    for column in range(0, width, TILE):
        part = slice(column, column + TILE)
        grad = dot_back(grad_ref[...], in_ref[part, :])
        for group in range(TILE // 128):
            order[column // 128 + group] = grad[:, group * 128 : (group + 1) * 128]
    gain = gain_ref[layer, 0:1, :]
    for frame in range(frames):
        own = slice(frame * patches, (frame + 1) * patches)
        grad = pick(order, frame, frames, patches)
        unit, inverse = unit_of(x_ref[own, :])
        next_ref[own, :] += unit_back(grad, unit, inverse, gain)
        norms_ref[2:3, :] += jnp.sum(grad * unit, 0, keepdims=True)
        norms_ref[3:4, :] += jnp.sum(grad, 0, keepdims=True)


def cost(micros):
    return pl.CostEstimate(flops=micros, bytes_accessed=micros, transcendentals=0)


class Fetched:
    def __init__(self, source, target, sem):
        self.target, self.shape = target, target.shape
        self.copy = pltpu.make_async_copy(source, target, sem)
        self.copy.start()

    def wait(self):
        if self.copy is not None:
            self.copy.wait()
            self.copy = None

    def __getitem__(self, index):
        self.wait()
        return self.target[index]


class Written:
    def __init__(self, source, target, sems):
        self.source, self.target, self.sems = source, target, sems
        self.shape = source.shape
        self.copies = []

    def __getitem__(self, index):
        return self.source[index]

    def __setitem__(self, index, values):
        self.source[index] = values

    def flush(self, columns=None):
        parts = (self.source, self.target)
        if columns is not None:
            parts = tuple(ref.at[:, columns] for ref in parts)
        copy = pltpu.make_async_copy(*parts, self.sems.at[len(self.copies)])
        copy.start()
        self.copies.append(copy)

    def wait(self):
        if not self.copies:
            self.flush()
        for copy in self.copies:
            copy.wait()


def call(kernel, outs, scratch, specs, micros):
    def run(*arrays):
        fetched = [index for index, kind in enumerate(specs) if kind == ROWS]
        count, results = len(specs), len(outs)

        def whole(*refs):
            ins, out_refs = list(refs[:count]), refs[count : count + results]
            rest = refs[count + results :]
            in_refs, rest = rest[: len(fetched)], rest[len(fetched) :]
            kept, rest = rest[:results], rest[results:]
            in_sems, out_sems = rest[0], rest[1]
            for place, index in enumerate(fetched):
                ins[index] = Fetched(ins[index], in_refs[place], in_sems.at[place])
            written = [
                Written(source, target, out_sems.at[index])
                for index, (source, target) in enumerate(zip(kept, out_refs))
            ]
            kernel(*ins, *written, *rest[2:])
            for index in fetched:
                ins[index].wait()
            for result in written:
                result.wait()

        return pl.pallas_call(
            whole,
            out_shape=[jax.ShapeDtypeStruct(shape, kind) for shape, kind in outs],
            in_specs=[SMEM if kind == SMALL else HBM for kind in specs],
            out_specs=[HBM] * results,
            scratch_shapes=[pltpu.VMEM(arrays[index].shape, arrays[index].dtype) for index in fetched]
            + [pltpu.VMEM(shape, kind) for shape, kind in outs]
            + [pltpu.SemaphoreType.DMA((len(fetched),)), pltpu.SemaphoreType.DMA((results, 4))]
            + scratch,
            compiler_params=pltpu.CompilerParams(vmem_limit_bytes=VMEM_BYTES),
            cost_estimate=cost(micros),
        )(*arrays)

    return run


def outer_group(place, pairs, groups, split, micros):
    rows = pairs[0][0].shape[1]
    parts = 2 if split else groups
    inner = parts // 2
    sizes = [right.shape[1] // parts for left, right in pairs]
    total = sum(sizes)
    tiles = []
    for side in range(2):
        for index, size in enumerate(sizes):
            for shard in range(inner):
                for start in range(0, size, 768):
                    tiles.append((side, index, shard, start, min(768, size - start)))
    count = len(pairs)

    def kernel(place_ref, *refs):
        lefts, rights = refs[:count], refs[count : 2 * count]
        outs = refs[2 * count : 2 * count + 2]
        left_refs = refs[2 * count + 2 : 3 * count + 2]
        right_refs, stage, left_sems, right_sems, out_sems = refs[3 * count + 2 :]
        arrivals = []
        lefts_here = []
        for number, (side, index, shard, start, size) in enumerate(tiles):
            if index == len(lefts_here):
                copy = pltpu.make_async_copy(lefts[index], left_refs[index], left_sems.at[index])
                copy.start()
                lefts_here.append(copy)
            if split:
                part = jnp.where(place_ref[0] % 2 == 0, 1 - side, side)
                begin = pl.multiple_of(part * sizes[index] + start, 128)
            else:
                begin = (2 * shard + 1 - side) * sizes[index] + start
            copy = pltpu.make_async_copy(
                rights[index].at[:, pl.ds(begin, size)],
                right_refs.at[number, pl.ds(0, rights[index].shape[0]), pl.ds(0, size)],
                right_sems.at[number],
            )
            copy.start()
            arrivals.append(copy)
        leaving = []
        waited = [False] * count
        for number, (side, index, shard, start, size) in enumerate(tiles):
            if not waited[index]:
                lefts_here[index].wait()
                waited[index] = True
            arrivals[number].wait()
            depth = lefts[index].shape[0]
            terms = dot_outer(left_refs[index][...], right_refs[number, 0:depth, 0:size])
            stage[number, :, 0:size] = terms.astype(HALF)
            column = sum(sizes[:index]) + start
            target = outs[side] if split else outs[side].at[shard]
            copy = pltpu.make_async_copy(
                stage.at[number, :, pl.ds(0, size)],
                target.at[:, pl.ds(column, size)],
                out_sems.at[number],
            )
            copy.start()
            leaving.append(copy)
        for copy in leaving:
            copy.wait()

    shape = (rows, total) if split else (inner, rows, total)
    lefts, rights = zip(*pairs)
    width = max(tile[4] for tile in tiles)
    return pl.pallas_call(
        kernel,
        out_shape=[jax.ShapeDtypeStruct(shape, HALF)] * 2,
        in_specs=[SMEM] + [HBM] * (2 * count),
        out_specs=[HBM] * 2,
        scratch_shapes=[pltpu.VMEM(left.shape, HALF) for left in lefts]
        + [
            pltpu.VMEM((len(tiles), max(left.shape[0] for left in lefts), width), HALF),
            pltpu.VMEM((len(tiles), rows, width), HALF),
            pltpu.SemaphoreType.DMA((count,)),
            pltpu.SemaphoreType.DMA((len(tiles),)),
            pltpu.SemaphoreType.DMA((len(tiles),)),
        ],
        compiler_params=pltpu.CompilerParams(vmem_limit_bytes=VMEM_BYTES),
        cost_estimate=cost(micros),
    )(place, *lefts, *rights)


def exchange(axis, bit):
    return (axis, [(index, index ^ bit) for index in range(lax.axis_size(axis))])


def shift(step):
    far = lax.axis_size(DP) // 2
    return (
        DP,
        [
            (start * 2 + near, (start + step) % far * 2 + near)
            for start in range(far)
            for near in range(2)
        ],
    )


def swap(values, axis, bit):
    return lax.ppermute(values, *exchange(axis, bit))


def reduce_group(parts):
    send, keep = parts
    other = yield [(send, exchange(TENSOR, 1))]
    values = keep + other[0]
    columns = values.shape[-1]
    blocks = lax.axis_size(DP)
    far = blocks // 2
    near = lax.axis_index(DP) % 2
    place = lax.axis_index(DP) // 2
    middle = columns // 2 // 128 * 128
    if values.ndim == 3:
        values = values.reshape(2, far, 2, -1, columns)
        x_dim, y_dim, x_place = 0, 2, 0
    else:
        values = values.reshape(far, 2, 2, -1, columns)
        x_dim, y_dim, x_place = 2, 1, lax.axis_index(TENSOR) // 2
    over_x, over_y = values[..., :middle], values[..., middle:]

    def of_x(array, mine, dim):
        return lax.dynamic_index_in_dim(array, x_place if mine else 1 - x_place, dim, False)

    def of_y(array, mine, dim):
        return lax.dynamic_index_in_dim(array, near if mine else 1 - near, dim, False)

    other = yield [
        (of_x(over_x, False, x_dim), exchange(TENSOR, 2)),
        (of_y(over_y, False, y_dim), exchange(DP, 1)),
    ]
    over_x = of_x(over_x, True, x_dim) + other[0]
    over_y = of_y(over_y, True, y_dim) + other[1]
    y_dim -= x_dim < y_dim
    x_dim -= x_dim > 0
    other = yield [
        (of_y(over_x, False, y_dim), exchange(DP, 1)),
        (of_x(over_y, False, x_dim), exchange(TENSOR, 2)),
    ]
    values = jnp.concatenate(
        [of_y(over_x, True, y_dim) + other[0], of_x(over_y, True, x_dim) + other[1]], -1
    )
    others = yield [
        (lax.dynamic_index_in_dim(values, (place + step) % far, 0, False), shift(step))
        for step in range(1, far)
    ]
    total = lax.dynamic_index_in_dim(values, place, 0, False).astype(FULL)
    for other in others:
        total = total + other.astype(FULL)
    return total


def reduce_norms(values):
    count = lax.axis_size(DP)
    far = count // 2
    for axis, bit in ((TENSOR, 1), (TENSOR, 2), (DP, 1)):
        other = yield [(values, exchange(axis, bit))]
        values = values + other[0]
    others = yield [(values, shift(step)) for step in range(1, far)]
    for other in others:
        values = values + other
    lanes = values.shape[1] // count
    return lax.dynamic_slice_in_dim(values, lax.axis_index(DP) * lanes, lanes, 1)


def reduce_attention(parts, sizes):
    values = (yield from reduce_group(parts)).astype(HALF)
    other = yield [(values, exchange(TENSOR, 2))]
    values = in_order(values, other[0], 2, 0)
    other = yield [(values, exchange(TENSOR, 1))]
    matrices = []
    begin = 0
    for size in sizes:
        end = begin + size // 2
        matrices.append(in_order(values[:, begin:end], other[0][:, begin:end], 1, 1).astype(FULL))
        begin = end
    return matrices


def in_order(values, other, bit, dim):
    first = lax.axis_index(TENSOR) // bit % 2 == 0
    return jnp.where(
        first,
        jnp.concatenate([values, other], dim),
        jnp.concatenate([other, values], dim),
    )


def reduce_far(parts):
    send, keep = parts
    other = yield [(send, exchange(TENSOR, 1))]
    values = keep + other[0]
    other = yield [(values[1], exchange(TENSOR, 2))]
    values = values[0] + other[0]
    values = values.reshape(-1, values.shape[-1])
    return lax.psum_scatter(values, DP, scatter_dimension=0, tiled=True).astype(FULL)


def reduce_whole(pairs):
    totals = []
    for left, right in pairs:
        total = lax.psum(dot_outer(left, right).astype(HALF), TENSOR)
        total = lax.psum_scatter(total, DP, scatter_dimension=0, tiled=True)
        totals.append(total.astype(FULL))
    return totals


class Flights:
    def __init__(self):
        self.running = {}
        self.results = {}
        self.asked = {}

    def start(self, name, steps):
        self.asked[name] = (steps, next(steps))

    def leave(self, values):
        sends = [[send for send, way in asked] for steps, asked in self.asked.values()]
        values, sends = lax.optimization_barrier((values, sends))
        for (name, (steps, asked)), ready in zip(self.asked.items(), sends):
            self.running[name] = (
                steps,
                [lax.ppermute(send, *way) for send, (unused, way) in zip(ready, asked)],
            )
        self.asked = {}
        return values

    def land(self, names, values):
        names = [name for name in names if name in self.running]
        held = [self.running[name][1] for name in names]
        values, held = lax.optimization_barrier((values, held))
        for name, arrived in zip(names, held):
            steps = self.running.pop(name)[0]
            try:
                self.asked[name] = (steps, steps.send(arrived))
            except StopIteration as stop:
                self.results[name] = stop.value
        return self.leave(values)


def spread(pieces):
    return [pieces[0]] + [swap(piece, TENSOR, away) for away, piece in enumerate(pieces) if away]


def pass_on(values, way):
    arrived = yield [(values, way)]
    return arrived[0]


def both_matrices(hidden_up, hidden_down, layer, near=None):
    matrices = [hidden_up[layer], hidden_down[layer]]
    if near is not None:
        half = matrices[0].shape[0] // 2
        matrices = [lax.dynamic_slice_in_dim(rows, near * half, half, 0) for rows in matrices]
    return jnp.stack(matrices)


def body(
    patch_tokens,
    class_tokens,
    frame_counts,
    patch_cotangent,
    class_cotangent,
    temporal_in,
    temporal_out,
    temporal_mix,
    spatial_in,
    spatial_out,
    hidden_up,
    hidden_down,
    norm_gain,
    norm_shift,
):
    frames, patches, width = patch_tokens.shape
    clips = class_tokens.shape[0]
    layers = temporal_in.shape[0]
    groups = lax.axis_size(TENSOR)
    place = jnp.stack([lax.axis_index(TENSOR), lax.axis_index(DP) % 2]).astype(jnp.int32)
    blocks_dp = lax.axis_size(DP)
    dims = (frames, patches, width, HEADS, groups)
    count = frames * patches
    rows = up_to(count + up_to(clips, 8), 80)
    spare = rows - count
    own_frames = frames // groups
    seq = groups * patches
    frame_span = up_to(seq + 1, 16)
    span = own_frames * frame_span
    hidden = groups * hidden_up.shape[2]
    piece_rows = own_frames * patches
    back_rows = up_to(piece_rows + 2 * own_frames, 8)

    ends = jnp.cumsum(frame_counts[0])
    frame_index = jnp.arange(frames, dtype=jnp.int32)
    clip_of = jnp.sum((frame_index[:, None] >= ends[None, :]).astype(jnp.int32), 1)
    clip_index = jnp.arange(spare, dtype=jnp.int32)
    member = (clip_index[:, None] == clip_of[None, :]).astype(FULL)
    counts = jnp.concatenate([frame_counts[0].astype(FULL), jnp.ones((spare - clips,), FULL)])
    share = member / counts[:, None]
    inverse_counts = 1.0 / counts
    row_index = jnp.arange(128, dtype=jnp.int32)
    row_clip = jnp.sum(
        jnp.where(row_index[:, None] % frames == frame_index[None, :], clip_of[None, :], 0), 1
    )
    same = jnp.logical_and(
        row_index[:, None] // frames == row_index[None, :] // frames,
        row_clip[:, None] == row_clip[None, :],
    )
    bias = jnp.where(same, 0.0, -1e30)

    def rows_of(patch, per_clip):
        return jnp.concatenate(
            [
                patch.reshape(count, width),
                per_clip,
                jnp.zeros((spare - clips, width), patch.dtype),
            ],
            0,
        ).astype(FULL)

    flights = Flights()
    near = lax.axis_index(DP) % 2
    gathered = [None] * layers
    by_core, by_x, by_y = exchange(TENSOR, 1), exchange(TENSOR, 2), exchange(DP, 1)

    def send(name, values, way):
        flights.start(name, pass_on(values, way))

    def arrived_here(name):
        return flights.results.pop(name)

    send("x0", both_matrices(hidden_up, hidden_down, 0, near), by_x)
    send("core0", both_matrices(hidden_up, hidden_down, 0), by_core)
    patch_rows = flights.leave(rows_of(patch_tokens, class_tokens))
    pieces_out = [((piece_rows, width), HALF)] * groups
    backs_out = [((back_rows, width), HALF)] * groups
    lane_buffer = pltpu.VMEM((width // 128, rows, 128), FULL)
    row_buffer = pltpu.VMEM((rows, width), FULL)
    square = pltpu.VMEM((width, width), HALF)
    wide = pltpu.VMEM((width, 3 * width), HALF)
    shards = pltpu.VMEM((groups, width, width), HALF)
    blocks = pltpu.VMEM((groups, back_rows, width), FULL)
    frame_rows = pltpu.VMEM((frames, width), FULL)
    saved = []
    for layer in range(layers):
        if layer:
            patch_rows = flights.land([f"x{layer}", f"core{layer}"], patch_rows)
            first = arrived_here(f"x{layer}")
            send("y1", first, by_y)
            patch_rows = flights.leave(patch_rows)
        time = call(
            partial(time_forward, dims, layer),
            [
                ((rows, width), HALF),
                ((rows, 3 * width), HALF),
                ((rows, 128), FULL),
                ((rows, width), HALF),
                ((rows, width), HALF),
                ((rows, width), FULL),
            ]
            + pieces_out
            + [((spare, width), FULL)],
            [wide, square, square, lane_buffer, row_buffer, blocks, pltpu.SemaphoreType.DMA((3,))],
            [SMALL, ROWS, ROWS, ROWS, ROWS, FAR, FAR, FAR],
            14,
        )(place, patch_rows, bias, norm_gain, norm_shift, temporal_in, temporal_out, temporal_mix)
        arrived = spread(time[6:10])
        if layer == 0:
            arrived = flights.land(("x0", "core0"), arrived)
            first = arrived_here("x0")
            send("y0", first, by_y)
            send("x1", both_matrices(hidden_up, hidden_down, 1, near), by_x)
        arrived = flights.leave(arrived)
        space = call(
            partial(space_forward, dims, layer),
            [((span, width), HALF), ((span, 3 * width), HALF), ((span, 128), FULL)] + backs_out,
            [wide, pltpu.VMEM((span, width), FULL), pltpu.SemaphoreType.DMA((1,))],
            [SMALL, SMALL, ROWS] + [ROWS] * groups + [FAR],
            9,
        )(place, clip_of, time[10], *arrived, spatial_in)
        arrived = spread(space[3:])
        arrived = flights.land([f"y{layer}"], arrived)
        second = arrived_here(f"y{layer}")
        send("first", first, by_core)
        send("second", second, by_core)
        if layer + 1 < layers:
            send("core1", both_matrices(hidden_up, hidden_down, 1), by_core)
        arrived = flights.leave(arrived)
        arrived = flights.land(("first", "second"), arrived)
        gathered[layer] = (
            arrived_here(f"core{layer}"),
            first,
            second,
            arrived_here("first"),
            arrived_here("second"),
        )
        feed = call(
            partial(feed_forward, dims, layer),
            [
                ((rows, width), HALF),
                ((rows, width), FULL),
                ((rows, width), HALF),
                ((rows, hidden), HALF),
                ((rows, hidden), HALF),
                ((rows, width), FULL),
            ],
            [
                square,
                shards,
                shards,
                row_buffer,
                blocks,
                frame_rows,
                pltpu.VMEM((rows, width), HALF),
                pltpu.SemaphoreType.DMA((1,)),
                pltpu.SemaphoreType.DMA((12,)),
            ],
            [SMALL] + [ROWS] * groups + [ROWS] * 4 + [FAR] * 8,
            15,
        )(
            place, *arrived, share, time[5], norm_gain, norm_shift, spatial_out,
            hidden_up, hidden_down, *gathered[layer],
        )
        saved.append((patch_rows, time, space, feed))
        patch_rows = feed[5]
    patch_output = patch_rows[:count].reshape(frames, patches, width).astype(HALF)
    class_output = patch_rows[count : count + clips].astype(HALF)

    grad_rows = rows_of(patch_cotangent, class_cotangent)
    usual = blocks_dp == 2 * NEAR
    norms = [None] * layers

    def start(name, pairs, split, micros):
        if split and not usual:
            flights.results[name] = reduce_whole(pairs)
            return
        parts = outer_group(place, pairs, groups, split, micros)
        if split:
            flights.start(name, reduce_attention(parts, [right.shape[1] for left, right in pairs]))
        elif usual:
            flights.start(name, reduce_group(parts))
        else:
            flights.start(name, reduce_far(parts))

    for layer in reversed(range(layers)):
        start_rows, time, space, feed = saved[layer]
        last = layer == 0
        feed_back = call(
            partial(feed_backward, dims, layer),
            [
                ((rows, width), HALF),
                ((rows, hidden), HALF),
                ((rows, width), HALF),
                ((rows, width), FULL),
                ((8, width), FULL),
            ]
            + pieces_out
            + [((8, width), FULL)],
            [
                square,
                shards,
                shards,
                row_buffer,
                row_buffer,
                blocks,
                pltpu.SemaphoreType.DMA((1,)),
                pltpu.SemaphoreType.DMA((12,)),
            ],
            [SMALL, SMALL] + [ROWS] * 5 + [FAR] * 8,
            23,
        )(
            place, clip_of, grad_rows, feed[4], feed[1],
            jnp.broadcast_to(inverse_counts[:, None], (spare, 128)), norm_gain, spatial_out,
            hidden_up, hidden_down, *gathered[layer],
        )
        update, grad_hidden, branch, back, feed_norms = feed_back[:5]
        arrived = spread(feed_back[5:9])
        pairs = ((feed[2], grad_hidden), (update, feed[3]))
        if last:
            start("feed0", pairs, False, 10)
            arrived = flights.land(("feed1", "attention1"), arrived)
        else:
            start("feed1", pairs, False, 10)
            arrived = flights.leave(arrived)
        space_back = call(
            partial(space_backward, dims, layer),
            [((span, 3 * width), HALF)] + backs_out,
            [
                wide,
                pltpu.VMEM((span, width), FULL),
                pltpu.VMEM((span, width), HALF),
                pltpu.SemaphoreType.DMA((1,)),
            ],
            [ROWS] * groups + [ROWS] * 3 + [FAR],
            29,
        )(*arrived, feed_back[9], space[1], space[2], spatial_in)
        arrived = spread(space_back[1:])
        pairs = ((space[0], space_back[0]), (feed[0], branch))
        if last:
            start("space0", pairs, True, 8)
            arrived = flights.land(("feed1", "feed0", "attention1"), arrived)
        else:
            space_pairs = pairs
            arrived = flights.land(("feed1",), arrived)
        time_back = call(
            partial(time_backward, dims, layer),
            [
                ((rows, width), HALF),
                ((rows, width), HALF),
                ((rows, 3 * width), HALF),
                ((rows, width), FULL),
                ((8, width), FULL),
            ],
            [
                wide,
                square,
                square,
                lane_buffer,
                row_buffer,
                blocks,
                frame_rows,
                pltpu.VMEM((rows, width), HALF),
                pltpu.SemaphoreType.DMA((3,)),
            ],
            [SMALL] + [ROWS] * groups + [ROWS] * 8 + [FAR] * 3,
            14,
        )(
            place, *arrived, member, back, time[5], start_rows, time[1], time[2], bias,
            norm_gain, temporal_in, temporal_out, temporal_mix,
        )
        grad_rows = time_back[3]
        norms[layer] = (time_back[4], feed_norms)
        pairs = ((time[0], time_back[2]), (time[3], time_back[1]), (time[4], time_back[0]))
        if last:
            ordered = [
                entry[at : at + 1]
                for part, at in ((0, 2), (0, 0), (1, 0), (0, 3), (0, 1), (1, 1))
                for entry in [norms[index][part] for index in range(layers)]
            ]
            ordered = jnp.concatenate(ordered, 0)
            if usual:
                flights.start("norms", reduce_norms(ordered))
            else:
                total = lax.psum(ordered, TENSOR)
                flights.results["norms"] = lax.psum_scatter(
                    total, DP, scatter_dimension=1, tiled=True
                )
            start("time0", pairs, True, 9)
            token = flights.land(("feed1", "attention1"), time_back[4])
        else:
            start("attention1", space_pairs + pairs, True, 17)
            grad_rows = flights.land(("feed1",), grad_rows)
    for names in (
        ("feed0", "space0"),
        ("time0", "attention1"),
        ("feed0", "space0"),
        ("time0", "attention1", "norms"),
        ("feed0", "space0"),
        ("time0", "attention1", "norms"),
        ("feed0", "space0"),
        ("time0", "norms"),
        ("space0",),
        ("time0", "norms"),
    ):
        token = flights.land(names, token)
    while flights.running:
        token = flights.land(list(flights.running), token)
    results = flights.results
    lanes = width // blocks_dp

    norm_sums = results["norms"].reshape(2, 3, layers, lanes).transpose(0, 2, 1, 3)
    feeds = (results["feed0"], results["feed1"])
    late = results["attention1"]
    time_sums = (results["time0"], late[2:])
    space_sums = (results["space0"], late[:2])
    gradients = (
        *[jnp.stack([sums[index] for sums in time_sums]) for index in range(3)],
        *[jnp.stack([sums[index] for sums in space_sums]) for index in range(2)],
        jnp.stack([sums[:, :width] for sums in feeds]),
        jnp.stack([sums[:, width:].T for sums in feeds]),
        norm_sums[0],
        norm_sums[1],
    )
    patch_grad = grad_rows[:count].reshape(frames, patches, width)
    class_grad = grad_rows[count : count + clips]
    return (patch_output, class_output, patch_grad, class_grad, *gradients)


def solution(mesh):
    placed = (
        P(DP, TENSOR, None),
        P(DP, None),
        P(DP, None),
        P(DP, TENSOR, None),
        P(DP, None),
        P(),
        P(),
        P(),
        P(),
        P(),
        P(None, None, TENSOR),
        P(None, TENSOR, None),
        P(),
        P(),
    )
    return jax.shard_map(
        body,
        mesh=mesh,
        in_specs=placed,
        out_specs=(
            P(DP, TENSOR, None),
            P(DP, None),
            P(DP, TENSOR, None),
            P(DP, None),
            P(None, DP, None),
            P(None, DP, None),
            P(None, DP, None),
            P(None, DP, None),
            P(None, DP, None),
            P(None, DP, TENSOR),
            P(None, TENSOR, DP),
            P(None, None, DP),
            P(None, None, DP),
        ),
        check_vma=False,
    )
```

```python
from functools import partial

import jax
import jax.numpy as jnp
from jax import lax
from jax.experimental import pallas as pl
from jax.experimental.pallas import tpu as pltpu
from jax.sharding import PartitionSpec as P

HEADS = 12
EPS = 1e-06
HIGH = lax.Precision.HIGHEST
HALF = jnp.bfloat16
FULL = jnp.float32
NEAR = 4
TENSOR = "tensor"
DP = "dp"
TILE = 256
VMEM_BYTES = 58 << 20
SMEM = pl.BlockSpec(memory_space=pltpu.SMEM)
SMALL, ROWS, FAR = range(3)
HBM = pl.BlockSpec(memory_space=pltpu.HBM)
ROOT_HALF = 0.5**0.5
DENSITY = (2.0 * 3.141592653589793) ** -0.5


def up_to(value, step):
    return -(-value // step) * step


def dot(left, right):
    return jnp.dot(left, right, preferred_element_type=FULL)


def dot_back(left, right):
    return lax.dot_general(left, right, (((1,), (1,)), ((), ())), preferred_element_type=FULL)


def dot_outer(left, right):
    return lax.dot_general(left, right, (((0,), (0,)), ((), ())), preferred_element_type=FULL)


def unit_of(values):
    centred = values - jnp.mean(values, -1, keepdims=True)
    inverse = lax.rsqrt(jnp.mean(centred * centred, -1, keepdims=True) + EPS)
    return centred * inverse, inverse


def unit_back(grad, unit, inverse, gain):
    scaled = grad * gain
    inner = (
        scaled
        - jnp.mean(scaled, -1, keepdims=True)
        - unit * jnp.mean(scaled * unit, -1, keepdims=True)
    )
    return inner * inverse


def head_lanes(head_size, half):
    lane = lax.broadcasted_iota(jnp.int32, (1, 2 * head_size), 1)
    return (lane // head_size) == half


def over_rows(rows, step, run):
    for start in range(0, rows, step):
        run(start, min(step, rows - start))


def two_heads(values, head_size):
    return jnp.concatenate(
        [jnp.where(head_lanes(head_size, half), values, 0) for half in range(2)], 0
    )


def one_of_two(values, head_size):
    rows = values.shape[0] // 2
    return jnp.where(head_lanes(head_size, 0), values[:rows], values[rows:])


def interleave(order, frame, frames, values):
    for group in range(order.shape[0]):
        part = values[:, group * 128 : (group + 1) * 128]
        order[group, pl.ds(frame, values.shape[0], stride=frames), :] = part


def pick(order, frame, frames, patches):
    own = pl.ds(frame, patches, stride=frames)
    return jnp.concatenate([order[group, own, :] for group in range(order.shape[0])], 1)


def shard_copies(place_ref, refs, target, which):
    own, core, far_first, far_second, core_first, core_second = refs
    half = far_first.shape[1]
    first = pl.multiple_of(place_ref[1] * half, half)
    second = pl.multiple_of((1 - place_ref[1]) * half, half)
    return [
        [(own, target.at[0])],
        [(core.at[which], target.at[1])],
        [
            (far_first.at[which], target.at[2, pl.ds(first, half)]),
            (far_second.at[which], target.at[2, pl.ds(second, half)]),
        ],
        [
            (core_first.at[which], target.at[3, pl.ds(first, half)]),
            (core_second.at[which], target.at[3, pl.ds(second, half)]),
        ],
    ]


def start_shards(place_ref, own, peers, up_ref, down_ref, sems):
    waits = []
    index = 0
    for pairs in zip(
        shard_copies(place_ref, (own[0],) + peers, up_ref, 0),
        shard_copies(place_ref, (own[1],) + peers, down_ref, 1),
    ):
        group = []
        for source, target in pairs[0] + pairs[1]:
            copy = pltpu.make_async_copy(source, target, sems.at[index])
            copy.start()
            group.append(copy)
            index += 1
        waits.append(group)
    return waits


def fetch(sources, targets, sems):
    copies = [
        pltpu.make_async_copy(source, target, sems.at[index])
        for index, (source, target) in enumerate(zip(sources, targets))
    ]
    for copy in copies:
        copy.start()
    return copies


def attend_forward(load, store, store_total, heads, head_size, bias):
    scale = head_size**-0.5
    totals = None
    if bias.shape[0] > 1:
        bias = jnp.concatenate([bias, bias], 0)
    for pair in range(heads // 2):
        query, key, value = (load(part, pair) for part in range(3))
        rows = query.shape[0]
        scores = dot_back(two_heads(query, head_size), key) * scale + bias
        top = jnp.max(scores, -1, keepdims=True)
        raised = jnp.exp(scores - top)
        total = jnp.sum(raised, -1, keepdims=True)
        mixed = dot(raised.astype(HALF), value) * (1.0 / total)
        log_total = top + jnp.log(total)
        if totals is None:
            lanes = lax.broadcasted_iota(jnp.int32, (rows, 128), 1)
            totals = jnp.zeros(lanes.shape, FULL)
        totals = jnp.where(lanes == pair * 2, log_total[:rows], totals)
        totals = jnp.where(lanes == pair * 2 + 1, log_total[rows:], totals)
        store(pair, one_of_two(mixed, head_size))
    store_total(totals)


def attend_backward(load, load_grad, totals, store, heads, head_size, bias):
    scale = head_size**-0.5
    totals = totals.T
    if bias.shape[1] > 1:
        bias = jnp.concatenate([bias, bias], 1)
    for pair in range(heads // 2):
        query, key, value = (load(part, pair) for part in range(3))
        query = two_heads(query, head_size)
        grad = two_heads(load_grad(pair), head_size)
        total = jnp.concatenate([totals[2 * pair + half : 2 * pair + half + 1] for half in range(2)], 1)
        prob = jnp.exp(dot_back(key, query) * scale + (bias - total))
        grad_prob = dot_back(value, grad)
        delta = jnp.sum(prob * grad_prob, 0, keepdims=True)
        grad_score = (prob * (grad_prob - delta)).astype(HALF)
        store(0, pair, one_of_two(dot_outer(grad_score, key), head_size) * scale)
        store(1, pair, dot(grad_score, query) * scale)
        store(2, pair, dot(prob.astype(HALF), grad))


def row_blocks(rows, step):
    return [(start, min(step, rows - start)) for start in range(0, rows, step)]


def time_forward(dims, layer, place_ref, x_ref, bias_ref, gain_ref, shift_ref, in_hbm, out_hbm, mix_hbm,
                 normed_ref, triple_ref, total_ref, mixed_ref, projected_ref, after_ref,
                 send0, send1, send2, send3, class_ref,
                 in_ref, out_ref, mix_ref, order, plain, blocks, sems):
    frames, patches, width, heads, groups = dims
    count = frames * patches
    rows = x_ref.shape[0]
    step = bias_ref.shape[0]
    copies = fetch(
        (in_hbm.at[layer], out_hbm.at[layer], mix_hbm.at[layer]), (in_ref, out_ref, mix_ref), sems
    )
    gain = gain_ref[layer, 0:1, :]
    shift = shift_ref[layer, 0:1, :]
    for frame in range(frames):
        unit, unused = unit_of(x_ref[frame * patches : (frame + 1) * patches, :])
        interleave(order, frame, frames, unit * gain + shift)
    for group in range(width // 128):
        order[group, count:, :] = jnp.zeros((rows - count, 128), FULL)
        normed_ref[:, group * 128 : (group + 1) * 128] = order[group].astype(HALF)
    normed_ref.flush()
    copies[0].wait()
    for column in range(0, 3 * width, TILE):
        part = slice(column, column + TILE)
        triple_ref[:, part] = dot(normed_ref[...], in_ref[:, part]).astype(HALF)
    triple_ref.flush()
    for begin, size in row_blocks(rows, step):
        own = slice(begin, begin + size)

        def load(part, pair):
            start = part * width + pair * 128
            return triple_ref[own, start : start + 128]

        def store(pair, mixed):
            order[pair, own, :] = mixed

        def store_total(totals):
            total_ref[own, :] = totals

        attend_forward(
            load, store, store_total, heads, width // heads, bias_ref[0:size, 0:size]
        )
    for frame in range(frames):
        plain[frame * patches : (frame + 1) * patches, :] = pick(order, frame, frames, patches)
    plain[count:, :] = jnp.zeros((rows - count, width), FULL)
    mixed_ref[...] = plain[...].astype(HALF)
    mixed_ref.flush()
    copies[1].wait()
    for column in range(0, width, TILE):
        part = slice(column, column + TILE)
        projected_ref[:, part] = dot(mixed_ref[...], out_ref[:, part]).astype(HALF)
    projected_ref.flush()
    copies[2].wait()
    for column in range(0, width, TILE):
        part = slice(column, column + TILE)
        after_ref[:, part] = x_ref[:, part] + dot(projected_ref[...], mix_ref[:, part])
    after_ref.flush()
    gain = gain_ref[layer, 1:2, :]
    shift = shift_ref[layer, 1:2, :]

    def norm(start, size):
        own = slice(start, start + size)
        unit, unused = unit_of(after_ref[own, :])
        plain[own, :] = unit * gain + shift

    over_rows(rows, 80, norm)
    send_blocks(plain, blocks, (send0, send1, send2, send3), place_ref[0], count // groups)
    class_ref[...] = plain[count:, :]


def send_blocks(plain, blocks, sends, place, size):
    groups = len(sends)
    for group in range(groups):
        blocks[group, 0:size, :] = plain[group * size : (group + 1) * size, :]
    for away in range(groups):
        sends[away][...] = blocks[place ^ away][0:size].astype(HALF)


def space_forward(dims, layer, place_ref, clip_ref, class_ref, piece0, piece1, piece2, piece3, in_hbm,
                  normed_ref, triple_ref, total_ref, send0, send1, send2, send3,
                  in_ref, plain, sems):
    frames, patches, width, heads, groups = dims
    own_frames = frames // groups
    seq = groups * patches
    rows = normed_ref.shape[0] // own_frames
    copies = fetch((in_hbm.at[layer],), (in_ref,), sems)
    pieces = [piece0, piece1, piece2, piece3]
    for away, piece in enumerate(pieces):
        values = piece[...].astype(FULL)
        for frame in range(own_frames):
            start = frame * rows + away * patches
            plain[start : start + patches, :] = values[frame * patches : (frame + 1) * patches]
    for frame in range(own_frames):
        start = frame * rows + seq
        plain[start : start + rows - seq, :] = jnp.zeros((rows - seq, width), FULL)
        clip = clip_ref[place_ref[0] * own_frames + frame]
        plain[start : start + 1, :] = class_ref[pl.ds(clip, 1), :]
    normed_ref[...] = plain[...].astype(HALF)
    normed_ref.flush()
    copies[0].wait()
    for column in range(0, 3 * width, TILE):
        part = slice(column, column + TILE)
        triple_ref[:, part] = dot(normed_ref[...], in_ref[:, part]).astype(HALF)
    triple_ref.flush()
    keys = lax.broadcasted_iota(jnp.int32, (1, rows), 1)
    bias = jnp.where(keys <= seq, 0.0, -1e30)

    for frame in range(own_frames):
        own = slice(frame * rows, (frame + 1) * rows)

        def load(part, pair):
            start = part * width + pair * 128
            return triple_ref[own, start : start + 128]

        def store(pair, mixed):
            plain[own, pair * 128 : (pair + 1) * 128] = mixed

        def store_total(totals):
            total_ref[own, :] = totals

        attend_forward(load, store, store_total, heads, width // heads, bias)
    return_pieces(plain, (send0, send1, send2, send3), own_frames, patches, rows)


def return_pieces(plain, sends, own_frames, patches, rows):
    seq = len(sends) * patches
    tail = []
    for frame in range(own_frames):
        row = plain[frame * rows + seq : frame * rows + seq + 1, :]
        high = row.astype(HALF).astype(FULL)
        tail += [high, row - high]
    size = own_frames * patches
    spare = sends[0].shape[0] - size - len(tail)
    tail.append(jnp.zeros((spare, plain.shape[1]), FULL))
    for away, send in enumerate(sends):
        kept = [
            plain[frame * rows + away * patches : frame * rows + (away + 1) * patches, :]
            for frame in range(own_frames)
        ]
        send[...] = jnp.concatenate(kept + tail, 0).astype(HALF)


def take_pieces(pieces, blocks, plain, frame_rows, place, size, own_frames):
    for away, piece in enumerate(pieces):
        blocks[place ^ away] = piece[...].astype(FULL)
    for group in range(len(pieces)):
        plain[group * size : (group + 1) * size, :] = blocks[group, 0:size, :]
        for frame in range(own_frames):
            start = size + 2 * frame
            frame_rows[group * own_frames + frame : group * own_frames + frame + 1, :] = (
                blocks[group, start : start + 1, :] + blocks[group, start + 1 : start + 2, :]
            )


def feed_forward(dims, layer, place_ref, piece0, piece1, piece2, piece3, share_ref, after_ref,
                 gain_ref, shift_ref, out_hbm,
                 up_hbm, down_hbm, peer1, peer2, peer3, peer4, peer5,
                 mixed_ref, rows_ref, normed_ref, active_ref, slope_ref, next_ref,
                 out_ref, up_ref, down_ref, plain, blocks, frame_rows, whole, out_sem, sems):
    frames, patches, width, heads, groups = dims
    count = frames * patches
    rows = after_ref.shape[0]
    size = count // groups
    place = place_ref[0]
    copies = fetch((out_hbm.at[layer],), (out_ref,), out_sem)
    own = (up_hbm.at[layer], down_hbm.at[layer])
    peers = (peer1, peer2, peer3, peer4, peer5)
    shards = start_shards(place_ref, own, peers, up_ref, down_ref, sems)
    take_pieces(
        (piece0, piece1, piece2, piece3), blocks, plain, frame_rows, place, size, frames // groups
    )
    plain[count:, :] = jnp.dot(
        share_ref[...], frame_rows[...], precision=HIGH, preferred_element_type=FULL
    )
    whole[...] = plain[...].astype(HALF)
    leader = jnp.where(place == 0, 1.0, 0.0).astype(FULL)
    kept = lax.broadcasted_iota(jnp.int32, (rows, 1), 0) < count
    kept = jnp.where(kept, 1.0, leader)
    mixed_ref[...] = (plain[...] * kept).astype(HALF)
    mixed_ref.flush()
    copies[0].wait()
    for column in range(0, width, TILE):
        part = slice(column, column + TILE)
        rows_ref[:, part] = after_ref[:, part] + dot(whole[...], out_ref[:, part])
    rows_ref.flush()
    gain = gain_ref[layer, 2:3, :]
    shift = shift_ref[layer, 2:3, :]

    def norm(start, size):
        own = slice(start, start + size)
        unit, unused = unit_of(rows_ref[own, :])
        plain[own, :] = unit * gain + shift

    over_rows(rows, 80, norm)
    whole[...] = plain[...].astype(HALF)
    normed_ref[...] = (plain[...] * kept).astype(HALF)
    normed_ref.flush()
    next_ref[...] = rows_ref[...]
    for away in range(groups):
        for copy in shards[away]:
            copy.wait()
        for column in range(0, width, TILE):
            part = slice(column, column + TILE)
            hidden = dot(whole[...], up_ref[away, :, part])
            below = 0.5 + 0.5 * lax.erf(hidden * ROOT_HALF)
            active = (hidden * below).astype(HALF)
            slope = below + hidden * (jnp.exp(hidden * hidden * -0.5) * DENSITY)
            start = away * width + column
            active_ref[:, start : start + TILE] = active
            slope_ref[:, start : start + TILE] = slope.astype(HALF)
        own = slice(away * width, (away + 1) * width)
        for column in range(0, width, TILE):
            part = slice(column, column + TILE)
            next_ref[:, part] += dot(active_ref[:, own], down_ref[away, :, part])
        end = count // 16 * 16
        active_ref[end:, own] = (active_ref[end:, own].astype(FULL) * kept[end:]).astype(HALF)
        active_ref.flush(own)
        slope_ref.flush(own)


def feed_backward(dims, layer, place_ref, clip_ref, grad_ref, slope_ref, rows_ref, share_ref, gain_ref,
                  out_hbm, up_hbm, down_hbm, peer1, peer2, peer3, peer4, peer5,
                  update_ref, hidden_ref, branch_ref, back_ref, norms_ref,
                  send0, send1, send2, send3, class_ref,
                  out_ref, up_ref, down_ref, total, plain, blocks, out_sem, sems):
    frames, patches, width, heads, groups = dims
    count = frames * patches
    rows = grad_ref.shape[0]
    place = place_ref[0]
    own_frames = frames // groups
    own = (up_hbm.at[layer], down_hbm.at[layer])
    peers = (peer1, peer2, peer3, peer4, peer5)
    shards = start_shards(place_ref, own, peers, up_ref, down_ref, sems)
    copies = fetch((out_hbm.at[layer],), (out_ref,), out_sem)
    update_ref[...] = grad_ref[...].astype(HALF)
    update_ref.flush()
    for away in range(groups):
        for copy in shards[away]:
            copy.wait()
        for column in range(0, width, TILE):
            part = slice(column, column + TILE)
            start = away * width + column
            grad_active = dot_back(update_ref[...], down_ref[away, part, :])
            slope = slope_ref[:, start : start + TILE].astype(FULL)
            grad_hidden = (grad_active * slope).astype(HALF)
            hidden_ref[:, start : start + TILE] = grad_hidden
        own = slice(away * width, (away + 1) * width)
        for column in range(0, width, TILE):
            part = slice(column, column + TILE)
            term = dot_back(hidden_ref[:, own], up_ref[away, part, :])
            if away == 0:
                total[:, part] = term
            else:
                total[:, part] += term
        hidden_ref.flush(own)
    gain = gain_ref[layer, 2:3, :]
    leader = jnp.where(place == 0, 1.0, 0.0).astype(FULL)
    norms_ref[...] = jnp.zeros(norms_ref.shape, FULL)
    def norm(start, size):
        own = slice(start, start + size)
        unit, inverse = unit_of(rows_ref[own, :])
        grad = total[own, :]
        back = grad_ref[own, :] + unit_back(grad, unit, inverse, gain)
        back_ref[own, :] = back
        branch_ref[own, :] = back.astype(HALF)
        kept = lax.broadcasted_iota(jnp.int32, (size, 1), 0) + start < count
        grad = jnp.where(kept, grad, grad * leader)
        norms_ref[0:1, :] += jnp.sum(grad * unit, 0, keepdims=True)
        norms_ref[1:2, :] += jnp.sum(grad, 0, keepdims=True)

    over_rows(rows, 80, norm)
    back_ref.flush()
    branch_ref.flush()
    copies[-1].wait()
    for column in range(0, width, TILE):
        part = slice(column, column + TILE)
        plain[:, part] = dot_back(branch_ref[...], out_ref[part, :])
    send_blocks(plain, blocks, (send0, send1, send2, send3), place, count // groups)
    for frame in range(own_frames):
        clip = clip_ref[place * own_frames + frame]
        class_ref[frame : frame + 1, :] = (
            plain[pl.ds(count + clip, 1), :] * share_ref[pl.ds(clip, 1), 0:1]
        )


def space_backward(dims, layer, piece0, piece1, piece2, piece3, class_ref, triple_ref, total_ref, in_hbm,
                   grad_ref, send0, send1, send2, send3,
                   in_ref, plain, mixed, sems):
    frames, patches, width, heads, groups = dims
    own_frames = frames // groups
    seq = groups * patches
    rows = triple_ref.shape[0] // own_frames
    copies = fetch((in_hbm.at[layer],), (in_ref,), sems)
    for away, piece in enumerate((piece0, piece1, piece2, piece3)):
        values = piece[...].astype(FULL)
        for frame in range(own_frames):
            start = frame * rows + away * patches
            plain[start : start + patches, :] = values[frame * patches : (frame + 1) * patches]
    for frame in range(own_frames):
        start = frame * rows + seq
        plain[start : start + rows - seq, :] = jnp.zeros((rows - seq, width), FULL)
        plain[start : start + 1, :] = class_ref[frame : frame + 1, :]
    mixed[...] = plain[...].astype(HALF)
    keys = lax.broadcasted_iota(jnp.int32, (rows, 1), 0)
    bias = jnp.where(keys <= seq, 0.0, -1e30)
    for frame in range(own_frames):
        own = slice(frame * rows, (frame + 1) * rows)

        def load(part, pair):
            start = part * width + pair * 128
            return triple_ref[own, start : start + 128]

        def load_grad(pair):
            return mixed[own, pair * 128 : (pair + 1) * 128]

        def store(part, pair, grad):
            start = part * width + pair * 128
            grad_ref[own, start : start + 128] = grad.astype(HALF)

        attend_backward(load, load_grad, total_ref[own, :], store, heads, width // heads, bias)
    grad_ref.flush()
    copies[0].wait()
    for column in range(0, width, TILE):
        part = slice(column, column + TILE)
        plain[:, part] = dot_back(grad_ref[...], in_ref[part, :])
    return_pieces(plain, (send0, send1, send2, send3), own_frames, patches, rows)


def time_backward(dims, layer, place_ref, piece0, piece1, piece2, piece3, member_ref, back_ref, after_ref, x_ref,
                  triple_ref, total_ref, bias_ref, gain_ref, in_hbm, out_hbm, mix_hbm,
                  branch_ref, projected_ref, grad_ref, next_ref, norms_ref,
                  in_ref, out_ref, mix_ref, order, plain, blocks, frame_rows, mixed, sems):
    frames, patches, width, heads, groups = dims
    count = frames * patches
    rows = x_ref.shape[0]
    step = bias_ref.shape[0]
    place = place_ref[0]
    copies = fetch(
        (mix_hbm.at[layer], out_hbm.at[layer], in_hbm.at[layer]), (mix_ref, out_ref, in_ref), sems
    )
    take_pieces(
        (piece0, piece1, piece2, piece3),
        blocks,
        plain,
        frame_rows,
        place,
        count // groups,
        frames // groups,
    )
    plain[count:, :] = jnp.dot(
        member_ref[...], frame_rows[...], precision=HIGH, preferred_element_type=FULL
    )
    leader = jnp.where(place == 0, 1.0, 0.0).astype(FULL)
    norms_ref[...] = jnp.zeros(norms_ref.shape, FULL)
    gain = gain_ref[layer, 1:2, :]

    def space_norm(start, size):
        own = slice(start, start + size)
        unit, inverse = unit_of(after_ref[own, :])
        grad = plain[own, :]
        back = back_ref[own, :] + unit_back(grad, unit, inverse, gain)
        next_ref[own, :] = back
        kept = lax.broadcasted_iota(jnp.int32, (size, 1), 0) + start < count
        branch_ref[own, :] = jnp.where(kept, back, 0.0).astype(HALF)
        grad = jnp.where(kept, grad, grad * leader)
        norms_ref[0:1, :] += jnp.sum(grad * unit, 0, keepdims=True)
        norms_ref[1:2, :] += jnp.sum(grad, 0, keepdims=True)

    over_rows(rows, 80, space_norm)
    branch_ref.flush()
    copies[0].wait()
    for column in range(0, width, TILE):
        part = slice(column, column + TILE)
        projected_ref[:, part] = dot_back(branch_ref[...], mix_ref[part, :]).astype(HALF)
    projected_ref.flush()
    copies[1].wait()
    for column in range(0, width, TILE):
        part = slice(column, column + TILE)
        plain[:, part] = dot_back(projected_ref[...], out_ref[part, :])
    for frame in range(frames):
        interleave(order, frame, frames, plain[frame * patches : (frame + 1) * patches, :])
    for group in range(width // 128):
        order[group, count:, :] = jnp.zeros((rows - count, 128), FULL)
        mixed[:, group * 128 : (group + 1) * 128] = order[group].astype(HALF)

    for begin, size in row_blocks(rows, step):
        own = slice(begin, begin + size)

        def load(part, pair):
            start = part * width + pair * 128
            return triple_ref[own, start : start + 128]

        def load_grad(pair):
            return mixed[own, pair * 128 : (pair + 1) * 128]

        def store(part, pair, grad):
            start = part * width + pair * 128
            grad_ref[own, start : start + 128] = grad.astype(HALF)

        attend_backward(
            load,
            load_grad,
            total_ref[own, :],
            store,
            heads,
            width // heads,
            bias_ref[0:size, 0:size],
        )
    grad_ref.flush()
    copies[2].wait()
    for column in range(0, width, TILE):
        part = slice(column, column + TILE)
        grad = dot_back(grad_ref[...], in_ref[part, :])
        for group in range(TILE // 128):
            order[column // 128 + group] = grad[:, group * 128 : (group + 1) * 128]
    gain = gain_ref[layer, 0:1, :]
    for frame in range(frames):
        own = slice(frame * patches, (frame + 1) * patches)
        grad = pick(order, frame, frames, patches)
        unit, inverse = unit_of(x_ref[own, :])
        next_ref[own, :] += unit_back(grad, unit, inverse, gain)
        norms_ref[2:3, :] += jnp.sum(grad * unit, 0, keepdims=True)
        norms_ref[3:4, :] += jnp.sum(grad, 0, keepdims=True)


def cost(micros):
    return pl.CostEstimate(flops=micros, bytes_accessed=micros, transcendentals=0)


class Fetched:
    def __init__(self, source, target, sem):
        self.target, self.shape = target, target.shape
        self.copy = pltpu.make_async_copy(source, target, sem)
        self.copy.start()

    def wait(self):
        if self.copy is not None:
            self.copy.wait()
            self.copy = None

    def __getitem__(self, index):
        self.wait()
        return self.target[index]


class Written:
    def __init__(self, source, target, sems):
        self.source, self.target, self.sems = source, target, sems
        self.shape = source.shape
        self.copies = []

    def __getitem__(self, index):
        return self.source[index]

    def __setitem__(self, index, values):
        self.source[index] = values

    def flush(self, columns=None):
        parts = (self.source, self.target)
        if columns is not None:
            parts = tuple(ref.at[:, columns] for ref in parts)
        copy = pltpu.make_async_copy(*parts, self.sems.at[len(self.copies)])
        copy.start()
        self.copies.append(copy)

    def wait(self):
        if not self.copies:
            self.flush()
        for copy in self.copies:
            copy.wait()


def call(kernel, outs, scratch, specs, micros):
    def run(*arrays):
        fetched = [index for index, kind in enumerate(specs) if kind == ROWS]
        count, results = len(specs), len(outs)

        def whole(*refs):
            ins, out_refs = list(refs[:count]), refs[count : count + results]
            rest = refs[count + results :]
            in_refs, rest = rest[: len(fetched)], rest[len(fetched) :]
            kept, rest = rest[:results], rest[results:]
            in_sems, out_sems = rest[0], rest[1]
            for place, index in enumerate(fetched):
                ins[index] = Fetched(ins[index], in_refs[place], in_sems.at[place])
            written = [
                Written(source, target, out_sems.at[index])
                for index, (source, target) in enumerate(zip(kept, out_refs))
            ]
            kernel(*ins, *written, *rest[2:])
            for index in fetched:
                ins[index].wait()
            for result in written:
                result.wait()

        return pl.pallas_call(
            whole,
            out_shape=[jax.ShapeDtypeStruct(shape, kind) for shape, kind in outs],
            in_specs=[SMEM if kind == SMALL else HBM for kind in specs],
            out_specs=[HBM] * results,
            scratch_shapes=[pltpu.VMEM(arrays[index].shape, arrays[index].dtype) for index in fetched]
            + [pltpu.VMEM(shape, kind) for shape, kind in outs]
            + [pltpu.SemaphoreType.DMA((len(fetched),)), pltpu.SemaphoreType.DMA((results, 4))]
            + scratch,
            compiler_params=pltpu.CompilerParams(vmem_limit_bytes=VMEM_BYTES),
            cost_estimate=cost(micros),
        )(*arrays)

    return run


def outer_group(place, pairs, groups, split, micros, whole=False):
    rows = pairs[0][0].shape[1]
    parts = 2 if split else groups
    inner = parts // 2
    sizes = [right.shape[1] // parts for left, right in pairs]
    total = sum(sizes)
    tiles = []
    for side in range(2):
        for index, size in enumerate(sizes):
            for shard in range(inner):
                for start in range(0, size, 768):
                    tiles.append((side, index, shard, start, min(768, size - start)))
    count = len(pairs)
    results = 1 if whole else 2

    def kernel(place_ref, *refs):
        lefts, rights = refs[:count], refs[count : 2 * count]
        outs = refs[2 * count : 2 * count + results]
        left_refs = refs[2 * count + results : 3 * count + results]
        right_refs, stage, left_sems, right_sems, out_sems = refs[3 * count + results :]
        arrivals = []
        lefts_here = []
        for number, (side, index, shard, start, size) in enumerate(tiles):
            if index == len(lefts_here):
                copy = pltpu.make_async_copy(lefts[index], left_refs[index], left_sems.at[index])
                copy.start()
                lefts_here.append(copy)
            if split:
                part = jnp.where(place_ref[0] % 2 == 0, 1 - side, side)
                begin = pl.multiple_of(part * sizes[index] + start, 128)
            else:
                begin = (2 * shard + 1 - side) * sizes[index] + start
            copy = pltpu.make_async_copy(
                rights[index].at[:, pl.ds(begin, size)],
                right_refs.at[number, pl.ds(0, rights[index].shape[0]), pl.ds(0, size)],
                right_sems.at[number],
            )
            copy.start()
            arrivals.append(copy)
        leaving = []
        waited = [False] * count
        for number, (side, index, shard, start, size) in enumerate(tiles):
            if not waited[index]:
                lefts_here[index].wait()
                waited[index] = True
            arrivals[number].wait()
            depth = lefts[index].shape[0]
            terms = dot_outer(left_refs[index][...], right_refs[number, 0:depth, 0:size])
            stage[number, :, 0:size] = terms.astype(HALF)
            column = sum(sizes[:index]) + start
            if whole:
                target = outs[0].at[(2 * shard + 1 - side) ^ place_ref[0]]
            else:
                target = outs[side] if split else outs[side].at[shard]
            copy = pltpu.make_async_copy(
                stage.at[number, :, pl.ds(0, size)],
                target.at[:, pl.ds(column, size)],
                out_sems.at[number],
            )
            copy.start()
            leaving.append(copy)
        for copy in leaving:
            copy.wait()

    shape = (rows, total) if split else (groups if whole else inner, rows, total)
    lefts, rights = zip(*pairs)
    width = max(tile[4] for tile in tiles)
    return pl.pallas_call(
        kernel,
        out_shape=[jax.ShapeDtypeStruct(shape, HALF)] * results,
        in_specs=[SMEM] + [HBM] * (2 * count),
        out_specs=[HBM] * results,
        scratch_shapes=[pltpu.VMEM(left.shape, HALF) for left in lefts]
        + [
            pltpu.VMEM((len(tiles), max(left.shape[0] for left in lefts), width), HALF),
            pltpu.VMEM((len(tiles), rows, width), HALF),
            pltpu.SemaphoreType.DMA((count,)),
            pltpu.SemaphoreType.DMA((len(tiles),)),
            pltpu.SemaphoreType.DMA((len(tiles),)),
        ],
        compiler_params=pltpu.CompilerParams(vmem_limit_bytes=VMEM_BYTES),
        cost_estimate=cost(micros),
    )(place, *lefts, *rights)


def exchange(axis, bit):
    return (axis, [(index, index ^ bit) for index in range(lax.axis_size(axis))])


def swap(values, axis, bit):
    return lax.ppermute(values, *exchange(axis, bit))


def reduce_group(groups, path):
    others = yield [(send, exchange(TENSOR, 1)) for send, keep in groups]
    sums = [keep + other for (send, keep), other in zip(groups, others)]
    values = sums[0] if len(sums) == 1 else jnp.concatenate(sums, -1)
    columns = values.shape[-1]
    blocks = lax.axis_size(DP)
    far = blocks // 2
    place = lax.axis_index(DP)
    bits = {"x": lax.axis_index(TENSOR) // 2, "y": place % 2, "u": place // 2 % 2, "w": place // 4}
    ways = {
        "x": exchange(TENSOR, 2),
        "y": exchange(DP, 1),
        "u": exchange(DP, 2),
        "w": exchange(DP, 4),
    }
    if values.ndim == 3:
        values = values.reshape(2, 2, 2, 2, -1, columns)
        dims = "xwuy"
        bits["x"] = 0
    else:
        values = values.reshape(2, 2, 2, 2, -1, columns)
        dims = "wuyx"

    def side(array, left, axis, mine):
        bit = bits[axis] if mine else 1 - bits[axis]
        return lax.dynamic_index_in_dim(array, bit, left.index(axis), False)

    if path == "both":
        middle = columns // 2 // 128 * 128
        tracks = [[values[..., :middle], "xy"], [values[..., middle:], "yx"]]
        left = [dims, dims]
        for step in range(2):
            others = yield [
                (side(array, rest, way[step], False), ways[way[step]])
                for (array, way), rest in zip(tracks, left)
            ]
            tracks = [
                [side(array, rest, way[step], True) + other, way]
                for (array, way), rest, other in zip(tracks, left, others)
            ]
            left = [rest.replace(way[step], "") for (array, way), rest in zip(tracks, left)]
        values = jnp.concatenate([array for array, way in tracks], -1)
        dims = left[0]
        path = "uw"
    for axis in path:
        other = yield [(side(values, dims, axis, False), ways[axis])]
        values = side(values, dims, axis, True) + other[0]
        dims = dims.replace(axis, "")
    return values


def reduce_norms(values):
    count = lax.axis_size(DP)
    for axis, bit in ((TENSOR, 1), (TENSOR, 2), (DP, 1), (DP, 2), (DP, 4)):
        other = yield [(values, exchange(axis, bit))]
        values = values + other[0]
    lanes = values.shape[1] // count
    return lax.dynamic_slice_in_dim(values, lax.axis_index(DP) * lanes, lanes, 1)


def reduce_attention(groups, path, sizes):
    values = yield from reduce_group(groups, path)
    other = yield [(values, exchange(TENSOR, 2))]
    values = in_order(values, other[0], 2, 0)
    other = yield [(values, exchange(TENSOR, 1))]
    matrices = []
    begin = 0
    for size in sizes:
        end = begin + size // 2
        matrices.append(in_order(values[:, begin:end], other[0][:, begin:end], 1, 1).astype(FULL))
        begin = end
    return matrices


def in_order(values, other, bit, dim):
    first = lax.axis_index(TENSOR) // bit % 2 == 0
    return jnp.where(
        first,
        jnp.concatenate([values, other], dim),
        jnp.concatenate([other, values], dim),
    )


def reduce_far(parts):
    send, keep = parts
    other = yield [(send, exchange(TENSOR, 1))]
    values = keep + other[0]
    other = yield [(values[1], exchange(TENSOR, 2))]
    values = values[0] + other[0]
    values = values.reshape(-1, values.shape[-1])
    return lax.psum_scatter(values, DP, scatter_dimension=0, tiled=True).astype(FULL)


def reduce_whole(pairs):
    totals = []
    for left, right in pairs:
        total = lax.psum(dot_outer(left, right).astype(HALF), TENSOR)
        total = lax.psum_scatter(total, DP, scatter_dimension=0, tiled=True)
        totals.append(total.astype(FULL))
    return totals


class Flights:
    def __init__(self):
        self.running = {}
        self.results = {}
        self.asked = {}

    def start(self, name, steps):
        self.asked[name] = (steps, next(steps))

    def leave(self, values, names=None):
        asked = {name: self.asked.pop(name) for name in list(names or self.asked) if name in self.asked}
        sends = [[send for send, way in entry[1]] for entry in asked.values()]
        values, sends = lax.optimization_barrier((values, sends))
        for (name, (steps, entry)), ready in zip(asked.items(), sends):
            self.running[name] = (
                steps,
                [lax.ppermute(send, *way) for send, (unused, way) in zip(ready, entry)],
            )
        return values

    def land(self, names, values):
        names = [name for name in names if name in self.running]
        held = [self.running[name][1] for name in names]
        values, held = lax.optimization_barrier((values, held))
        for name, arrived in zip(names, held):
            steps = self.running.pop(name)[0]
            try:
                self.asked[name] = (steps, steps.send(arrived))
            except StopIteration as stop:
                self.results[name] = stop.value
        return values

    def turn(self, names, values):
        return self.leave(self.land(names, values), names)


def spread(pieces):
    return [pieces[0]] + [swap(piece, TENSOR, away) for away, piece in enumerate(pieces) if away]


def pass_on(values, way):
    arrived = yield [(values, way)]
    return arrived[0]


def both_matrices(hidden_up, hidden_down, layer, near=None):
    matrices = [hidden_up[layer], hidden_down[layer]]
    if near is not None:
        half = matrices[0].shape[0] // 2
        matrices = [lax.dynamic_slice_in_dim(rows, near * half, half, 0) for rows in matrices]
    return jnp.stack(matrices)


def body(
    patch_tokens,
    class_tokens,
    frame_counts,
    patch_cotangent,
    class_cotangent,
    temporal_in,
    temporal_out,
    temporal_mix,
    spatial_in,
    spatial_out,
    hidden_up,
    hidden_down,
    norm_gain,
    norm_shift,
):
    frames, patches, width = patch_tokens.shape
    clips = class_tokens.shape[0]
    layers = temporal_in.shape[0]
    groups = lax.axis_size(TENSOR)
    place = jnp.stack([lax.axis_index(TENSOR), lax.axis_index(DP) % 2]).astype(jnp.int32)
    blocks_dp = lax.axis_size(DP)
    dims = (frames, patches, width, HEADS, groups)
    count = frames * patches
    rows = up_to(count + up_to(clips, 8), 80)
    spare = rows - count
    own_frames = frames // groups
    seq = groups * patches
    frame_span = up_to(seq + 1, 16)
    span = own_frames * frame_span
    hidden = groups * hidden_up.shape[2]
    piece_rows = own_frames * patches
    back_rows = up_to(piece_rows + 2 * own_frames, 8)

    ends = jnp.cumsum(frame_counts[0])
    frame_index = jnp.arange(frames, dtype=jnp.int32)
    clip_of = jnp.sum((frame_index[:, None] >= ends[None, :]).astype(jnp.int32), 1)
    clip_index = jnp.arange(spare, dtype=jnp.int32)
    member = (clip_index[:, None] == clip_of[None, :]).astype(FULL)
    counts = jnp.concatenate([frame_counts[0].astype(FULL), jnp.ones((spare - clips,), FULL)])
    share = member / counts[:, None]
    inverse_counts = 1.0 / counts
    row_index = jnp.arange(128, dtype=jnp.int32)
    row_clip = jnp.sum(
        jnp.where(row_index[:, None] % frames == frame_index[None, :], clip_of[None, :], 0), 1
    )
    same = jnp.logical_and(
        row_index[:, None] // frames == row_index[None, :] // frames,
        row_clip[:, None] == row_clip[None, :],
    )
    bias = jnp.where(same, 0.0, -1e30)

    def rows_of(patch, per_clip):
        return jnp.concatenate(
            [
                patch.reshape(count, width),
                per_clip,
                jnp.zeros((spare - clips, width), patch.dtype),
            ],
            0,
        ).astype(FULL)

    flights = Flights()
    near = lax.axis_index(DP) % 2
    gathered = [None] * layers
    by_core, by_x, by_y = exchange(TENSOR, 1), exchange(TENSOR, 2), exchange(DP, 1)

    def send(name, values, way):
        flights.start(name, pass_on(values, way))

    def arrived_here(name):
        return flights.results.pop(name)

    send("x0", both_matrices(hidden_up, hidden_down, 0, near), by_x)
    send("core0", both_matrices(hidden_up, hidden_down, 0), by_core)
    patch_rows = flights.leave(rows_of(patch_tokens, class_tokens))
    pieces_out = [((piece_rows, width), HALF)] * groups
    backs_out = [((back_rows, width), HALF)] * groups
    lane_buffer = pltpu.VMEM((width // 128, rows, 128), FULL)
    row_buffer = pltpu.VMEM((rows, width), FULL)
    square = pltpu.VMEM((width, width), HALF)
    wide = pltpu.VMEM((width, 3 * width), HALF)
    shards = pltpu.VMEM((groups, width, width), HALF)
    blocks = pltpu.VMEM((groups, back_rows, width), FULL)
    frame_rows = pltpu.VMEM((frames, width), FULL)
    saved = []
    for layer in range(layers):
        if layer:
            patch_rows = flights.land([f"x{layer}", f"core{layer}"], patch_rows)
            first = arrived_here(f"x{layer}")
            send("y1", first, by_y)
            patch_rows = flights.leave(patch_rows)
        time = call(
            partial(time_forward, dims, layer),
            [
                ((rows, width), HALF),
                ((rows, 3 * width), HALF),
                ((rows, 128), FULL),
                ((rows, width), HALF),
                ((rows, width), HALF),
                ((rows, width), FULL),
            ]
            + pieces_out
            + [((spare, width), FULL)],
            [wide, square, square, lane_buffer, row_buffer, blocks, pltpu.SemaphoreType.DMA((3,))],
            [SMALL, ROWS, ROWS, ROWS, ROWS, FAR, FAR, FAR],
            14,
        )(place, patch_rows, bias, norm_gain, norm_shift, temporal_in, temporal_out, temporal_mix)
        arrived = spread(time[6:10])
        if layer == 0:
            arrived = flights.land(("x0", "core0"), arrived)
            first = arrived_here("x0")
            send("y0", first, by_y)
            send("x1", both_matrices(hidden_up, hidden_down, 1, near), by_x)
        arrived = flights.leave(arrived)
        space = call(
            partial(space_forward, dims, layer),
            [((span, width), HALF), ((span, 3 * width), HALF), ((span, 128), FULL)] + backs_out,
            [wide, pltpu.VMEM((span, width), FULL), pltpu.SemaphoreType.DMA((1,))],
            [SMALL, SMALL, ROWS] + [ROWS] * groups + [FAR],
            9,
        )(place, clip_of, time[10], *arrived, spatial_in)
        arrived = spread(space[3:])
        arrived = flights.land([f"y{layer}"], arrived)
        second = arrived_here(f"y{layer}")
        send("first", first, by_core)
        send("second", second, by_core)
        if layer + 1 < layers:
            send("core1", both_matrices(hidden_up, hidden_down, 1), by_core)
        arrived = flights.leave(arrived)
        arrived = flights.land(("first", "second"), arrived)
        gathered[layer] = (
            arrived_here(f"core{layer}"),
            first,
            second,
            arrived_here("first"),
            arrived_here("second"),
        )
        feed = call(
            partial(feed_forward, dims, layer),
            [
                ((rows, width), HALF),
                ((rows, width), FULL),
                ((rows, width), HALF),
                ((rows, hidden), HALF),
                ((rows, hidden), HALF),
                ((rows, width), FULL),
            ],
            [
                square,
                shards,
                shards,
                row_buffer,
                blocks,
                frame_rows,
                pltpu.VMEM((rows, width), HALF),
                pltpu.SemaphoreType.DMA((1,)),
                pltpu.SemaphoreType.DMA((12,)),
            ],
            [SMALL] + [ROWS] * groups + [ROWS] * 4 + [FAR] * 8,
            15,
        )(
            place, *arrived, share, time[5], norm_gain, norm_shift, spatial_out,
            hidden_up, hidden_down, *gathered[layer],
        )
        saved.append((patch_rows, time, space, feed))
        patch_rows = feed[5]
    patch_output = patch_rows[:count].reshape(frames, patches, width).astype(HALF)
    class_output = patch_rows[count : count + clips].astype(HALF)

    grad_rows = rows_of(patch_cotangent, class_cotangent)
    usual = blocks_dp == 2 * NEAR
    norms = [None] * layers

    def outer(pairs, split, micros):
        return outer_group(place, pairs, groups, split, micros)

    def start(name, pairs, path, split, micros, first=()):
        pairs = tuple(pairs)
        if split and not usual:
            flights.results[name] = reduce_whole([pair for early in first for pair in early[0]] + list(pairs))
            return
        parts = [early[1] for early in first] + [outer(pairs, split, micros)]
        if split:
            sizes = []
            for own in [early[0] for early in first] + [pairs]:
                sizes.append([right.shape[1] for left, right in own])
            flights.start(name, reduce_attention(parts, path, sum(sizes, [])))
        elif usual:
            flights.start(name, reduce_group(parts, path))
        else:
            flights.start(name, reduce_far(parts[0]))

    for layer in reversed(range(layers)):
        start_rows, time, space, feed = saved[layer]
        last = layer == 0
        feed_back = call(
            partial(feed_backward, dims, layer),
            [
                ((rows, width), HALF),
                ((rows, hidden), HALF),
                ((rows, width), HALF),
                ((rows, width), FULL),
                ((8, width), FULL),
            ]
            + pieces_out
            + [((8, width), FULL)],
            [
                square,
                shards,
                shards,
                row_buffer,
                row_buffer,
                blocks,
                pltpu.SemaphoreType.DMA((1,)),
                pltpu.SemaphoreType.DMA((12,)),
            ],
            [SMALL, SMALL] + [ROWS] * 5 + [FAR] * 8,
            23,
        )(
            place, clip_of, grad_rows, feed[4], feed[1],
            jnp.broadcast_to(inverse_counts[:, None], (spare, 128)), norm_gain, spatial_out,
            hidden_up, hidden_down, *gathered[layer],
        )
        update, grad_hidden, branch, back, feed_norms = feed_back[:5]
        arrived = spread(feed_back[5:9])
        pairs = ((feed[2], grad_hidden), (update, feed[3]))
        if last:
            pairs = flights.turn(["feed1"], pairs)
            time_pairs = lax.optimization_barrier((time_pairs, pairs))[0]
            start("attention1", time_pairs, "both", True, 9, [early])
            pairs = flights.leave(pairs, ["attention1"])
            start("feed0", pairs, "both", False, 10)
            arrived, feed_sum = lax.optimization_barrier((arrived, feed_sum))
            feed_sum = lax.psum_scatter(feed_sum, DP, scatter_dimension=0, tiled=True)
            arrived = flights.turn(["feed1", "attention1"], arrived)
        else:
            total = outer_group(place, pairs, groups, False, 10, True)[0]
            arrived, total = lax.optimization_barrier((arrived, total))
            total = total.reshape(-1, total.shape[-1])
            feed_sum = lax.psum_scatter(total, TENSOR, scatter_dimension=0, tiled=True)
        arrived = flights.leave(arrived)
        space_back = call(
            partial(space_backward, dims, layer),
            [((span, 3 * width), HALF)] + backs_out,
            [
                wide,
                pltpu.VMEM((span, width), FULL),
                pltpu.VMEM((span, width), HALF),
                pltpu.SemaphoreType.DMA((1,)),
            ],
            [ROWS] * groups + [ROWS] * 3 + [FAR],
            29,
        )(*arrived, feed_back[9], space[1], space[2], spatial_in)
        pieces = space_back[1:]
        if last:
            pieces = flights.land(["feed1", "feed0"], pieces)
        arrived = spread(pieces)
        pairs = ((space[0], space_back[0]), (feed[0], branch))
        if last:
            start("space0", pairs, "xyuw", True, 8)
            arrived = flights.land(["attention1"], arrived)
            arrived = flights.leave(arrived)
        else:
            pairs = flights.turn(["feed1"], pairs)
            if usual:
                early = (pairs, outer(pairs, True, 8))
                arrived, parts = lax.optimization_barrier((arrived, early[1]))
                early = (pairs, parts)
            else:
                early = (pairs, None)
        time_back = call(
            partial(time_backward, dims, layer),
            [
                ((rows, width), HALF),
                ((rows, width), HALF),
                ((rows, 3 * width), HALF),
                ((rows, width), FULL),
                ((8, width), FULL),
            ],
            [
                wide,
                square,
                square,
                lane_buffer,
                row_buffer,
                blocks,
                frame_rows,
                pltpu.VMEM((rows, width), HALF),
                pltpu.SemaphoreType.DMA((3,)),
            ],
            [SMALL] + [ROWS] * groups + [ROWS] * 8 + [FAR] * 3,
            14,
        )(
            place, *arrived, member, back, time[5], start_rows, time[1], time[2], bias,
            norm_gain, temporal_in, temporal_out, temporal_mix,
        )
        grad_rows = time_back[3]
        norms[layer] = (time_back[4], feed_norms)
        pairs = ((time[0], time_back[2]), (time[3], time_back[1]), (time[4], time_back[0]))
        if last:
            ordered = [
                entry[at : at + 1]
                for part, at in ((0, 2), (0, 0), (1, 0), (0, 3), (0, 1), (1, 1))
                for entry in [norms[index][part] for index in range(layers)]
            ]
            ordered = jnp.concatenate(ordered, 0)
            if usual:
                flights.start("norms", reduce_norms(ordered))
            else:
                total = lax.psum(ordered, TENSOR)
                flights.results["norms"] = lax.psum_scatter(
                    total, DP, scatter_dimension=1, tiled=True
                )
            start("time0", pairs, "both", True, 9)
            token = grad_rows[count : count + clips]
            token = flights.leave(token, ["time0"])
            token, flights.results["feed1"] = lax.optimization_barrier((token, feed_sum))
        else:
            time_pairs = pairs
            grad_rows = flights.turn(["feed1"], grad_rows)
    for names in (
        ("attention1", "feed0", "space0"),
        ("attention1", "feed0", "time0", "norms"),
        ("space0", "time0", "norms"),
        ("attention1", "feed0"),
        ("space0", "time0", "norms"),
        ("attention1", "feed0"),
        ("space0", "time0", "norms"),
        ("attention1",),
        ("space0", "time0", "norms"),
        ("space0", "time0"),
    ):
        token = flights.turn(names, token)
    while flights.running:
        token = flights.turn(list(flights.running), token)
    results = flights.results
    lanes = width // blocks_dp

    norm_sums = results["norms"].reshape(2, 3, layers, lanes).transpose(0, 2, 1, 3)
    feeds = (results["feed0"], results["feed1"])
    late = results["attention1"]
    time_sums = (results["time0"], late[2:])
    space_sums = (results["space0"], late[:2])
    gradients = (
        *[jnp.stack([sums[index] for sums in time_sums]) for index in range(3)],
        *[jnp.stack([sums[index] for sums in space_sums]) for index in range(2)],
        jnp.stack([sums[:, :width].astype(FULL) for sums in feeds]),
        jnp.stack([sums[:, width:].T.astype(FULL) for sums in feeds]),
        norm_sums[0],
        norm_sums[1],
    )
    patch_grad = grad_rows[:count].reshape(frames, patches, width)
    class_grad = token
    return (patch_output, class_output, patch_grad, class_grad, *gradients)


def solution(mesh):
    placed = (
        P(DP, TENSOR, None),
        P(DP, None),
        P(DP, None),
        P(DP, TENSOR, None),
        P(DP, None),
        P(),
        P(),
        P(),
        P(),
        P(),
        P(None, None, TENSOR),
        P(None, TENSOR, None),
        P(),
        P(),
    )
    return jax.shard_map(
        body,
        mesh=mesh,
        in_specs=placed,
        out_specs=(
            P(DP, TENSOR, None),
            P(DP, None),
            P(DP, TENSOR, None),
            P(DP, None),
            P(None, DP, None),
            P(None, DP, None),
            P(None, DP, None),
            P(None, DP, None),
            P(None, DP, None),
            P(None, DP, TENSOR),
            P(None, TENSOR, DP),
            P(None, None, DP),
            P(None, None, DP),
        ),
        check_vma=False,
    )
```

```python
from functools import partial

import jax
import jax.numpy as jnp
from jax import lax
from jax.experimental import pallas as pl
from jax.experimental.pallas import tpu as pltpu
from jax.sharding import PartitionSpec as P

HEADS = 12
EPS = 1e-06
HIGH = lax.Precision.HIGHEST
HALF = jnp.bfloat16
FULL = jnp.float32
NEAR = 4
TENSOR = "tensor"
DP = "dp"
TILE = 256
VMEM_BYTES = 58 << 20
SMEM = pl.BlockSpec(memory_space=pltpu.SMEM)
SMALL, ROWS, FAR = range(3)
HBM = pl.BlockSpec(memory_space=pltpu.HBM)
ROOT_HALF = 0.5**0.5
DENSITY = (2.0 * 3.141592653589793) ** -0.5


def up_to(value, step):
    return -(-value // step) * step


def dot(left, right):
    return jnp.dot(left, right, preferred_element_type=FULL)


def dot_back(left, right):
    return lax.dot_general(left, right, (((1,), (1,)), ((), ())), preferred_element_type=FULL)


def dot_outer(left, right):
    return lax.dot_general(left, right, (((0,), (0,)), ((), ())), preferred_element_type=FULL)


def unit_of(values):
    centred = values - jnp.mean(values, -1, keepdims=True)
    inverse = lax.rsqrt(jnp.mean(centred * centred, -1, keepdims=True) + EPS)
    return centred * inverse, inverse


def unit_back(grad, unit, inverse, gain):
    scaled = grad * gain
    inner = (
        scaled
        - jnp.mean(scaled, -1, keepdims=True)
        - unit * jnp.mean(scaled * unit, -1, keepdims=True)
    )
    return inner * inverse


def head_lanes(head_size, half):
    lane = lax.broadcasted_iota(jnp.int32, (1, 2 * head_size), 1)
    return (lane // head_size) == half


def over_rows(rows, step, run):
    for start in range(0, rows, step):
        run(start, min(step, rows - start))


def two_heads(values, head_size):
    return jnp.concatenate(
        [jnp.where(head_lanes(head_size, half), values, 0) for half in range(2)], 0
    )


def one_of_two(values, head_size):
    rows = values.shape[0] // 2
    return jnp.where(head_lanes(head_size, 0), values[:rows], values[rows:])


def interleave(order, frame, frames, values):
    for group in range(order.shape[0]):
        part = values[:, group * 128 : (group + 1) * 128]
        order[group, pl.ds(frame, values.shape[0], stride=frames), :] = part


def pick(order, frame, frames, patches):
    own = pl.ds(frame, patches, stride=frames)
    return jnp.concatenate([order[group, own, :] for group in range(order.shape[0])], 1)


def shard_copies(place_ref, refs, target, which):
    own, core, far_first, far_second, core_first, core_second = refs
    half = far_first.shape[1]
    first = pl.multiple_of(place_ref[1] * half, half)
    second = pl.multiple_of((1 - place_ref[1]) * half, half)
    return [
        [(own, target.at[0])],
        [(core, target.at[1])],
        [
            (far_first.at[which], target.at[2, pl.ds(first, half)]),
            (far_second.at[which], target.at[2, pl.ds(second, half)]),
        ],
        [
            (core_first.at[which], target.at[3, pl.ds(first, half)]),
            (core_second.at[which], target.at[3, pl.ds(second, half)]),
        ],
    ]


def start_shards(place_ref, own, peers, up_ref, down_ref, sems):
    waits = []
    index = 0
    for pairs in zip(
        shard_copies(place_ref, own[:2] + peers, up_ref, 0),
        shard_copies(place_ref, own[2:] + peers, down_ref, 1),
    ):
        group = []
        for source, target in pairs[0] + pairs[1]:
            copy = pltpu.make_async_copy(source, target, sems.at[index])
            copy.start()
            group.append(copy)
            index += 1
        waits.append(group)
    return waits


def fetch(sources, targets, sems):
    copies = [
        pltpu.make_async_copy(source, target, sems.at[index])
        for index, (source, target) in enumerate(zip(sources, targets))
    ]
    for copy in copies:
        copy.start()
    return copies


def attend_forward(load, store, store_total, heads, head_size, bias):
    scale = head_size**-0.5
    totals = None
    if bias.shape[0] > 1:
        bias = jnp.concatenate([bias, bias], 0)
    for pair in range(heads // 2):
        query, key, value = (load(part, pair) for part in range(3))
        rows = query.shape[0]
        scores = dot_back(two_heads(query, head_size), key) * scale + bias
        top = jnp.max(scores, -1, keepdims=True)
        raised = jnp.exp(scores - top)
        total = jnp.sum(raised, -1, keepdims=True)
        mixed = dot(raised.astype(HALF), value) * (1.0 / total)
        log_total = top + jnp.log(total)
        if totals is None:
            lanes = lax.broadcasted_iota(jnp.int32, (rows, 128), 1)
            totals = jnp.zeros(lanes.shape, FULL)
        totals = jnp.where(lanes == pair * 2, log_total[:rows], totals)
        totals = jnp.where(lanes == pair * 2 + 1, log_total[rows:], totals)
        store(pair, one_of_two(mixed, head_size))
    store_total(totals)


def attend_backward(load, load_grad, totals, store, heads, head_size, bias):
    scale = head_size**-0.5
    totals = totals.T
    if bias.shape[1] > 1:
        bias = jnp.concatenate([bias, bias], 1)
    for pair in range(heads // 2):
        query, key, value = (load(part, pair) for part in range(3))
        query = two_heads(query, head_size)
        grad = two_heads(load_grad(pair), head_size)
        total = jnp.concatenate([totals[2 * pair + half : 2 * pair + half + 1] for half in range(2)], 1)
        prob = jnp.exp(dot_back(key, query) * scale + (bias - total))
        grad_prob = dot_back(value, grad)
        delta = jnp.sum(prob * grad_prob, 0, keepdims=True)
        grad_score = (prob * (grad_prob - delta)).astype(HALF)
        store(0, pair, one_of_two(dot_outer(grad_score, key), head_size) * scale)
        store(1, pair, dot(grad_score, query) * scale)
        store(2, pair, dot(prob.astype(HALF), grad))


def row_blocks(rows, step):
    return [(start, min(step, rows - start)) for start in range(0, rows, step)]


def time_forward(dims, layer, place_ref, x_ref, bias_ref, gain_ref, shift_ref, in_hbm, out_hbm, mix_hbm,
                 normed_ref, triple_ref, total_ref, mixed_ref, projected_ref, after_ref,
                 send0, send1, send2, send3, class_ref,
                 in_ref, out_ref, mix_ref, order, plain, blocks, sems):
    frames, patches, width, heads, groups = dims
    count = frames * patches
    rows = x_ref.shape[0]
    step = bias_ref.shape[0]
    copies = fetch(
        (in_hbm.at[layer], out_hbm.at[layer], mix_hbm.at[layer]), (in_ref, out_ref, mix_ref), sems
    )
    gain = gain_ref[layer, 0:1, :]
    shift = shift_ref[layer, 0:1, :]
    for frame in range(frames):
        unit, unused = unit_of(x_ref[frame * patches : (frame + 1) * patches, :])
        interleave(order, frame, frames, unit * gain + shift)
    for group in range(width // 128):
        order[group, count:, :] = jnp.zeros((rows - count, 128), FULL)
        normed_ref[:, group * 128 : (group + 1) * 128] = order[group].astype(HALF)
    normed_ref.flush()
    copies[0].wait()
    for column in range(0, 3 * width, TILE):
        part = slice(column, column + TILE)
        triple_ref[:, part] = dot(normed_ref[...], in_ref[:, part]).astype(HALF)
    triple_ref.flush()
    for begin, size in row_blocks(rows, step):
        own = slice(begin, begin + size)

        def load(part, pair):
            start = part * width + pair * 128
            return triple_ref[own, start : start + 128]

        def store(pair, mixed):
            order[pair, own, :] = mixed

        def store_total(totals):
            total_ref[own, :] = totals

        attend_forward(
            load, store, store_total, heads, width // heads, bias_ref[0:size, 0:size]
        )
    for frame in range(frames):
        plain[frame * patches : (frame + 1) * patches, :] = pick(order, frame, frames, patches)
    plain[count:, :] = jnp.zeros((rows - count, width), FULL)
    mixed_ref[...] = plain[...].astype(HALF)
    mixed_ref.flush()
    copies[1].wait()
    for column in range(0, width, TILE):
        part = slice(column, column + TILE)
        projected_ref[:, part] = dot(mixed_ref[...], out_ref[:, part]).astype(HALF)
    projected_ref.flush()
    copies[2].wait()
    for column in range(0, width, TILE):
        part = slice(column, column + TILE)
        after_ref[:, part] = x_ref[:, part] + dot(projected_ref[...], mix_ref[:, part])
    after_ref.flush()
    gain = gain_ref[layer, 1:2, :]
    shift = shift_ref[layer, 1:2, :]

    def norm(start, size):
        own = slice(start, start + size)
        unit, unused = unit_of(after_ref[own, :])
        plain[own, :] = unit * gain + shift

    over_rows(rows, 80, norm)
    send_blocks(plain, blocks, (send0, send1, send2, send3), place_ref[0], count // groups)
    class_ref[...] = plain[count:, :]


def send_blocks(plain, blocks, sends, place, size):
    groups = len(sends)
    rows = sends[0].shape[0]
    for group in range(groups):
        blocks[group, 0:size, :] = plain[group * size : (group + 1) * size, :]
        blocks[group, size:rows, :] = jnp.zeros((rows - size, plain.shape[1]), FULL)
    for away in range(groups):
        sends[away][...] = blocks[place ^ away][0:rows].astype(HALF)


def space_forward(dims, layer, place_ref, clip_ref, class_ref, piece0, piece1, piece2, piece3, in_hbm,
                  normed_ref, triple_ref, total_ref, send0, send1, send2, send3,
                  in_ref, plain, sems):
    frames, patches, width, heads, groups = dims
    own_frames = frames // groups
    seq = groups * patches
    rows = normed_ref.shape[0] // own_frames
    copies = fetch((in_hbm.at[layer],), (in_ref,), sems)
    pieces = [piece0, piece1, piece2, piece3]
    for away, piece in enumerate(pieces):
        values = piece[...].astype(FULL)
        for frame in range(own_frames):
            start = frame * rows + away * patches
            plain[start : start + patches, :] = values[frame * patches : (frame + 1) * patches]
    for frame in range(own_frames):
        start = frame * rows + seq
        plain[start : start + rows - seq, :] = jnp.zeros((rows - seq, width), FULL)
        clip = clip_ref[place_ref[0] * own_frames + frame]
        plain[start : start + 1, :] = class_ref[pl.ds(clip, 1), :]
    normed_ref[...] = plain[...].astype(HALF)
    normed_ref.flush()
    copies[0].wait()
    for column in range(0, 3 * width, TILE):
        part = slice(column, column + TILE)
        triple_ref[:, part] = dot(normed_ref[...], in_ref[:, part]).astype(HALF)
    triple_ref.flush()
    keys = lax.broadcasted_iota(jnp.int32, (1, rows), 1)
    bias = jnp.where(keys <= seq, 0.0, -1e30)

    for frame in range(own_frames):
        own = slice(frame * rows, (frame + 1) * rows)

        def load(part, pair):
            start = part * width + pair * 128
            return triple_ref[own, start : start + 128]

        def store(pair, mixed):
            plain[own, pair * 128 : (pair + 1) * 128] = mixed

        def store_total(totals):
            total_ref[own, :] = totals

        attend_forward(load, store, store_total, heads, width // heads, bias)
    return_pieces(plain, (send0, send1, send2, send3), own_frames, patches, rows)


def return_pieces(plain, sends, own_frames, patches, rows):
    seq = len(sends) * patches
    tail = []
    for frame in range(own_frames):
        row = plain[frame * rows + seq : frame * rows + seq + 1, :]
        high = row.astype(HALF).astype(FULL)
        tail += [high, row - high]
    size = own_frames * patches
    spare = sends[0].shape[0] - size - len(tail)
    tail.append(jnp.zeros((spare, plain.shape[1]), FULL))
    for away, send in enumerate(sends):
        kept = [
            plain[frame * rows + away * patches : frame * rows + (away + 1) * patches, :]
            for frame in range(own_frames)
        ]
        send[...] = jnp.concatenate(kept + tail, 0).astype(HALF)


def take_pieces(pieces, blocks, plain, frame_rows, place, size, own_frames):
    for away, piece in enumerate(pieces):
        blocks[place ^ away] = piece[...].astype(FULL)
    for group in range(len(pieces)):
        plain[group * size : (group + 1) * size, :] = blocks[group, 0:size, :]
        for frame in range(own_frames):
            start = size + 2 * frame
            frame_rows[group * own_frames + frame : group * own_frames + frame + 1, :] = (
                blocks[group, start : start + 1, :] + blocks[group, start + 1 : start + 2, :]
            )


def feed_forward(dims, layer, place_ref, piece0, piece1, piece2, piece3, share_ref, after_ref,
                 gain_ref, shift_ref, out_hbm,
                 up_hbm, down_hbm, peer_up, peer_down, peer2, peer3, peer4, peer5,
                 mixed_ref, rows_ref, normed_ref, active_ref, slope_ref, next_ref,
                 out_ref, up_ref, down_ref, plain, blocks, frame_rows, whole, out_sem, sems):
    frames, patches, width, heads, groups = dims
    count = frames * patches
    rows = after_ref.shape[0]
    size = count // groups
    place = place_ref[0]
    copies = fetch((out_hbm.at[layer],), (out_ref,), out_sem)
    own = (up_hbm.at[layer], peer_up.at[layer], down_hbm.at[layer], peer_down.at[layer])
    peers = (peer2, peer3, peer4, peer5)
    shards = start_shards(place_ref, own, peers, up_ref, down_ref, sems)
    take_pieces(
        (piece0, piece1, piece2, piece3), blocks, plain, frame_rows, place, size, frames // groups
    )
    plain[count:, :] = jnp.dot(
        share_ref[...], frame_rows[...], precision=HIGH, preferred_element_type=FULL
    )
    whole[...] = plain[...].astype(HALF)
    leader = jnp.where(place == 0, 1.0, 0.0).astype(FULL)
    kept = lax.broadcasted_iota(jnp.int32, (rows, 1), 0) < count
    kept = jnp.where(kept, 1.0, leader)
    mixed_ref[...] = (plain[...] * kept).astype(HALF)
    mixed_ref.flush()
    copies[0].wait()
    for column in range(0, width, TILE):
        part = slice(column, column + TILE)
        rows_ref[:, part] = after_ref[:, part] + dot(whole[...], out_ref[:, part])
    rows_ref.flush()
    gain = gain_ref[layer, 2:3, :]
    shift = shift_ref[layer, 2:3, :]

    def norm(start, size):
        own = slice(start, start + size)
        unit, unused = unit_of(rows_ref[own, :])
        plain[own, :] = unit * gain + shift

    over_rows(rows, 80, norm)
    whole[...] = plain[...].astype(HALF)
    normed_ref[...] = (plain[...] * kept).astype(HALF)
    normed_ref.flush()
    next_ref[...] = rows_ref[...]
    for away in range(groups):
        for copy in shards[away]:
            copy.wait()
        for column in range(0, width, TILE):
            part = slice(column, column + TILE)
            hidden = dot(whole[...], up_ref[away, :, part])
            below = 0.5 + 0.5 * lax.erf(hidden * ROOT_HALF)
            active = (hidden * below).astype(HALF)
            slope = below + hidden * (jnp.exp(hidden * hidden * -0.5) * DENSITY)
            start = away * width + column
            active_ref[:, start : start + TILE] = active
            slope_ref[:, start : start + TILE] = slope.astype(HALF)
        own = slice(away * width, (away + 1) * width)
        for column in range(0, width, TILE):
            part = slice(column, column + TILE)
            next_ref[:, part] += dot(active_ref[:, own], down_ref[away, :, part])
        end = count // 16 * 16
        active_ref[end:, own] = (active_ref[end:, own].astype(FULL) * kept[end:]).astype(HALF)
        active_ref.flush(own)
        slope_ref.flush(own)


def feed_backward(dims, layer, place_ref, clip_ref, grad_ref, slope_ref, rows_ref, share_ref, gain_ref,
                  out_hbm, up_hbm, down_hbm, peer_up, peer_down, peer2, peer3, peer4, peer5,
                  update_ref, hidden_ref, branch_ref, back_ref, norms_ref,
                  send0, send1, send2, send3, class_ref,
                  out_ref, up_ref, down_ref, total, plain, blocks, out_sem, sems):
    frames, patches, width, heads, groups = dims
    count = frames * patches
    rows = grad_ref.shape[0]
    place = place_ref[0]
    own_frames = frames // groups
    own = (up_hbm.at[layer], peer_up.at[layer], down_hbm.at[layer], peer_down.at[layer])
    peers = (peer2, peer3, peer4, peer5)
    shards = start_shards(place_ref, own, peers, up_ref, down_ref, sems)
    copies = fetch((out_hbm.at[layer],), (out_ref,), out_sem)
    update_ref[...] = grad_ref[...].astype(HALF)
    update_ref.flush()
    for away in range(groups):
        for copy in shards[away]:
            copy.wait()
        for column in range(0, width, TILE):
            part = slice(column, column + TILE)
            start = away * width + column
            grad_active = dot_back(update_ref[...], down_ref[away, part, :])
            slope = slope_ref[:, start : start + TILE].astype(FULL)
            grad_hidden = (grad_active * slope).astype(HALF)
            hidden_ref[:, start : start + TILE] = grad_hidden
        own = slice(away * width, (away + 1) * width)
        for column in range(0, width, TILE):
            part = slice(column, column + TILE)
            term = dot_back(hidden_ref[:, own], up_ref[away, part, :])
            if away == 0:
                total[:, part] = term
            else:
                total[:, part] += term
        hidden_ref.flush(own)
    gain = gain_ref[layer, 2:3, :]
    leader = jnp.where(place == 0, 1.0, 0.0).astype(FULL)
    norms_ref[...] = jnp.zeros(norms_ref.shape, FULL)
    def norm(start, size):
        own = slice(start, start + size)
        unit, inverse = unit_of(rows_ref[own, :])
        grad = total[own, :]
        back = grad_ref[own, :] + unit_back(grad, unit, inverse, gain)
        back_ref[own, :] = back
        branch_ref[own, :] = back.astype(HALF)
        kept = lax.broadcasted_iota(jnp.int32, (size, 1), 0) + start < count
        grad = jnp.where(kept, grad, grad * leader)
        norms_ref[0:1, :] += jnp.sum(grad * unit, 0, keepdims=True)
        norms_ref[1:2, :] += jnp.sum(grad, 0, keepdims=True)

    over_rows(rows, 80, norm)
    back_ref.flush()
    branch_ref.flush()
    copies[-1].wait()
    for column in range(0, width, TILE):
        part = slice(column, column + TILE)
        plain[:, part] = dot_back(branch_ref[...], out_ref[part, :])
    send_blocks(plain, blocks, (send0, send1, send2, send3), place, count // groups)
    for frame in range(own_frames):
        clip = clip_ref[place * own_frames + frame]
        class_ref[frame : frame + 1, :] = (
            plain[pl.ds(count + clip, 1), :] * share_ref[pl.ds(clip, 1), 0:1]
        )


def space_backward(dims, layer, piece0, piece1, piece2, piece3, class_ref, triple_ref, total_ref, in_hbm,
                   grad_ref, send0, send1, send2, send3,
                   in_ref, plain, mixed, sems):
    frames, patches, width, heads, groups = dims
    own_frames = frames // groups
    seq = groups * patches
    rows = triple_ref.shape[0] // own_frames
    copies = fetch((in_hbm.at[layer],), (in_ref,), sems)
    for away, piece in enumerate((piece0, piece1, piece2, piece3)):
        values = piece[...].astype(FULL)
        for frame in range(own_frames):
            start = frame * rows + away * patches
            plain[start : start + patches, :] = values[frame * patches : (frame + 1) * patches]
    for frame in range(own_frames):
        start = frame * rows + seq
        plain[start : start + rows - seq, :] = jnp.zeros((rows - seq, width), FULL)
        plain[start : start + 1, :] = class_ref[frame : frame + 1, :]
    mixed[...] = plain[...].astype(HALF)
    keys = lax.broadcasted_iota(jnp.int32, (rows, 1), 0)
    bias = jnp.where(keys <= seq, 0.0, -1e30)
    for frame in range(own_frames):
        own = slice(frame * rows, (frame + 1) * rows)

        def load(part, pair):
            start = part * width + pair * 128
            return triple_ref[own, start : start + 128]

        def load_grad(pair):
            return mixed[own, pair * 128 : (pair + 1) * 128]

        def store(part, pair, grad):
            start = part * width + pair * 128
            grad_ref[own, start : start + 128] = grad.astype(HALF)

        attend_backward(load, load_grad, total_ref[own, :], store, heads, width // heads, bias)
    grad_ref.flush()
    copies[0].wait()
    for column in range(0, width, TILE):
        part = slice(column, column + TILE)
        plain[:, part] = dot_back(grad_ref[...], in_ref[part, :])
    return_pieces(plain, (send0, send1, send2, send3), own_frames, patches, rows)


def time_backward(dims, layer, place_ref, piece0, piece1, piece2, piece3, member_ref, back_ref, after_ref, x_ref,
                  triple_ref, total_ref, bias_ref, gain_ref, in_hbm, out_hbm, mix_hbm,
                  branch_ref, projected_ref, grad_ref, next_ref, norms_ref,
                  in_ref, out_ref, mix_ref, order, plain, blocks, frame_rows, mixed, sems):
    frames, patches, width, heads, groups = dims
    count = frames * patches
    rows = x_ref.shape[0]
    step = bias_ref.shape[0]
    place = place_ref[0]
    copies = fetch(
        (mix_hbm.at[layer], out_hbm.at[layer], in_hbm.at[layer]), (mix_ref, out_ref, in_ref), sems
    )
    take_pieces(
        (piece0, piece1, piece2, piece3),
        blocks,
        plain,
        frame_rows,
        place,
        count // groups,
        frames // groups,
    )
    plain[count:, :] = jnp.dot(
        member_ref[...], frame_rows[...], precision=HIGH, preferred_element_type=FULL
    )
    leader = jnp.where(place == 0, 1.0, 0.0).astype(FULL)
    norms_ref[...] = jnp.zeros(norms_ref.shape, FULL)
    gain = gain_ref[layer, 1:2, :]

    def space_norm(start, size):
        own = slice(start, start + size)
        unit, inverse = unit_of(after_ref[own, :])
        grad = plain[own, :]
        back = back_ref[own, :] + unit_back(grad, unit, inverse, gain)
        next_ref[own, :] = back
        kept = lax.broadcasted_iota(jnp.int32, (size, 1), 0) + start < count
        branch_ref[own, :] = jnp.where(kept, back, 0.0).astype(HALF)
        grad = jnp.where(kept, grad, grad * leader)
        norms_ref[0:1, :] += jnp.sum(grad * unit, 0, keepdims=True)
        norms_ref[1:2, :] += jnp.sum(grad, 0, keepdims=True)

    over_rows(rows, 80, space_norm)
    branch_ref.flush()
    copies[0].wait()
    for column in range(0, width, TILE):
        part = slice(column, column + TILE)
        projected_ref[:, part] = dot_back(branch_ref[...], mix_ref[part, :]).astype(HALF)
    projected_ref.flush()
    copies[1].wait()
    for column in range(0, width, TILE):
        part = slice(column, column + TILE)
        plain[:, part] = dot_back(projected_ref[...], out_ref[part, :])
    for frame in range(frames):
        interleave(order, frame, frames, plain[frame * patches : (frame + 1) * patches, :])
    for group in range(width // 128):
        order[group, count:, :] = jnp.zeros((rows - count, 128), FULL)
        mixed[:, group * 128 : (group + 1) * 128] = order[group].astype(HALF)

    for begin, size in row_blocks(rows, step):
        own = slice(begin, begin + size)

        def load(part, pair):
            start = part * width + pair * 128
            return triple_ref[own, start : start + 128]

        def load_grad(pair):
            return mixed[own, pair * 128 : (pair + 1) * 128]

        def store(part, pair, grad):
            start = part * width + pair * 128
            grad_ref[own, start : start + 128] = grad.astype(HALF)

        attend_backward(
            load,
            load_grad,
            total_ref[own, :],
            store,
            heads,
            width // heads,
            bias_ref[0:size, 0:size],
        )
    grad_ref.flush()
    copies[2].wait()
    for column in range(0, width, TILE):
        part = slice(column, column + TILE)
        grad = dot_back(grad_ref[...], in_ref[part, :])
        for group in range(TILE // 128):
            order[column // 128 + group] = grad[:, group * 128 : (group + 1) * 128]
    gain = gain_ref[layer, 0:1, :]
    for frame in range(frames):
        own = slice(frame * patches, (frame + 1) * patches)
        grad = pick(order, frame, frames, patches)
        unit, inverse = unit_of(x_ref[own, :])
        next_ref[own, :] += unit_back(grad, unit, inverse, gain)
        norms_ref[2:3, :] += jnp.sum(grad * unit, 0, keepdims=True)
        norms_ref[3:4, :] += jnp.sum(grad, 0, keepdims=True)


def cost(micros):
    return pl.CostEstimate(flops=micros, bytes_accessed=micros, transcendentals=0)


class Fetched:
    def __init__(self, source, target, sem):
        self.target, self.shape = target, target.shape
        self.copy = pltpu.make_async_copy(source, target, sem)
        self.copy.start()

    def wait(self):
        if self.copy is not None:
            self.copy.wait()
            self.copy = None

    def __getitem__(self, index):
        self.wait()
        return self.target[index]


class Written:
    def __init__(self, source, target, sems):
        self.source, self.target, self.sems = source, target, sems
        self.shape = source.shape
        self.copies = []

    def __getitem__(self, index):
        return self.source[index]

    def __setitem__(self, index, values):
        self.source[index] = values

    def flush(self, columns=None):
        parts = (self.source, self.target)
        if columns is not None:
            parts = tuple(ref.at[:, columns] for ref in parts)
        copy = pltpu.make_async_copy(*parts, self.sems.at[len(self.copies)])
        copy.start()
        self.copies.append(copy)

    def wait(self):
        if not self.copies:
            self.flush()
        for copy in self.copies:
            copy.wait()


def call(kernel, outs, scratch, specs, micros):
    def run(*arrays):
        fetched = [index for index, kind in enumerate(specs) if kind == ROWS]
        count, results = len(specs), len(outs)

        def whole(*refs):
            ins, out_refs = list(refs[:count]), refs[count : count + results]
            rest = refs[count + results :]
            in_refs, rest = rest[: len(fetched)], rest[len(fetched) :]
            kept, rest = rest[:results], rest[results:]
            in_sems, out_sems = rest[0], rest[1]
            for place, index in enumerate(fetched):
                ins[index] = Fetched(ins[index], in_refs[place], in_sems.at[place])
            written = [
                Written(source, target, out_sems.at[index])
                for index, (source, target) in enumerate(zip(kept, out_refs))
            ]
            kernel(*ins, *written, *rest[2:])
            for index in fetched:
                ins[index].wait()
            for result in written:
                result.wait()

        return pl.pallas_call(
            whole,
            out_shape=[jax.ShapeDtypeStruct(shape, kind) for shape, kind in outs],
            in_specs=[SMEM if kind == SMALL else HBM for kind in specs],
            out_specs=[HBM] * results,
            scratch_shapes=[pltpu.VMEM(arrays[index].shape, arrays[index].dtype) for index in fetched]
            + [pltpu.VMEM(shape, kind) for shape, kind in outs]
            + [pltpu.SemaphoreType.DMA((len(fetched),)), pltpu.SemaphoreType.DMA((results, 4))]
            + scratch,
            compiler_params=pltpu.CompilerParams(vmem_limit_bytes=VMEM_BYTES),
            cost_estimate=cost(micros),
        )(*arrays)

    return run


def outer_group(place, pairs, groups, split, micros, whole=False):
    rows = pairs[0][0].shape[1]
    parts = 2 if split else groups
    inner = parts // 2
    sizes = [right.shape[1] // parts for left, right in pairs]
    total = sum(sizes)
    tiles = []
    for side in range(2):
        for index, size in enumerate(sizes):
            for shard in range(inner):
                for start in range(0, size, 768):
                    tiles.append((side, index, shard, start, min(768, size - start)))
    count = len(pairs)
    results = 1 if whole else 2

    def kernel(place_ref, *refs):
        lefts, rights = refs[:count], refs[count : 2 * count]
        outs = refs[2 * count : 2 * count + results]
        left_refs = refs[2 * count + results : 3 * count + results]
        right_refs, stage, left_sems, right_sems, out_sems = refs[3 * count + results :]
        arrivals = []
        lefts_here = []
        for number, (side, index, shard, start, size) in enumerate(tiles):
            if index == len(lefts_here):
                copy = pltpu.make_async_copy(lefts[index], left_refs[index], left_sems.at[index])
                copy.start()
                lefts_here.append(copy)
            if split:
                part = jnp.where(place_ref[0] % 2 == 0, 1 - side, side)
                begin = pl.multiple_of(part * sizes[index] + start, 128)
            else:
                begin = (2 * shard + 1 - side) * sizes[index] + start
            copy = pltpu.make_async_copy(
                rights[index].at[:, pl.ds(begin, size)],
                right_refs.at[number, pl.ds(0, rights[index].shape[0]), pl.ds(0, size)],
                right_sems.at[number],
            )
            copy.start()
            arrivals.append(copy)
        leaving = []
        waited = [False] * count
        for number, (side, index, shard, start, size) in enumerate(tiles):
            if not waited[index]:
                lefts_here[index].wait()
                waited[index] = True
            arrivals[number].wait()
            depth = lefts[index].shape[0]
            terms = dot_outer(left_refs[index][...], right_refs[number, 0:depth, 0:size])
            stage[number, :, 0:size] = terms.astype(HALF)
            column = sum(sizes[:index]) + start
            if whole:
                target = outs[0].at[(2 * shard + 1 - side) ^ place_ref[0]]
            else:
                target = outs[side] if split else outs[side].at[shard]
            copy = pltpu.make_async_copy(
                stage.at[number, :, pl.ds(0, size)],
                target.at[:, pl.ds(column, size)],
                out_sems.at[number],
            )
            copy.start()
            leaving.append(copy)
        for copy in leaving:
            copy.wait()

    shape = (rows, total) if split else (groups if whole else inner, rows, total)
    lefts, rights = zip(*pairs)
    width = max(tile[4] for tile in tiles)
    return pl.pallas_call(
        kernel,
        out_shape=[jax.ShapeDtypeStruct(shape, HALF)] * results,
        in_specs=[SMEM] + [HBM] * (2 * count),
        out_specs=[HBM] * results,
        scratch_shapes=[pltpu.VMEM(left.shape, HALF) for left in lefts]
        + [
            pltpu.VMEM((len(tiles), max(left.shape[0] for left in lefts), width), HALF),
            pltpu.VMEM((len(tiles), rows, width), HALF),
            pltpu.SemaphoreType.DMA((count,)),
            pltpu.SemaphoreType.DMA((len(tiles),)),
            pltpu.SemaphoreType.DMA((len(tiles),)),
        ],
        compiler_params=pltpu.CompilerParams(vmem_limit_bytes=VMEM_BYTES),
        cost_estimate=cost(micros),
    )(place, *lefts, *rights)


def exchange(axis, bit):
    return (axis, [(index, index ^ bit) for index in range(lax.axis_size(axis))])


def swap(values, axis, bit):
    return lax.ppermute(values, *exchange(axis, bit))


def reduce_group(groups, path):
    others = yield [(send, exchange(TENSOR, 1)) for send, keep in groups]
    sums = [keep + other for (send, keep), other in zip(groups, others)]
    values = sums[0] if len(sums) == 1 else jnp.concatenate(sums, -1)
    columns = values.shape[-1]
    blocks = lax.axis_size(DP)
    far = blocks // 2
    place = lax.axis_index(DP)
    bits = {"x": lax.axis_index(TENSOR) // 2, "y": place % 2, "u": place // 2 % 2, "w": place // 4}
    ways = {
        "x": exchange(TENSOR, 2),
        "y": exchange(DP, 1),
        "u": exchange(DP, 2),
        "w": exchange(DP, 4),
    }
    if values.ndim == 3:
        values = values.reshape(2, 2, 2, 2, -1, columns)
        dims = "xwuy"
        bits["x"] = 0
    else:
        values = values.reshape(2, 2, 2, 2, -1, columns)
        dims = "wuyx"

    def side(array, left, axis, mine):
        bit = bits[axis] if mine else 1 - bits[axis]
        return lax.dynamic_index_in_dim(array, bit, left.index(axis), False)

    if path == "both":
        middle = columns // 2 // 128 * 128
        tracks = [[values[..., :middle], "xy"], [values[..., middle:], "yx"]]
        left = [dims, dims]
        for step in range(2):
            others = yield [
                (side(array, rest, way[step], False), ways[way[step]])
                for (array, way), rest in zip(tracks, left)
            ]
            tracks = [
                [side(array, rest, way[step], True) + other, way]
                for (array, way), rest, other in zip(tracks, left, others)
            ]
            left = [rest.replace(way[step], "") for (array, way), rest in zip(tracks, left)]
        values = jnp.concatenate([array for array, way in tracks], -1)
        dims = left[0]
        path = "uw"
    for axis in path:
        other = yield [(side(values, dims, axis, False), ways[axis])]
        values = side(values, dims, axis, True) + other[0]
        dims = dims.replace(axis, "")
    return values


def reduce_norms(values):
    count = lax.axis_size(DP)
    for axis, bit in ((TENSOR, 1), (TENSOR, 2), (DP, 1), (DP, 2), (DP, 4)):
        other = yield [(values, exchange(axis, bit))]
        values = values + other[0]
    lanes = values.shape[1] // count
    return lax.dynamic_slice_in_dim(values, lax.axis_index(DP) * lanes, lanes, 1)


def reduce_attention(groups, path, sizes):
    values = yield from reduce_group(groups, path)
    other = yield [(values, exchange(TENSOR, 2))]
    values = in_order(values, other[0], 2, 0)
    other = yield [(values, exchange(TENSOR, 1))]
    matrices = []
    begin = 0
    for size in sizes:
        end = begin + size // 2
        matrices.append(in_order(values[:, begin:end], other[0][:, begin:end], 1, 1).astype(FULL))
        begin = end
    return matrices


def in_order(values, other, bit, dim):
    first = lax.axis_index(TENSOR) // bit % 2 == 0
    return jnp.where(
        first,
        jnp.concatenate([values, other], dim),
        jnp.concatenate([other, values], dim),
    )


def reduce_far(parts):
    send, keep = parts
    other = yield [(send, exchange(TENSOR, 1))]
    values = keep + other[0]
    other = yield [(values[1], exchange(TENSOR, 2))]
    values = values[0] + other[0]
    values = values.reshape(-1, values.shape[-1])
    return lax.psum_scatter(values, DP, scatter_dimension=0, tiled=True).astype(FULL)


def reduce_whole(pairs):
    totals = []
    for left, right in pairs:
        total = lax.psum(dot_outer(left, right).astype(HALF), TENSOR)
        total = lax.psum_scatter(total, DP, scatter_dimension=0, tiled=True)
        totals.append(total.astype(FULL))
    return totals


class Flights:
    def __init__(self):
        self.running = {}
        self.results = {}
        self.asked = {}

    def start(self, name, steps):
        self.asked[name] = (steps, next(steps))

    def leave(self, values, names=None):
        asked = {name: self.asked.pop(name) for name in list(names or self.asked) if name in self.asked}
        sends = [[send for send, way in entry[1]] for entry in asked.values()]
        values, sends = lax.optimization_barrier((values, sends))
        for (name, (steps, entry)), ready in zip(asked.items(), sends):
            self.running[name] = (
                steps,
                [lax.ppermute(send, *way) for send, (unused, way) in zip(ready, entry)],
            )
        return values

    def land(self, names, values):
        names = [name for name in names if name in self.running]
        held = [self.running[name][1] for name in names]
        values, held = lax.optimization_barrier((values, held))
        for name, arrived in zip(names, held):
            steps = self.running.pop(name)[0]
            try:
                self.asked[name] = (steps, steps.send(arrived))
            except StopIteration as stop:
                self.results[name] = stop.value
        return values

    def turn(self, names, values):
        return self.leave(self.land(names, values), names)


def spread(pieces):
    return [pieces[0]] + [swap(piece, TENSOR, away) for away, piece in enumerate(pieces) if away]


def pass_on(values, way):
    arrived = yield [(values, way)]
    return arrived[0]


def both_matrices(hidden_up, hidden_down, layer, near):
    half = hidden_up.shape[1] // 2
    return jnp.stack(
        [
            lax.dynamic_slice_in_dim(matrices[layer], near * half, half, 0)
            for matrices in (hidden_up, hidden_down)
        ]
    )


def body(
    patch_tokens,
    class_tokens,
    frame_counts,
    patch_cotangent,
    class_cotangent,
    temporal_in,
    temporal_out,
    temporal_mix,
    spatial_in,
    spatial_out,
    hidden_up,
    hidden_down,
    norm_gain,
    norm_shift,
):
    frames, patches, width = patch_tokens.shape
    clips = class_tokens.shape[0]
    layers = temporal_in.shape[0]
    groups = lax.axis_size(TENSOR)
    place = jnp.stack([lax.axis_index(TENSOR), lax.axis_index(DP) % 2]).astype(jnp.int32)
    blocks_dp = lax.axis_size(DP)
    dims = (frames, patches, width, HEADS, groups)
    count = frames * patches
    rows = up_to(count + up_to(clips, 8), 80)
    spare = rows - count
    own_frames = frames // groups
    seq = groups * patches
    frame_span = up_to(seq + 1, 16)
    span = own_frames * frame_span
    hidden = groups * hidden_up.shape[2]
    piece_rows = own_frames * patches
    back_rows = up_to(piece_rows + 2 * own_frames, 16)

    ends = jnp.cumsum(frame_counts[0])
    frame_index = jnp.arange(frames, dtype=jnp.int32)
    clip_of = jnp.sum((frame_index[:, None] >= ends[None, :]).astype(jnp.int32), 1)
    clip_index = jnp.arange(spare, dtype=jnp.int32)
    member = (clip_index[:, None] == clip_of[None, :]).astype(FULL)
    counts = jnp.concatenate([frame_counts[0].astype(FULL), jnp.ones((spare - clips,), FULL)])
    share = member / counts[:, None]
    inverse_counts = 1.0 / counts
    row_index = jnp.arange(128, dtype=jnp.int32)
    row_clip = jnp.sum(
        jnp.where(row_index[:, None] % frames == frame_index[None, :], clip_of[None, :], 0), 1
    )
    same = jnp.logical_and(
        row_index[:, None] // frames == row_index[None, :] // frames,
        row_clip[:, None] == row_clip[None, :],
    )
    bias = jnp.where(same, 0.0, -1e30)

    def rows_of(patch, per_clip):
        return jnp.concatenate(
            [
                patch.reshape(count, width),
                per_clip,
                jnp.zeros((spare - clips, width), patch.dtype),
            ],
            0,
        ).astype(FULL)

    flights = Flights()
    near = lax.axis_index(DP) % 2
    gathered = [None] * layers
    by_core, by_x, by_y = exchange(TENSOR, 1), exchange(TENSOR, 2), exchange(DP, 1)

    def send(name, values, way):
        flights.start(name, pass_on(values, way))

    def arrived_here(name):
        return flights.results.pop(name)

    send("x0", both_matrices(hidden_up, hidden_down, 0, near), by_x)
    send("up", hidden_up, by_core)
    send("down", hidden_down, by_core)
    patch_rows = flights.leave(rows_of(patch_tokens, class_tokens))
    pieces_out = [((up_to(piece_rows, 16), width), HALF)] * groups
    backs_out = [((back_rows, width), HALF)] * groups
    lane_buffer = pltpu.VMEM((width // 128, rows, 128), FULL)
    row_buffer = pltpu.VMEM((rows, width), FULL)
    square = pltpu.VMEM((width, width), HALF)
    wide = pltpu.VMEM((width, 3 * width), HALF)
    shards = pltpu.VMEM((groups, width, width), HALF)
    blocks = pltpu.VMEM((groups, back_rows, width), FULL)
    frame_rows = pltpu.VMEM((frames, width), FULL)
    saved = []
    for layer in range(layers):
        time = call(
            partial(time_forward, dims, layer),
            [
                ((rows, width), HALF),
                ((rows, 3 * width), HALF),
                ((rows, 128), FULL),
                ((rows, width), HALF),
                ((rows, width), HALF),
                ((rows, width), FULL),
            ]
            + pieces_out
            + [((spare, width), FULL)],
            [wide, square, square, lane_buffer, row_buffer, blocks, pltpu.SemaphoreType.DMA((3,))],
            [SMALL, ROWS, ROWS, ROWS, ROWS, FAR, FAR, FAR],
            14,
        )(place, patch_rows, bias, norm_gain, norm_shift, temporal_in, temporal_out, temporal_mix)
        pieces = time[6:10]
        if layer:
            pieces = flights.land(["x1"], pieces)
            first = arrived_here("x1")
            send("y1", first, by_y)
            pieces = flights.leave(pieces)
        arrived = spread(pieces)
        if layer == 0:
            arrived = flights.land(("x0", "up", "down"), arrived)
            core_shards = (arrived_here("up"), arrived_here("down"))
            first = arrived_here("x0")
            send("y0", first, by_y)
            send("x1", both_matrices(hidden_up, hidden_down, 1, near), by_x)
        arrived = flights.leave(arrived)
        space = call(
            partial(space_forward, dims, layer),
            [((span, width), HALF), ((span, 3 * width), HALF), ((span, 128), FULL)] + backs_out,
            [wide, pltpu.VMEM((span, width), FULL), pltpu.SemaphoreType.DMA((1,))],
            [SMALL, SMALL, ROWS] + [ROWS] * groups + [FAR],
            9,
        )(place, clip_of, time[10], *arrived, spatial_in)
        arrived = spread(space[3:])
        arrived = flights.land([f"y{layer}"], arrived)
        second = arrived_here(f"y{layer}")
        send("first", first, by_core)
        send("second", second, by_core)
        arrived = flights.leave(arrived)
        arrived = flights.land(("first", "second"), arrived)
        gathered[layer] = (
            *core_shards,
            first,
            second,
            arrived_here("first"),
            arrived_here("second"),
        )
        feed = call(
            partial(feed_forward, dims, layer),
            [
                ((rows, width), HALF),
                ((rows, width), FULL),
                ((rows, width), HALF),
                ((rows, hidden), HALF),
                ((rows, hidden), HALF),
                ((rows, width), FULL),
            ],
            [
                square,
                shards,
                shards,
                row_buffer,
                blocks,
                frame_rows,
                pltpu.VMEM((rows, width), HALF),
                pltpu.SemaphoreType.DMA((1,)),
                pltpu.SemaphoreType.DMA((12,)),
            ],
            [SMALL] + [ROWS] * groups + [ROWS] * 4 + [FAR] * 9,
            15,
        )(
            place, *arrived, share, time[5], norm_gain, norm_shift, spatial_out,
            hidden_up, hidden_down, *gathered[layer],
        )
        saved.append((patch_rows, time, space, feed))
        patch_rows = feed[5]
    patch_output = patch_rows[:count].reshape(frames, patches, width).astype(HALF)
    class_output = patch_rows[count : count + clips].astype(HALF)

    grad_rows = rows_of(patch_cotangent, class_cotangent)
    usual = blocks_dp == 2 * NEAR
    norms = [None] * layers

    def outer(pairs, split, micros):
        return outer_group(place, pairs, groups, split, micros)

    def start(name, pairs, path, split, micros, first=()):
        pairs = tuple(pairs)
        if split and not usual:
            flights.results[name] = reduce_whole([pair for early in first for pair in early[0]] + list(pairs))
            return
        parts = [early[1] for early in first] + [outer(pairs, split, micros)]
        if split:
            sizes = []
            for own in [early[0] for early in first] + [pairs]:
                sizes.append([right.shape[1] for left, right in own])
            flights.start(name, reduce_attention(parts, path, sum(sizes, [])))
        elif usual:
            flights.start(name, reduce_group(parts, path))
        else:
            flights.start(name, reduce_far(parts[0]))

    for layer in reversed(range(layers)):
        start_rows, time, space, feed = saved[layer]
        last = layer == 0
        feed_back = call(
            partial(feed_backward, dims, layer),
            [
                ((rows, width), HALF),
                ((rows, hidden), HALF),
                ((rows, width), HALF),
                ((rows, width), FULL),
                ((8, width), FULL),
            ]
            + pieces_out
            + [((8, width), FULL)],
            [
                square,
                shards,
                shards,
                row_buffer,
                row_buffer,
                blocks,
                pltpu.SemaphoreType.DMA((1,)),
                pltpu.SemaphoreType.DMA((12,)),
            ],
            [SMALL, SMALL] + [ROWS] * 5 + [FAR] * 9,
            23,
        )(
            place, clip_of, grad_rows, feed[4], feed[1],
            jnp.broadcast_to(inverse_counts[:, None], (spare, 128)), norm_gain, spatial_out,
            hidden_up, hidden_down, *gathered[layer],
        )
        update, grad_hidden, branch, back, feed_norms = feed_back[:5]
        arrived = spread(feed_back[5:9])
        pairs = ((feed[2], grad_hidden), (update, feed[3]))
        if last:
            pairs = flights.turn(["feed1"], pairs)
            time_pairs = lax.optimization_barrier((time_pairs, pairs))[0]
            start("attention1", time_pairs, "both", True, 9, [early])
            pairs = flights.leave(pairs, ["attention1"])
            start("feed0", pairs, "both", False, 10)
            arrived, feed_sum = lax.optimization_barrier((arrived, feed_sum))
            feed_sum = lax.psum_scatter(feed_sum, DP, scatter_dimension=0, tiled=True)
            arrived = flights.turn(["feed1", "attention1"], arrived)
        else:
            total = outer_group(place, pairs, groups, False, 10, True)[0]
            arrived, total = lax.optimization_barrier((arrived, total))
            total = total.reshape(-1, total.shape[-1])
            feed_sum = lax.psum_scatter(total, TENSOR, scatter_dimension=0, tiled=True)
        arrived = flights.leave(arrived)
        space_back = call(
            partial(space_backward, dims, layer),
            [((span, 3 * width), HALF)] + backs_out,
            [
                wide,
                pltpu.VMEM((span, width), FULL),
                pltpu.VMEM((span, width), HALF),
                pltpu.SemaphoreType.DMA((1,)),
            ],
            [ROWS] * groups + [ROWS] * 3 + [FAR],
            29,
        )(*arrived, feed_back[9], space[1], space[2], spatial_in)
        pieces = space_back[1:]
        if last:
            pieces = flights.land(["feed1", "feed0"], pieces)
        arrived = spread(pieces)
        pairs = ((space[0], space_back[0]), (feed[0], branch))
        if last:
            start("space0", pairs, "xyuw", True, 8)
            arrived = flights.land(["attention1"], arrived)
            arrived = flights.leave(arrived)
        else:
            pairs = flights.turn(["feed1"], pairs)
            if usual:
                early = (pairs, outer(pairs, True, 8))
                arrived, parts = lax.optimization_barrier((arrived, early[1]))
                early = (pairs, parts)
            else:
                early = (pairs, None)
        time_back = call(
            partial(time_backward, dims, layer),
            [
                ((rows, width), HALF),
                ((rows, width), HALF),
                ((rows, 3 * width), HALF),
                ((rows, width), FULL),
                ((8, width), FULL),
            ],
            [
                wide,
                square,
                square,
                lane_buffer,
                row_buffer,
                blocks,
                frame_rows,
                pltpu.VMEM((rows, width), HALF),
                pltpu.SemaphoreType.DMA((3,)),
            ],
            [SMALL] + [ROWS] * groups + [ROWS] * 8 + [FAR] * 3,
            14,
        )(
            place, *arrived, member, back, time[5], start_rows, time[1], time[2], bias,
            norm_gain, temporal_in, temporal_out, temporal_mix,
        )
        grad_rows = time_back[3]
        norms[layer] = (time_back[4], feed_norms)
        pairs = ((time[0], time_back[2]), (time[3], time_back[1]), (time[4], time_back[0]))
        if last:
            ordered = [
                entry[at : at + 1]
                for part, at in ((0, 2), (0, 0), (1, 0), (0, 3), (0, 1), (1, 1))
                for entry in [norms[index][part] for index in range(layers)]
            ]
            ordered = jnp.concatenate(ordered, 0)
            if usual:
                flights.start("norms", reduce_norms(ordered))
            else:
                total = lax.psum(ordered, TENSOR)
                flights.results["norms"] = lax.psum_scatter(
                    total, DP, scatter_dimension=1, tiled=True
                )
            start("time0", pairs, "both", True, 9)
            token = grad_rows[count : count + clips]
            token = flights.leave(token, ["time0"])
            token, flights.results["feed1"] = lax.optimization_barrier((token, feed_sum))
        else:
            time_pairs = pairs
            grad_rows = flights.turn(["feed1"], grad_rows)
    for names in (
        ("attention1", "feed0", "space0"),
        ("attention1", "feed0", "time0", "norms"),
        ("space0", "time0", "norms"),
        ("attention1", "feed0"),
        ("space0", "time0", "norms"),
        ("attention1", "feed0"),
        ("space0", "time0", "norms"),
        ("attention1",),
        ("space0", "time0", "norms"),
        ("space0", "time0"),
    ):
        token = flights.turn(names, token)
    while flights.running:
        token = flights.turn(list(flights.running), token)
    results = flights.results
    lanes = width // blocks_dp

    norm_sums = results["norms"].reshape(2, 3, layers, lanes).transpose(0, 2, 1, 3)
    feeds = (results["feed0"], results["feed1"])
    late = results["attention1"]
    time_sums = (results["time0"], late[2:])
    space_sums = (results["space0"], late[:2])
    gradients = (
        *[jnp.stack([sums[index] for sums in time_sums]) for index in range(3)],
        *[jnp.stack([sums[index] for sums in space_sums]) for index in range(2)],
        jnp.stack([sums[:, :width].astype(FULL) for sums in feeds]),
        jnp.stack([sums[:, width:].T.astype(FULL) for sums in feeds]),
        norm_sums[0],
        norm_sums[1],
    )
    patch_grad = grad_rows[:count].reshape(frames, patches, width)
    class_grad = token
    return (patch_output, class_output, patch_grad, class_grad, *gradients)


def solution(mesh):
    placed = (
        P(DP, TENSOR, None),
        P(DP, None),
        P(DP, None),
        P(DP, TENSOR, None),
        P(DP, None),
        P(),
        P(),
        P(),
        P(),
        P(),
        P(None, None, TENSOR),
        P(None, TENSOR, None),
        P(),
        P(),
    )
    return jax.shard_map(
        body,
        mesh=mesh,
        in_specs=placed,
        out_specs=(
            P(DP, TENSOR, None),
            P(DP, None),
            P(DP, TENSOR, None),
            P(DP, None),
            P(None, DP, None),
            P(None, DP, None),
            P(None, DP, None),
            P(None, DP, None),
            P(None, DP, None),
            P(None, DP, TENSOR),
            P(None, TENSOR, DP),
            P(None, None, DP),
            P(None, None, DP),
        ),
        check_vma=False,
    )
```

```python
from functools import partial

import jax
import jax.numpy as jnp
from jax import lax
from jax.experimental import pallas as pl
from jax.experimental.pallas import tpu as pltpu
from jax.sharding import PartitionSpec as P

HEADS = 12
EPS = 1e-06
HIGH = lax.Precision.HIGHEST
HALF = jnp.bfloat16
FULL = jnp.float32
NEAR = 4
TENSOR = "tensor"
DP = "dp"
TILE = 256
VMEM_BYTES = 58 << 20
SMEM = pl.BlockSpec(memory_space=pltpu.SMEM)
SMALL, ROWS, FAR = range(3)
HBM = pl.BlockSpec(memory_space=pltpu.HBM)
ROOT_HALF = 0.5**0.5
DENSITY = (2.0 * 3.141592653589793) ** -0.5


def up_to(value, step):
    return -(-value // step) * step


def dot(left, right):
    return jnp.dot(left, right, preferred_element_type=FULL)


def dot_back(left, right):
    return lax.dot_general(left, right, (((1,), (1,)), ((), ())), preferred_element_type=FULL)


def dot_outer(left, right):
    return lax.dot_general(left, right, (((0,), (0,)), ((), ())), preferred_element_type=FULL)


def unit_of(values):
    centred = values - jnp.mean(values, -1, keepdims=True)
    inverse = lax.rsqrt(jnp.mean(centred * centred, -1, keepdims=True) + EPS)
    return centred * inverse, inverse


def unit_back(grad, unit, inverse, gain):
    scaled = grad * gain
    inner = (
        scaled
        - jnp.mean(scaled, -1, keepdims=True)
        - unit * jnp.mean(scaled * unit, -1, keepdims=True)
    )
    return inner * inverse


def head_lanes(head_size, half):
    lane = lax.broadcasted_iota(jnp.int32, (1, 2 * head_size), 1)
    return (lane // head_size) == half


def over_rows(rows, step, run):
    for start in range(0, rows, step):
        run(start, min(step, rows - start))


def two_heads(values, head_size):
    return jnp.concatenate(
        [jnp.where(head_lanes(head_size, half), values, 0) for half in range(2)], 0
    )


def one_of_two(values, head_size):
    rows = values.shape[0] // 2
    return jnp.where(head_lanes(head_size, 0), values[:rows], values[rows:])


def interleave(order, frame, frames, values):
    for group in range(order.shape[0]):
        part = values[:, group * 128 : (group + 1) * 128]
        order[group, pl.ds(frame, values.shape[0], stride=frames), :] = part


def pick(order, frame, frames, patches):
    own = pl.ds(frame, patches, stride=frames)
    return jnp.concatenate([order[group, own, :] for group in range(order.shape[0])], 1)


def shard_copies(place_ref, refs, target, which):
    own, core, far_first, far_second, core_first, core_second = refs
    half = far_first.shape[1]
    first = pl.multiple_of(place_ref[1] * half, half)
    second = pl.multiple_of((1 - place_ref[1]) * half, half)
    return [
        [(own, target.at[0])],
        [(core, target.at[1])],
        [
            (far_first.at[which], target.at[2, pl.ds(first, half)]),
            (far_second.at[which], target.at[2, pl.ds(second, half)]),
        ],
        [
            (core_first.at[which], target.at[3, pl.ds(first, half)]),
            (core_second.at[which], target.at[3, pl.ds(second, half)]),
        ],
    ]


def start_shards(place_ref, own, peers, up_ref, down_ref, sems):
    waits = []
    index = 0
    for pairs in zip(
        shard_copies(place_ref, own[:2] + peers, up_ref, 0),
        shard_copies(place_ref, own[2:] + peers, down_ref, 1),
    ):
        group = []
        for source, target in pairs[0] + pairs[1]:
            copy = pltpu.make_async_copy(source, target, sems.at[index])
            copy.start()
            group.append(copy)
            index += 1
        waits.append(group)
    return waits


def fetch(sources, targets, sems):
    copies = [
        pltpu.make_async_copy(source, target, sems.at[index])
        for index, (source, target) in enumerate(zip(sources, targets))
    ]
    for copy in copies:
        copy.start()
    return copies


def attend_forward(load, store, store_total, heads, head_size, bias):
    scale = head_size**-0.5
    totals = None
    if bias.shape[0] > 1:
        bias = jnp.concatenate([bias, bias], 0)
    for pair in range(heads // 2):
        query, key, value = (load(part, pair) for part in range(3))
        rows = query.shape[0]
        scores = dot_back(two_heads(query, head_size), key) * scale + bias
        top = jnp.max(scores, -1, keepdims=True)
        raised = jnp.exp(scores - top)
        total = jnp.sum(raised, -1, keepdims=True)
        mixed = dot(raised.astype(HALF), value) * (1.0 / total)
        log_total = top + jnp.log(total)
        if totals is None:
            lanes = lax.broadcasted_iota(jnp.int32, (rows, 128), 1)
            totals = jnp.zeros(lanes.shape, FULL)
        totals = jnp.where(lanes == pair * 2, log_total[:rows], totals)
        totals = jnp.where(lanes == pair * 2 + 1, log_total[rows:], totals)
        store(pair, one_of_two(mixed, head_size))
    store_total(totals)


def attend_backward(load, load_grad, totals, store, heads, head_size, bias):
    scale = head_size**-0.5
    totals = totals.T
    if bias.shape[1] > 1:
        bias = jnp.concatenate([bias, bias], 1)
    for pair in range(heads // 2):
        query, key, value = (load(part, pair) for part in range(3))
        query = two_heads(query, head_size)
        grad = two_heads(load_grad(pair), head_size)
        total = jnp.concatenate([totals[2 * pair + half : 2 * pair + half + 1] for half in range(2)], 1)
        prob = jnp.exp(dot_back(key, query) * scale + (bias - total))
        grad_prob = dot_back(value, grad)
        delta = jnp.sum(prob * grad_prob, 0, keepdims=True)
        grad_score = (prob * (grad_prob - delta)).astype(HALF)
        store(0, pair, one_of_two(dot_outer(grad_score, key), head_size) * scale)
        store(1, pair, dot(grad_score, query) * scale)
        store(2, pair, dot(prob.astype(HALF), grad))


def row_blocks(rows, step):
    return [(start, min(step, rows - start)) for start in range(0, rows, step)]


def time_forward(dims, layer, place_ref, x_ref, bias_ref, gain_ref, shift_ref, in_hbm, out_hbm, mix_hbm,
                 normed_ref, triple_ref, total_ref, mixed_ref, projected_ref, after_ref,
                 send0, send1, send2, send3, class_ref,
                 in_ref, out_ref, mix_ref, order, plain, blocks, sems):
    frames, patches, width, heads, groups = dims
    count = frames * patches
    rows = x_ref.shape[0]
    step = bias_ref.shape[0]
    copies = fetch(
        (in_hbm.at[layer], out_hbm.at[layer], mix_hbm.at[layer]), (in_ref, out_ref, mix_ref), sems
    )
    yield
    gain = gain_ref[layer, 0:1, :]
    shift = shift_ref[layer, 0:1, :]
    for frame in range(frames):
        unit, unused = unit_of(x_ref[frame * patches : (frame + 1) * patches, :])
        interleave(order, frame, frames, unit * gain + shift)
    for group in range(width // 128):
        order[group, count:, :] = jnp.zeros((rows - count, 128), FULL)
        normed_ref[:, group * 128 : (group + 1) * 128] = order[group].astype(HALF)
    normed_ref.flush()
    copies[0].wait()
    for column in range(0, 3 * width, TILE):
        part = slice(column, column + TILE)
        triple_ref[:, part] = dot(normed_ref[...], in_ref[:, part]).astype(HALF)
    triple_ref.flush()
    for begin, size in row_blocks(rows, step):
        own = slice(begin, begin + size)

        def load(part, pair):
            start = part * width + pair * 128
            return triple_ref[own, start : start + 128]

        def store(pair, mixed):
            order[pair, own, :] = mixed

        def store_total(totals):
            total_ref[own, :] = totals

        attend_forward(
            load, store, store_total, heads, width // heads, bias_ref[0:size, 0:size]
        )
    for frame in range(frames):
        plain[frame * patches : (frame + 1) * patches, :] = pick(order, frame, frames, patches)
    plain[count:, :] = jnp.zeros((rows - count, width), FULL)
    mixed_ref[...] = plain[...].astype(HALF)
    mixed_ref.flush()
    copies[1].wait()
    for column in range(0, width, TILE):
        part = slice(column, column + TILE)
        projected_ref[:, part] = dot(mixed_ref[...], out_ref[:, part]).astype(HALF)
    projected_ref.flush()
    copies[2].wait()
    for column in range(0, width, TILE):
        part = slice(column, column + TILE)
        after_ref[:, part] = x_ref[:, part] + dot(projected_ref[...], mix_ref[:, part])
    after_ref.flush()
    gain = gain_ref[layer, 1:2, :]
    shift = shift_ref[layer, 1:2, :]

    def norm(start, size):
        own = slice(start, start + size)
        unit, unused = unit_of(after_ref[own, :])
        plain[own, :] = unit * gain + shift

    over_rows(rows, 80, norm)
    send_blocks(plain, blocks, (send0, send1, send2, send3), place_ref[0], count // groups)
    class_ref[...] = plain[count:, :]


def send_blocks(plain, blocks, sends, place, size):
    groups = len(sends)
    rows = sends[0].shape[0]
    for group in range(groups):
        blocks[group, 0:size, :] = plain[group * size : (group + 1) * size, :]
        blocks[group, size:rows, :] = jnp.zeros((rows - size, plain.shape[1]), FULL)
    for away in range(groups):
        sends[away][...] = blocks[place ^ away][0:rows].astype(HALF)


def space_forward(dims, layer, place_ref, clip_ref, class_ref, piece0, piece1, piece2, piece3, in_hbm,
                  normed_ref, triple_ref, total_ref, send0, send1, send2, send3,
                  in_ref, plain, sems):
    frames, patches, width, heads, groups = dims
    own_frames = frames // groups
    seq = groups * patches
    rows = normed_ref.shape[0] // own_frames
    copies = fetch((in_hbm.at[layer],), (in_ref,), sems)
    yield
    pieces = [piece0, piece1, piece2, piece3]
    for away, piece in enumerate(pieces):
        values = piece[...].astype(FULL)
        for frame in range(own_frames):
            start = frame * rows + away * patches
            plain[start : start + patches, :] = values[frame * patches : (frame + 1) * patches]
    for frame in range(own_frames):
        start = frame * rows + seq
        plain[start : start + rows - seq, :] = jnp.zeros((rows - seq, width), FULL)
        clip = clip_ref[place_ref[0] * own_frames + frame]
        plain[start : start + 1, :] = class_ref[pl.ds(clip, 1), :]
    normed_ref[...] = plain[...].astype(HALF)
    normed_ref.flush()
    copies[0].wait()
    for column in range(0, 3 * width, TILE):
        part = slice(column, column + TILE)
        triple_ref[:, part] = dot(normed_ref[...], in_ref[:, part]).astype(HALF)
    triple_ref.flush()
    keys = lax.broadcasted_iota(jnp.int32, (1, rows), 1)
    bias = jnp.where(keys <= seq, 0.0, -1e30)

    for frame in range(own_frames):
        own = slice(frame * rows, (frame + 1) * rows)

        def load(part, pair):
            start = part * width + pair * 128
            return triple_ref[own, start : start + 128]

        def store(pair, mixed):
            plain[own, pair * 128 : (pair + 1) * 128] = mixed

        def store_total(totals):
            total_ref[own, :] = totals

        attend_forward(load, store, store_total, heads, width // heads, bias)
    return_pieces(plain, (send0, send1, send2, send3), own_frames, patches, rows)


def return_pieces(plain, sends, own_frames, patches, rows):
    seq = len(sends) * patches
    tail = []
    for frame in range(own_frames):
        row = plain[frame * rows + seq : frame * rows + seq + 1, :]
        high = row.astype(HALF).astype(FULL)
        tail += [high, row - high]
    size = own_frames * patches
    spare = sends[0].shape[0] - size - len(tail)
    tail.append(jnp.zeros((spare, plain.shape[1]), FULL))
    for away, send in enumerate(sends):
        kept = [
            plain[frame * rows + away * patches : frame * rows + (away + 1) * patches, :]
            for frame in range(own_frames)
        ]
        send[...] = jnp.concatenate(kept + tail, 0).astype(HALF)


def take_pieces(pieces, blocks, plain, frame_rows, place, size, own_frames):
    for away, piece in enumerate(pieces):
        blocks[place ^ away] = piece[...].astype(FULL)
    for group in range(len(pieces)):
        plain[group * size : (group + 1) * size, :] = blocks[group, 0:size, :]
        for frame in range(own_frames):
            start = size + 2 * frame
            frame_rows[group * own_frames + frame : group * own_frames + frame + 1, :] = (
                blocks[group, start : start + 1, :] + blocks[group, start + 1 : start + 2, :]
            )


def feed_forward(dims, layer, place_ref, piece0, piece1, piece2, piece3, share_ref, after_ref,
                 gain_ref, shift_ref, out_hbm,
                 up_hbm, down_hbm, peer_up, peer_down, peer2, peer3, peer4, peer5,
                 mixed_ref, rows_ref, normed_ref, active_ref, slope_ref, next_ref,
                 out_ref, up_ref, down_ref, plain, blocks, frame_rows, whole, out_sem, sems):
    frames, patches, width, heads, groups = dims
    count = frames * patches
    rows = after_ref.shape[0]
    size = count // groups
    place = place_ref[0]
    copies = fetch((out_hbm.at[layer],), (out_ref,), out_sem)
    own = (up_hbm.at[layer], peer_up.at[layer], down_hbm.at[layer], peer_down.at[layer])
    peers = (peer2, peer3, peer4, peer5)
    shards = start_shards(place_ref, own, peers, up_ref, down_ref, sems)
    yield
    take_pieces(
        (piece0, piece1, piece2, piece3), blocks, plain, frame_rows, place, size, frames // groups
    )
    plain[count:, :] = jnp.dot(
        share_ref[...], frame_rows[...], precision=HIGH, preferred_element_type=FULL
    )
    whole[...] = plain[...].astype(HALF)
    leader = jnp.where(place == 0, 1.0, 0.0).astype(FULL)
    kept = lax.broadcasted_iota(jnp.int32, (rows, 1), 0) < count
    kept = jnp.where(kept, 1.0, leader)
    mixed_ref[...] = (plain[...] * kept).astype(HALF)
    mixed_ref.flush()
    copies[0].wait()
    for column in range(0, width, TILE):
        part = slice(column, column + TILE)
        rows_ref[:, part] = after_ref[:, part] + dot(whole[...], out_ref[:, part])
    rows_ref.flush()
    gain = gain_ref[layer, 2:3, :]
    shift = shift_ref[layer, 2:3, :]

    def norm(start, size):
        own = slice(start, start + size)
        unit, unused = unit_of(rows_ref[own, :])
        plain[own, :] = unit * gain + shift

    over_rows(rows, 80, norm)
    whole[...] = plain[...].astype(HALF)
    normed_ref[...] = (plain[...] * kept).astype(HALF)
    normed_ref.flush()
    next_ref[...] = rows_ref[...]
    for away in range(groups):
        for copy in shards[away]:
            copy.wait()
        for column in range(0, width, TILE):
            part = slice(column, column + TILE)
            hidden = dot(whole[...], up_ref[away, :, part])
            below = 0.5 + 0.5 * lax.erf(hidden * ROOT_HALF)
            active = (hidden * below).astype(HALF)
            slope = below + hidden * (jnp.exp(hidden * hidden * -0.5) * DENSITY)
            start = away * width + column
            active_ref[:, start : start + TILE] = active
            slope_ref[:, start : start + TILE] = slope.astype(HALF)
        own = slice(away * width, (away + 1) * width)
        for column in range(0, width, TILE):
            part = slice(column, column + TILE)
            next_ref[:, part] += dot(active_ref[:, own], down_ref[away, :, part])
        end = count // 16 * 16
        active_ref[end:, own] = (active_ref[end:, own].astype(FULL) * kept[end:]).astype(HALF)
        active_ref.flush(own)
        slope_ref.flush(own)
    next_ref.flush()


def feed_backward(dims, layer, place_ref, clip_ref, grad_ref, slope_ref, rows_ref, share_ref, gain_ref,
                  out_hbm, up_hbm, down_hbm, peer_up, peer_down, peer2, peer3, peer4, peer5,
                  update_ref, hidden_ref, branch_ref, back_ref, norms_ref,
                  send0, send1, send2, send3, class_ref,
                  out_ref, up_ref, down_ref, total, plain, blocks, out_sem, sems):
    frames, patches, width, heads, groups = dims
    count = frames * patches
    rows = grad_ref.shape[0]
    place = place_ref[0]
    own_frames = frames // groups
    own = (up_hbm.at[layer], peer_up.at[layer], down_hbm.at[layer], peer_down.at[layer])
    peers = (peer2, peer3, peer4, peer5)
    shards = start_shards(place_ref, own, peers, up_ref, down_ref, sems)
    copies = fetch((out_hbm.at[layer],), (out_ref,), out_sem)
    yield
    update_ref[...] = grad_ref[...].astype(HALF)
    update_ref.flush()
    for away in range(groups):
        for copy in shards[away]:
            copy.wait()
        for column in range(0, width, TILE):
            part = slice(column, column + TILE)
            start = away * width + column
            grad_active = dot_back(update_ref[...], down_ref[away, part, :])
            slope = slope_ref[:, start : start + TILE].astype(FULL)
            grad_hidden = (grad_active * slope).astype(HALF)
            hidden_ref[:, start : start + TILE] = grad_hidden
        own = slice(away * width, (away + 1) * width)
        for column in range(0, width, TILE):
            part = slice(column, column + TILE)
            term = dot_back(hidden_ref[:, own], up_ref[away, part, :])
            if away == 0:
                total[:, part] = term
            else:
                total[:, part] += term
        hidden_ref.flush(own)
    gain = gain_ref[layer, 2:3, :]
    leader = jnp.where(place == 0, 1.0, 0.0).astype(FULL)
    norms_ref[...] = jnp.zeros(norms_ref.shape, FULL)
    def norm(start, size):
        own = slice(start, start + size)
        unit, inverse = unit_of(rows_ref[own, :])
        grad = total[own, :]
        back = grad_ref[own, :] + unit_back(grad, unit, inverse, gain)
        back_ref[own, :] = back
        branch_ref[own, :] = back.astype(HALF)
        kept = lax.broadcasted_iota(jnp.int32, (size, 1), 0) + start < count
        grad = jnp.where(kept, grad, grad * leader)
        norms_ref[0:1, :] += jnp.sum(grad * unit, 0, keepdims=True)
        norms_ref[1:2, :] += jnp.sum(grad, 0, keepdims=True)

    over_rows(rows, 80, norm)
    back_ref.flush()
    branch_ref.flush()
    copies[-1].wait()
    for column in range(0, width, TILE):
        part = slice(column, column + TILE)
        plain[:, part] = dot_back(branch_ref[...], out_ref[part, :])
    send_blocks(plain, blocks, (send0, send1, send2, send3), place, count // groups)
    for frame in range(own_frames):
        clip = clip_ref[place * own_frames + frame]
        class_ref[frame : frame + 1, :] = (
            plain[pl.ds(count + clip, 1), :] * share_ref[pl.ds(clip, 1), 0:1]
        )


def space_backward(dims, layer, piece0, piece1, piece2, piece3, class_ref, triple_ref, total_ref, in_hbm,
                   grad_ref, send0, send1, send2, send3,
                   in_ref, plain, mixed, sems):
    frames, patches, width, heads, groups = dims
    own_frames = frames // groups
    seq = groups * patches
    rows = triple_ref.shape[0] // own_frames
    copies = fetch((in_hbm.at[layer],), (in_ref,), sems)
    yield
    for away, piece in enumerate((piece0, piece1, piece2, piece3)):
        values = piece[...].astype(FULL)
        for frame in range(own_frames):
            start = frame * rows + away * patches
            plain[start : start + patches, :] = values[frame * patches : (frame + 1) * patches]
    for frame in range(own_frames):
        start = frame * rows + seq
        plain[start : start + rows - seq, :] = jnp.zeros((rows - seq, width), FULL)
        plain[start : start + 1, :] = class_ref[frame : frame + 1, :]
    mixed[...] = plain[...].astype(HALF)
    keys = lax.broadcasted_iota(jnp.int32, (rows, 1), 0)
    bias = jnp.where(keys <= seq, 0.0, -1e30)
    for frame in range(own_frames):
        own = slice(frame * rows, (frame + 1) * rows)

        def load(part, pair):
            start = part * width + pair * 128
            return triple_ref[own, start : start + 128]

        def load_grad(pair):
            return mixed[own, pair * 128 : (pair + 1) * 128]

        def store(part, pair, grad):
            start = part * width + pair * 128
            grad_ref[own, start : start + 128] = grad.astype(HALF)

        attend_backward(load, load_grad, total_ref[own, :], store, heads, width // heads, bias)
    grad_ref.flush()
    copies[0].wait()
    for column in range(0, width, TILE):
        part = slice(column, column + TILE)
        plain[:, part] = dot_back(grad_ref[...], in_ref[part, :])
    return_pieces(plain, (send0, send1, send2, send3), own_frames, patches, rows)


def time_backward(dims, layer, place_ref, piece0, piece1, piece2, piece3, member_ref, back_ref, after_ref, x_ref,
                  triple_ref, total_ref, bias_ref, gain_ref, in_hbm, out_hbm, mix_hbm,
                  branch_ref, projected_ref, grad_ref, next_ref, norms_ref,
                  in_ref, out_ref, mix_ref, order, plain, blocks, frame_rows, mixed, sems):
    frames, patches, width, heads, groups = dims
    count = frames * patches
    rows = x_ref.shape[0]
    step = bias_ref.shape[0]
    place = place_ref[0]
    copies = fetch(
        (mix_hbm.at[layer], out_hbm.at[layer], in_hbm.at[layer]), (mix_ref, out_ref, in_ref), sems
    )
    yield
    take_pieces(
        (piece0, piece1, piece2, piece3),
        blocks,
        plain,
        frame_rows,
        place,
        count // groups,
        frames // groups,
    )
    plain[count:, :] = jnp.dot(
        member_ref[...], frame_rows[...], precision=HIGH, preferred_element_type=FULL
    )
    leader = jnp.where(place == 0, 1.0, 0.0).astype(FULL)
    norms_ref[...] = jnp.zeros(norms_ref.shape, FULL)
    gain = gain_ref[layer, 1:2, :]

    def space_norm(start, size):
        own = slice(start, start + size)
        unit, inverse = unit_of(after_ref[own, :])
        grad = plain[own, :]
        back = back_ref[own, :] + unit_back(grad, unit, inverse, gain)
        next_ref[own, :] = back
        kept = lax.broadcasted_iota(jnp.int32, (size, 1), 0) + start < count
        branch_ref[own, :] = jnp.where(kept, back, 0.0).astype(HALF)
        grad = jnp.where(kept, grad, grad * leader)
        norms_ref[0:1, :] += jnp.sum(grad * unit, 0, keepdims=True)
        norms_ref[1:2, :] += jnp.sum(grad, 0, keepdims=True)

    over_rows(rows, 80, space_norm)
    branch_ref.flush()
    copies[0].wait()
    for column in range(0, width, TILE):
        part = slice(column, column + TILE)
        projected_ref[:, part] = dot_back(branch_ref[...], mix_ref[part, :]).astype(HALF)
    projected_ref.flush()
    copies[1].wait()
    for column in range(0, width, TILE):
        part = slice(column, column + TILE)
        plain[:, part] = dot_back(projected_ref[...], out_ref[part, :])
    for frame in range(frames):
        interleave(order, frame, frames, plain[frame * patches : (frame + 1) * patches, :])
    for group in range(width // 128):
        order[group, count:, :] = jnp.zeros((rows - count, 128), FULL)
        mixed[:, group * 128 : (group + 1) * 128] = order[group].astype(HALF)

    for begin, size in row_blocks(rows, step):
        own = slice(begin, begin + size)

        def load(part, pair):
            start = part * width + pair * 128
            return triple_ref[own, start : start + 128]

        def load_grad(pair):
            return mixed[own, pair * 128 : (pair + 1) * 128]

        def store(part, pair, grad):
            start = part * width + pair * 128
            grad_ref[own, start : start + 128] = grad.astype(HALF)

        attend_backward(
            load,
            load_grad,
            total_ref[own, :],
            store,
            heads,
            width // heads,
            bias_ref[0:size, 0:size],
        )
    grad_ref.flush()
    copies[2].wait()
    for column in range(0, width, TILE):
        part = slice(column, column + TILE)
        grad = dot_back(grad_ref[...], in_ref[part, :])
        for group in range(TILE // 128):
            order[column // 128 + group] = grad[:, group * 128 : (group + 1) * 128]
    gain = gain_ref[layer, 0:1, :]
    for frame in range(frames):
        own = slice(frame * patches, (frame + 1) * patches)
        grad = pick(order, frame, frames, patches)
        unit, inverse = unit_of(x_ref[own, :])
        next_ref[own, :] += unit_back(grad, unit, inverse, gain)
        norms_ref[2:3, :] += jnp.sum(grad * unit, 0, keepdims=True)
        norms_ref[3:4, :] += jnp.sum(grad, 0, keepdims=True)
    next_ref.flush()


def cost(micros):
    return pl.CostEstimate(flops=micros, bytes_accessed=micros, transcendentals=0)


class Fetched:
    def __init__(self, source, target, sem):
        self.target, self.shape = target, target.shape
        self.copy = pltpu.make_async_copy(source, target, sem)
        self.copy.start()

    def wait(self):
        if self.copy is not None:
            self.copy.wait()
            self.copy = None

    def __getitem__(self, index):
        self.wait()
        return self.target[index]


class Written:
    def __init__(self, source, target, sems):
        self.source, self.target, self.sems = source, target, sems
        self.shape = source.shape
        self.copies = []

    def __getitem__(self, index):
        return self.source[index]

    def __setitem__(self, index, values):
        self.source[index] = values

    def flush(self, columns=None):
        parts = (self.source, self.target)
        if columns is not None:
            parts = tuple(ref.at[:, columns] for ref in parts)
        copy = pltpu.make_async_copy(*parts, self.sems.at[len(self.copies)])
        copy.start()
        self.copies.append(copy)

    def wait(self):
        if not self.copies:
            self.flush()
        for copy in self.copies:
            copy.wait()


class Result:
    def __init__(self, index):
        self.index = index


def step_of(kernel, outs, scratch, specs, micros):
    return lambda *arrays: (kernel, outs, scratch, specs, micros, arrays)


def call(kernel, outs, scratch, specs, micros):
    return lambda *arrays: call_steps((kernel, outs, scratch, specs, micros, arrays))


def call_steps(*steps):
    outs = sum([list(step[1]) for step in steps], [])
    scratch = sum([list(step[2]) for step in steps], [])
    specs, arrays = [], []
    for step in steps:
        for kind, array in zip(step[3], step[5]):
            if not isinstance(array, Result):
                specs.append(kind)
                arrays.append(array)

    def kernel(*refs):
        ins = list(refs[: len(specs)])
        written = list(refs[len(specs) : len(specs) + len(outs)])
        rest = list(refs[len(specs) + len(outs) :])
        before = ()
        runs = []
        for unused, own_outs, own_scratch, unused, unused, own_arrays in steps:
            given = [before[a.index] if isinstance(a, Result) else ins.pop(0) for a in own_arrays]
            before = [written.pop(0) for out in own_outs]
            given += before + [rest.pop(0) for buffer in own_scratch]
            runs.append(given)
        runs = [step[0](*given) for step, given in zip(steps, runs)]
        for run in runs:
            next(run)
        for run in runs:
            for unused in run:
                pass

    results = call_arrays(kernel, outs, scratch, specs, sum(step[4] for step in steps))(*arrays)
    parts = []
    for step in steps:
        parts.append(results[: len(step[1])])
        results = results[len(step[1]) :]
    return parts[0] if len(steps) == 1 else parts


def call_arrays(kernel, outs, scratch, specs, micros):
    def run(*arrays):
        fetched = [index for index, kind in enumerate(specs) if kind == ROWS]
        count, results = len(specs), len(outs)

        def whole(*refs):
            ins, out_refs = list(refs[:count]), refs[count : count + results]
            rest = refs[count + results :]
            in_refs, rest = rest[: len(fetched)], rest[len(fetched) :]
            kept, rest = rest[:results], rest[results:]
            in_sems, out_sems = rest[0], rest[1]
            for place, index in enumerate(fetched):
                ins[index] = Fetched(ins[index], in_refs[place], in_sems.at[place])
            written = [
                Written(source, target, out_sems.at[index])
                for index, (source, target) in enumerate(zip(kept, out_refs))
            ]
            kernel(*ins, *written, *rest[2:])
            for index in fetched:
                ins[index].wait()
            for result in written:
                result.wait()

        return pl.pallas_call(
            whole,
            out_shape=[jax.ShapeDtypeStruct(shape, kind) for shape, kind in outs],
            in_specs=[SMEM if kind == SMALL else HBM for kind in specs],
            out_specs=[HBM] * results,
            scratch_shapes=[pltpu.VMEM(arrays[index].shape, arrays[index].dtype) for index in fetched]
            + [pltpu.VMEM(shape, kind) for shape, kind in outs]
            + [pltpu.SemaphoreType.DMA((len(fetched),)), pltpu.SemaphoreType.DMA((results, 4))]
            + scratch,
            compiler_params=pltpu.CompilerParams(vmem_limit_bytes=VMEM_BYTES),
            cost_estimate=cost(micros),
        )(*arrays)

    return run


def outer_group(place, pairs, groups, split, micros, whole=False):
    rows = pairs[0][0].shape[1]
    parts = 2 if split else groups
    inner = parts // 2
    sizes = [right.shape[1] // parts for left, right in pairs]
    total = sum(sizes)
    tiles = []
    for side in range(2):
        for index, size in enumerate(sizes):
            for shard in range(inner):
                for start in range(0, size, 768):
                    tiles.append((side, index, shard, start, min(768, size - start)))
    count = len(pairs)
    results = 1 if whole else 2

    def kernel(place_ref, *refs):
        lefts, rights = refs[:count], refs[count : 2 * count]
        outs = refs[2 * count : 2 * count + results]
        left_refs = refs[2 * count + results : 3 * count + results]
        right_refs, stage, left_sems, right_sems, out_sems = refs[3 * count + results :]
        arrivals = []
        lefts_here = []
        for number, (side, index, shard, start, size) in enumerate(tiles):
            if index == len(lefts_here):
                copy = pltpu.make_async_copy(lefts[index], left_refs[index], left_sems.at[index])
                copy.start()
                lefts_here.append(copy)
            if split:
                part = jnp.where(place_ref[0] % 2 == 0, 1 - side, side)
                begin = pl.multiple_of(part * sizes[index] + start, 128)
            else:
                begin = (2 * shard + 1 - side) * sizes[index] + start
            copy = pltpu.make_async_copy(
                rights[index].at[:, pl.ds(begin, size)],
                right_refs.at[number, pl.ds(0, rights[index].shape[0]), pl.ds(0, size)],
                right_sems.at[number],
            )
            copy.start()
            arrivals.append(copy)
        leaving = []
        waited = [False] * count
        for number, (side, index, shard, start, size) in enumerate(tiles):
            if not waited[index]:
                lefts_here[index].wait()
                waited[index] = True
            arrivals[number].wait()
            depth = lefts[index].shape[0]
            terms = dot_outer(left_refs[index][...], right_refs[number, 0:depth, 0:size])
            stage[number, :, 0:size] = terms.astype(HALF)
            column = sum(sizes[:index]) + start
            if whole:
                target = outs[0].at[(2 * shard + 1 - side) ^ place_ref[0]]
            else:
                target = outs[side] if split else outs[side].at[shard]
            copy = pltpu.make_async_copy(
                stage.at[number, :, pl.ds(0, size)],
                target.at[:, pl.ds(column, size)],
                out_sems.at[number],
            )
            copy.start()
            leaving.append(copy)
        for copy in leaving:
            copy.wait()

    shape = (rows, total) if split else (groups if whole else inner, rows, total)
    lefts, rights = zip(*pairs)
    width = max(tile[4] for tile in tiles)
    return pl.pallas_call(
        kernel,
        out_shape=[jax.ShapeDtypeStruct(shape, HALF)] * results,
        in_specs=[SMEM] + [HBM] * (2 * count),
        out_specs=[HBM] * results,
        scratch_shapes=[pltpu.VMEM(left.shape, HALF) for left in lefts]
        + [
            pltpu.VMEM((len(tiles), max(left.shape[0] for left in lefts), width), HALF),
            pltpu.VMEM((len(tiles), rows, width), HALF),
            pltpu.SemaphoreType.DMA((count,)),
            pltpu.SemaphoreType.DMA((len(tiles),)),
            pltpu.SemaphoreType.DMA((len(tiles),)),
        ],
        compiler_params=pltpu.CompilerParams(vmem_limit_bytes=VMEM_BYTES),
        cost_estimate=cost(micros),
    )(place, *lefts, *rights)


def exchange(axis, bit):
    return (axis, [(index, index ^ bit) for index in range(lax.axis_size(axis))])


def swap(values, axis, bit):
    return lax.ppermute(values, *exchange(axis, bit))


def reduce_group(groups, path):
    others = yield [(send, exchange(TENSOR, 1)) for send, keep in groups]
    sums = [keep + other for (send, keep), other in zip(groups, others)]
    values = sums[0] if len(sums) == 1 else jnp.concatenate(sums, -1)
    columns = values.shape[-1]
    blocks = lax.axis_size(DP)
    far = blocks // 2
    place = lax.axis_index(DP)
    bits = {"x": lax.axis_index(TENSOR) // 2, "y": place % 2, "u": place // 2 % 2, "w": place // 4}
    ways = {
        "x": exchange(TENSOR, 2),
        "y": exchange(DP, 1),
        "u": exchange(DP, 2),
        "w": exchange(DP, 4),
    }
    if values.ndim == 3:
        values = values.reshape(2, 2, 2, 2, -1, columns)
        dims = "xwuy"
        bits["x"] = 0
    else:
        values = values.reshape(2, 2, 2, 2, -1, columns)
        dims = "wuyx"

    def side(array, left, axis, mine):
        bit = bits[axis] if mine else 1 - bits[axis]
        return lax.dynamic_index_in_dim(array, bit, left.index(axis), False)

    if path == "both":
        middle = columns // 2 // 128 * 128
        tracks = [[values[..., :middle], "xy"], [values[..., middle:], "yx"]]
        left = [dims, dims]
        for step in range(2):
            others = yield [
                (side(array, rest, way[step], False), ways[way[step]])
                for (array, way), rest in zip(tracks, left)
            ]
            tracks = [
                [side(array, rest, way[step], True) + other, way]
                for (array, way), rest, other in zip(tracks, left, others)
            ]
            left = [rest.replace(way[step], "") for (array, way), rest in zip(tracks, left)]
        values = jnp.concatenate([array for array, way in tracks], -1)
        dims = left[0]
        path = "uw"
    for axis in path:
        other = yield [(side(values, dims, axis, False), ways[axis])]
        values = side(values, dims, axis, True) + other[0]
        dims = dims.replace(axis, "")
    return values


def reduce_norms(values):
    count = lax.axis_size(DP)
    for axis, bit in ((TENSOR, 1), (TENSOR, 2), (DP, 1), (DP, 2), (DP, 4)):
        other = yield [(values, exchange(axis, bit))]
        values = values + other[0]
    lanes = values.shape[1] // count
    return lax.dynamic_slice_in_dim(values, lax.axis_index(DP) * lanes, lanes, 1)


def reduce_attention(groups, path, sizes):
    values = yield from reduce_group(groups, path)
    other = yield [(values, exchange(TENSOR, 2))]
    values = in_order(values, other[0], 2, 0)
    other = yield [(values, exchange(TENSOR, 1))]
    matrices = []
    begin = 0
    for size in sizes:
        end = begin + size // 2
        matrices.append(in_order(values[:, begin:end], other[0][:, begin:end], 1, 1).astype(FULL))
        begin = end
    return matrices


def in_order(values, other, bit, dim):
    first = lax.axis_index(TENSOR) // bit % 2 == 0
    return jnp.where(
        first,
        jnp.concatenate([values, other], dim),
        jnp.concatenate([other, values], dim),
    )


def reduce_far(parts):
    send, keep = parts
    other = yield [(send, exchange(TENSOR, 1))]
    values = keep + other[0]
    other = yield [(values[1], exchange(TENSOR, 2))]
    values = values[0] + other[0]
    values = values.reshape(-1, values.shape[-1])
    return lax.psum_scatter(values, DP, scatter_dimension=0, tiled=True).astype(FULL)


def reduce_whole(pairs):
    totals = []
    for left, right in pairs:
        total = lax.psum(dot_outer(left, right).astype(HALF), TENSOR)
        total = lax.psum_scatter(total, DP, scatter_dimension=0, tiled=True)
        totals.append(total.astype(FULL))
    return totals


class Flights:
    def __init__(self):
        self.running = {}
        self.results = {}
        self.asked = {}

    def start(self, name, steps):
        self.asked[name] = (steps, next(steps))

    def leave(self, values, names=None):
        asked = {name: self.asked.pop(name) for name in list(names or self.asked) if name in self.asked}
        sends = [[send for send, way in entry[1]] for entry in asked.values()]
        values, sends = lax.optimization_barrier((values, sends))
        for (name, (steps, entry)), ready in zip(asked.items(), sends):
            self.running[name] = (
                steps,
                [lax.ppermute(send, *way) for send, (unused, way) in zip(ready, entry)],
            )
        return values

    def land(self, names, values):
        names = [name for name in names if name in self.running]
        held = [self.running[name][1] for name in names]
        values, held = lax.optimization_barrier((values, held))
        for name, arrived in zip(names, held):
            steps = self.running.pop(name)[0]
            try:
                self.asked[name] = (steps, steps.send(arrived))
            except StopIteration as stop:
                self.results[name] = stop.value
        return values

    def turn(self, names, values):
        return self.leave(self.land(names, values), names)


def spread(pieces):
    return [pieces[0]] + [swap(piece, TENSOR, away) for away, piece in enumerate(pieces) if away]


def pass_on(values, way):
    arrived = yield [(values, way)]
    return arrived[0]


def both_matrices(hidden_up, hidden_down, layer, near):
    half = hidden_up.shape[1] // 2
    return jnp.stack(
        [
            lax.dynamic_slice_in_dim(matrices[layer], near * half, half, 0)
            for matrices in (hidden_up, hidden_down)
        ]
    )


def body(
    patch_tokens,
    class_tokens,
    frame_counts,
    patch_cotangent,
    class_cotangent,
    temporal_in,
    temporal_out,
    temporal_mix,
    spatial_in,
    spatial_out,
    hidden_up,
    hidden_down,
    norm_gain,
    norm_shift,
):
    frames, patches, width = patch_tokens.shape
    clips = class_tokens.shape[0]
    layers = temporal_in.shape[0]
    groups = lax.axis_size(TENSOR)
    place = jnp.stack([lax.axis_index(TENSOR), lax.axis_index(DP) % 2]).astype(jnp.int32)
    blocks_dp = lax.axis_size(DP)
    dims = (frames, patches, width, HEADS, groups)
    count = frames * patches
    rows = up_to(count + up_to(clips, 8), 80)
    spare = rows - count
    own_frames = frames // groups
    seq = groups * patches
    frame_span = up_to(seq + 1, 16)
    span = own_frames * frame_span
    hidden = groups * hidden_up.shape[2]
    piece_rows = own_frames * patches
    back_rows = up_to(piece_rows + 2 * own_frames, 16)

    ends = jnp.cumsum(frame_counts[0])
    frame_index = jnp.arange(frames, dtype=jnp.int32)
    clip_of = jnp.sum((frame_index[:, None] >= ends[None, :]).astype(jnp.int32), 1)
    clip_index = jnp.arange(spare, dtype=jnp.int32)
    member = (clip_index[:, None] == clip_of[None, :]).astype(FULL)
    counts = jnp.concatenate([frame_counts[0].astype(FULL), jnp.ones((spare - clips,), FULL)])
    share = member / counts[:, None]
    inverse_counts = 1.0 / counts
    row_index = jnp.arange(128, dtype=jnp.int32)
    row_clip = jnp.sum(
        jnp.where(row_index[:, None] % frames == frame_index[None, :], clip_of[None, :], 0), 1
    )
    same = jnp.logical_and(
        row_index[:, None] // frames == row_index[None, :] // frames,
        row_clip[:, None] == row_clip[None, :],
    )
    bias = jnp.where(same, 0.0, -1e30)

    def rows_of(patch, per_clip):
        return jnp.concatenate(
            [
                patch.reshape(count, width),
                per_clip,
                jnp.zeros((spare - clips, width), patch.dtype),
            ],
            0,
        ).astype(FULL)

    flights = Flights()
    near = lax.axis_index(DP) % 2
    gathered = [None] * layers
    by_core, by_x, by_y = exchange(TENSOR, 1), exchange(TENSOR, 2), exchange(DP, 1)

    def send(name, values, way):
        flights.start(name, pass_on(values, way))

    def arrived_here(name):
        return flights.results.pop(name)

    send("x0", both_matrices(hidden_up, hidden_down, 0, near), by_x)
    send("up", hidden_up, by_core)
    send("down", hidden_down, by_core)
    patch_rows = flights.leave(rows_of(patch_tokens, class_tokens))
    pieces_out = [((up_to(piece_rows, 16), width), HALF)] * groups
    backs_out = [((back_rows, width), HALF)] * groups
    lane_buffer = pltpu.VMEM((width // 128, rows, 128), FULL)
    row_buffer = pltpu.VMEM((rows, width), FULL)
    square = pltpu.VMEM((width, width), HALF)
    wide = pltpu.VMEM((width, 3 * width), HALF)
    shards = pltpu.VMEM((groups, width, width), HALF)
    blocks = pltpu.VMEM((groups, back_rows, width), FULL)
    frame_rows = pltpu.VMEM((frames, width), FULL)
    def time_step(layer, patch_rows):
        return step_of(
            partial(time_forward, dims, layer),
            [
                ((rows, width), HALF),
                ((rows, 3 * width), HALF),
                ((rows, 128), FULL),
                ((rows, width), HALF),
                ((rows, width), HALF),
                ((rows, width), FULL),
            ]
            + pieces_out
            + [((spare, width), FULL)],
            [wide, square, square, lane_buffer, row_buffer, blocks, pltpu.SemaphoreType.DMA((3,))],
            [SMALL, ROWS, ROWS, ROWS, ROWS, FAR, FAR, FAR],
            14,
        )(place, patch_rows, bias, norm_gain, norm_shift, temporal_in, temporal_out, temporal_mix)

    def feed_step(layer, arrived, after):
        return step_of(
            partial(feed_forward, dims, layer),
            [
                ((rows, width), HALF),
                ((rows, width), FULL),
                ((rows, width), HALF),
                ((rows, hidden), HALF),
                ((rows, hidden), HALF),
                ((rows, width), FULL),
            ],
            [
                square,
                shards,
                shards,
                row_buffer,
                blocks,
                frame_rows,
                pltpu.VMEM((rows, width), HALF),
                pltpu.SemaphoreType.DMA((1,)),
                pltpu.SemaphoreType.DMA((12,)),
            ],
            [SMALL] + [ROWS] * groups + [ROWS] * 4 + [FAR] * 9,
            15,
        )(
            place, *arrived, share, after, norm_gain, norm_shift, spatial_out,
            hidden_up, hidden_down, *gathered[layer],
        )

    def feed_back_step(layer, grad_rows, slope, rows_in):
        return step_of(
            partial(feed_backward, dims, layer),
            [
                ((rows, width), HALF),
                ((rows, hidden), HALF),
                ((rows, width), HALF),
                ((rows, width), FULL),
                ((8, width), FULL),
            ]
            + pieces_out
            + [((8, width), FULL)],
            [
                square,
                shards,
                shards,
                row_buffer,
                row_buffer,
                blocks,
                pltpu.SemaphoreType.DMA((1,)),
                pltpu.SemaphoreType.DMA((12,)),
            ],
            [SMALL, SMALL] + [ROWS] * 5 + [FAR] * 9,
            23,
        )(
            place, clip_of, grad_rows, slope, rows_in,
            jnp.broadcast_to(inverse_counts[:, None], (spare, 128)), norm_gain, spatial_out,
            hidden_up, hidden_down, *gathered[layer],
        )

    def time_back_step(layer, arrived, back, time, start_rows):
        return step_of(
            partial(time_backward, dims, layer),
            [
                ((rows, width), HALF),
                ((rows, width), HALF),
                ((rows, 3 * width), HALF),
                ((rows, width), FULL),
                ((8, width), FULL),
            ],
            [
                wide,
                square,
                square,
                lane_buffer,
                row_buffer,
                blocks,
                frame_rows,
                pltpu.VMEM((rows, width), HALF),
                pltpu.SemaphoreType.DMA((3,)),
            ],
            [SMALL] + [ROWS] * groups + [ROWS] * 8 + [FAR] * 3,
            14,
        )(
            place, *arrived, member, back, time[5], start_rows, time[1], time[2], bias,
            norm_gain, temporal_in, temporal_out, temporal_mix,
        )

    saved = []
    grad_rows = rows_of(patch_cotangent, class_cotangent)
    time = call_steps(time_step(0, patch_rows))
    for layer in range(layers):
        pieces = time[6:10]
        if layer:
            pieces = flights.land(["x1"], pieces)
            first = arrived_here("x1")
            send("y1", first, by_y)
            pieces = flights.leave(pieces)
        arrived = spread(pieces)
        if layer == 0:
            arrived = flights.land(("x0", "up", "down"), arrived)
            core_shards = (arrived_here("up"), arrived_here("down"))
            first = arrived_here("x0")
            send("y0", first, by_y)
            send("x1", both_matrices(hidden_up, hidden_down, 1, near), by_x)
        arrived = flights.leave(arrived)
        space = call(
            partial(space_forward, dims, layer),
            [((span, width), HALF), ((span, 3 * width), HALF), ((span, 128), FULL)] + backs_out,
            [wide, pltpu.VMEM((span, width), FULL), pltpu.SemaphoreType.DMA((1,))],
            [SMALL, SMALL, ROWS] + [ROWS] * groups + [FAR],
            9,
        )(place, clip_of, time[10], *arrived, spatial_in)
        arrived = spread(space[3:])
        arrived = flights.land([f"y{layer}"], arrived)
        second = arrived_here(f"y{layer}")
        send("first", first, by_core)
        send("second", second, by_core)
        arrived = flights.leave(arrived)
        arrived = flights.land(("first", "second"), arrived)
        gathered[layer] = (
            *core_shards,
            first,
            second,
            arrived_here("first"),
            arrived_here("second"),
        )
        step = feed_step(layer, arrived, time[5])
        if layer + 1 < layers:
            feed, later = call_steps(step, time_step(layer + 1, Result(5)))
        else:
            feed, later = call_steps(
                step, feed_back_step(layer, grad_rows, Result(4), Result(1))
            )
        saved.append((patch_rows, time, space, feed))
        patch_rows = feed[5]
        time = later
    feed_back = later
    patch_output = patch_rows[:count].reshape(frames, patches, width).astype(HALF)
    class_output = patch_rows[count : count + clips].astype(HALF)

    usual = blocks_dp == 2 * NEAR
    norms = [None] * layers

    def outer(pairs, split, micros):
        return outer_group(place, pairs, groups, split, micros)

    def start(name, pairs, path, split, micros, first=()):
        pairs = tuple(pairs)
        if split and not usual:
            flights.results[name] = reduce_whole([pair for early in first for pair in early[0]] + list(pairs))
            return
        parts = [early[1] for early in first] + [outer(pairs, split, micros)]
        if split:
            sizes = []
            for own in [early[0] for early in first] + [pairs]:
                sizes.append([right.shape[1] for left, right in own])
            flights.start(name, reduce_attention(parts, path, sum(sizes, [])))
        elif usual:
            flights.start(name, reduce_group(parts, path))
        else:
            flights.start(name, reduce_far(parts[0]))

    for layer in reversed(range(layers)):
        start_rows, time, space, feed = saved[layer]
        last = layer == 0
        update, grad_hidden, branch, back, feed_norms = feed_back[:5]
        arrived = spread(feed_back[5:9])
        pairs = ((feed[2], grad_hidden), (update, feed[3]))
        if last:
            pairs = flights.turn(["feed1"], pairs)
            time_pairs = lax.optimization_barrier((time_pairs, pairs))[0]
            start("attention1", time_pairs, "both", True, 9, [early])
            pairs = flights.leave(pairs, ["attention1"])
            start("feed0", pairs, "both", False, 10)
            arrived, feed_sum = lax.optimization_barrier((arrived, feed_sum))
            feed_sum = lax.psum_scatter(feed_sum, DP, scatter_dimension=0, tiled=True)
            arrived = flights.turn(["feed1", "attention1"], arrived)
        else:
            total = outer_group(place, pairs, groups, False, 10, True)[0]
            arrived, total = lax.optimization_barrier((arrived, total))
            total = total.reshape(-1, total.shape[-1])
            feed_sum = lax.psum_scatter(total, TENSOR, scatter_dimension=0, tiled=True)
        arrived = flights.leave(arrived)
        space_back = call(
            partial(space_backward, dims, layer),
            [((span, 3 * width), HALF)] + backs_out,
            [
                wide,
                pltpu.VMEM((span, width), FULL),
                pltpu.VMEM((span, width), HALF),
                pltpu.SemaphoreType.DMA((1,)),
            ],
            [ROWS] * groups + [ROWS] * 3 + [FAR],
            29,
        )(*arrived, feed_back[9], space[1], space[2], spatial_in)
        pieces = space_back[1:]
        if last:
            pieces = flights.land(["feed1", "feed0"], pieces)
        arrived = spread(pieces)
        pairs = ((space[0], space_back[0]), (feed[0], branch))
        if last:
            start("space0", pairs, "xyuw", True, 8)
            arrived = flights.land(["attention1"], arrived)
            arrived = flights.leave(arrived)
        else:
            pairs = flights.turn(["feed1"], pairs)
            if usual:
                early = (pairs, outer(pairs, True, 8))
                arrived, parts = lax.optimization_barrier((arrived, early[1]))
                early = (pairs, parts)
            else:
                early = (pairs, None)
        step = time_back_step(layer, arrived, back, time, start_rows)
        if last:
            time_back = call_steps(step)
        else:
            ahead = saved[layer - 1][3]
            time_back, later = call_steps(
                step, feed_back_step(layer - 1, Result(3), ahead[4], ahead[1])
            )
        grad_rows = time_back[3]
        norms[layer] = (time_back[4], feed_norms)
        pairs = ((time[0], time_back[2]), (time[3], time_back[1]), (time[4], time_back[0]))
        if last:
            ordered = [
                entry[at : at + 1]
                for part, at in ((0, 2), (0, 0), (1, 0), (0, 3), (0, 1), (1, 1))
                for entry in [norms[index][part] for index in range(layers)]
            ]
            ordered = jnp.concatenate(ordered, 0)
            if usual:
                flights.start("norms", reduce_norms(ordered))
            else:
                total = lax.psum(ordered, TENSOR)
                flights.results["norms"] = lax.psum_scatter(
                    total, DP, scatter_dimension=1, tiled=True
                )
            start("time0", pairs, "both", True, 9)
            token = grad_rows[count : count + clips]
            token = flights.leave(token, ["time0"])
            token, flights.results["feed1"] = lax.optimization_barrier((token, feed_sum))
        else:
            time_pairs = pairs
            feed_back = later
    for names in (
        ("attention1", "feed0", "space0"),
        ("attention1", "feed0", "time0", "norms"),
        ("space0", "time0", "norms"),
        ("attention1", "feed0"),
        ("space0", "time0", "norms"),
        ("attention1", "feed0"),
        ("space0", "time0", "norms"),
        ("attention1",),
        ("space0", "time0", "norms"),
        ("space0", "time0"),
    ):
        token = flights.turn(names, token)
    while flights.running:
        token = flights.turn(list(flights.running), token)
    results = flights.results
    lanes = width // blocks_dp

    norm_sums = results["norms"].reshape(2, 3, layers, lanes).transpose(0, 2, 1, 3)
    feeds = (results["feed0"], results["feed1"])
    late = results["attention1"]
    time_sums = (results["time0"], late[2:])
    space_sums = (results["space0"], late[:2])
    gradients = (
        *[jnp.stack([sums[index] for sums in time_sums]) for index in range(3)],
        *[jnp.stack([sums[index] for sums in space_sums]) for index in range(2)],
        jnp.stack([sums[:, :width].astype(FULL) for sums in feeds]),
        jnp.stack([sums[:, width:].T.astype(FULL) for sums in feeds]),
        norm_sums[0],
        norm_sums[1],
    )
    patch_grad = grad_rows[:count].reshape(frames, patches, width)
    class_grad = token
    return (patch_output, class_output, patch_grad, class_grad, *gradients)


def solution(mesh):
    placed = (
        P(DP, TENSOR, None),
        P(DP, None),
        P(DP, None),
        P(DP, TENSOR, None),
        P(DP, None),
        P(),
        P(),
        P(),
        P(),
        P(),
        P(None, None, TENSOR),
        P(None, TENSOR, None),
        P(),
        P(),
    )
    return jax.shard_map(
        body,
        mesh=mesh,
        in_specs=placed,
        out_specs=(
            P(DP, TENSOR, None),
            P(DP, None),
            P(DP, TENSOR, None),
            P(DP, None),
            P(None, DP, None),
            P(None, DP, None),
            P(None, DP, None),
            P(None, DP, None),
            P(None, DP, None),
            P(None, DP, TENSOR),
            P(None, TENSOR, DP),
            P(None, None, DP),
            P(None, None, DP),
        ),
        check_vma=False,
    )
```

```python
from functools import partial

import jax
import jax.numpy as jnp
from jax import lax
from jax.experimental import pallas as pl
from jax.experimental.pallas import tpu as pltpu
from jax.sharding import PartitionSpec as P

HEADS = 12
EPS = 1e-06
HIGH = lax.Precision.HIGHEST
HALF = jnp.bfloat16
FULL = jnp.float32
NEAR = 4
TENSOR = "tensor"
DP = "dp"
TILE = 256
VMEM_BYTES = 58 << 20
SMEM = pl.BlockSpec(memory_space=pltpu.SMEM)
SMALL, ROWS, FAR = range(3)
HBM = pl.BlockSpec(memory_space=pltpu.HBM)
ROOT_HALF = 0.5**0.5
DENSITY = (2.0 * 3.141592653589793) ** -0.5


def up_to(value, step):
    return -(-value // step) * step


def dot(left, right):
    return jnp.dot(left, right, preferred_element_type=FULL)


def dot_back(left, right):
    return lax.dot_general(left, right, (((1,), (1,)), ((), ())), preferred_element_type=FULL)


def dot_outer(left, right):
    return lax.dot_general(left, right, (((0,), (0,)), ((), ())), preferred_element_type=FULL)


def unit_of(values):
    centred = values - jnp.mean(values, -1, keepdims=True)
    inverse = lax.rsqrt(jnp.mean(centred * centred, -1, keepdims=True) + EPS)
    return centred * inverse, inverse


def unit_back(grad, unit, inverse, gain):
    scaled = grad * gain
    inner = (
        scaled
        - jnp.mean(scaled, -1, keepdims=True)
        - unit * jnp.mean(scaled * unit, -1, keepdims=True)
    )
    return inner * inverse


def head_lanes(head_size, half):
    lane = lax.broadcasted_iota(jnp.int32, (1, 2 * head_size), 1)
    return (lane // head_size) == half


def over_rows(rows, step, run):
    for start in range(0, rows, step):
        run(start, min(step, rows - start))


def two_heads(values, head_size):
    return jnp.concatenate(
        [jnp.where(head_lanes(head_size, half), values, 0) for half in range(2)], 0
    )


def one_of_two(values, head_size):
    rows = values.shape[0] // 2
    return jnp.where(head_lanes(head_size, 0), values[:rows], values[rows:])


def interleave(order, frame, frames, values):
    for group in range(order.shape[0]):
        part = values[:, group * 128 : (group + 1) * 128]
        order[group, pl.ds(frame, values.shape[0], stride=frames), :] = part


def pick(order, frame, frames, patches):
    own = pl.ds(frame, patches, stride=frames)
    return jnp.concatenate([order[group, own, :] for group in range(order.shape[0])], 1)


def shard_copies(place_ref, refs, target, which):
    own, core, far_first, far_second, core_first, core_second = refs
    half = far_first.shape[1]
    first = pl.multiple_of(place_ref[1] * half, half)
    second = pl.multiple_of((1 - place_ref[1]) * half, half)
    return [
        [(own, target.at[0])],
        [(core, target.at[1])],
        [
            (far_first.at[which], target.at[2, pl.ds(first, half)]),
            (far_second.at[which], target.at[2, pl.ds(second, half)]),
        ],
        [
            (core_first.at[which], target.at[3, pl.ds(first, half)]),
            (core_second.at[which], target.at[3, pl.ds(second, half)]),
        ],
    ]


def start_shards(place_ref, own, peers, up_ref, down_ref, sems):
    waits = []
    index = 0
    for pairs in zip(
        shard_copies(place_ref, own[:2] + peers, up_ref, 0),
        shard_copies(place_ref, own[2:] + peers, down_ref, 1),
    ):
        group = []
        for source, target in pairs[0] + pairs[1]:
            copy = pltpu.make_async_copy(source, target, sems.at[index])
            copy.start()
            group.append(copy)
            index += 1
        waits.append(group)
    return waits


def fetch(sources, targets, sems):
    copies = [
        pltpu.make_async_copy(source, target, sems.at[index])
        for index, (source, target) in enumerate(zip(sources, targets))
    ]
    for copy in copies:
        copy.start()
    return copies


def attend_forward(load, store, store_total, heads, head_size, bias):
    scale = head_size**-0.5
    totals = None
    if bias.shape[0] > 1:
        bias = jnp.concatenate([bias, bias], 0)
    for pair in range(heads // 2):
        query, key, value = (load(part, pair) for part in range(3))
        rows = query.shape[0]
        scores = dot_back(two_heads(query, head_size), key) * scale + bias
        top = jnp.max(scores, -1, keepdims=True)
        raised = jnp.exp(scores - top)
        total = jnp.sum(raised, -1, keepdims=True)
        mixed = dot(raised.astype(HALF), value) * (1.0 / total)
        log_total = top + jnp.log(total)
        if totals is None:
            lanes = lax.broadcasted_iota(jnp.int32, (rows, 128), 1)
            totals = jnp.zeros(lanes.shape, FULL)
        totals = jnp.where(lanes == pair * 2, log_total[:rows], totals)
        totals = jnp.where(lanes == pair * 2 + 1, log_total[rows:], totals)
        store(pair, one_of_two(mixed, head_size))
    store_total(totals)


def attend_backward(load, load_grad, totals, store, heads, head_size, bias):
    scale = head_size**-0.5
    totals = totals.T
    if bias.shape[1] > 1:
        bias = jnp.concatenate([bias, bias], 1)
    for pair in range(heads // 2):
        query, key, value = (load(part, pair) for part in range(3))
        query = two_heads(query, head_size)
        grad = two_heads(load_grad(pair), head_size)
        total = jnp.concatenate([totals[2 * pair + half : 2 * pair + half + 1] for half in range(2)], 1)
        prob = jnp.exp(dot_back(key, query) * scale + (bias - total))
        grad_prob = dot_back(value, grad)
        delta = jnp.sum(prob * grad_prob, 0, keepdims=True)
        grad_score = (prob * (grad_prob - delta)).astype(HALF)
        store(0, pair, one_of_two(dot_outer(grad_score, key), head_size) * scale)
        store(1, pair, dot(grad_score, query) * scale)
        store(2, pair, dot(prob.astype(HALF), grad))


def row_blocks(rows, step):
    return [(start, min(step, rows - start)) for start in range(0, rows, step)]


def time_forward(dims, layer, place_ref, x_ref, bias_ref, gain_ref, shift_ref, in_hbm, out_hbm, mix_hbm,
                 normed_ref, triple_ref, total_ref, mixed_ref, projected_ref, after_ref,
                 send0, send1, send2, send3, class_ref,
                 in_ref, out_ref, mix_ref, order, plain, blocks, sems):
    frames, patches, width, heads, groups = dims
    count = frames * patches
    rows = x_ref.shape[0]
    step = bias_ref.shape[0]
    copies = fetch(
        (in_hbm.at[layer], out_hbm.at[layer], mix_hbm.at[layer]), (in_ref, out_ref, mix_ref), sems
    )
    yield
    gain = gain_ref[layer, 0:1, :]
    shift = shift_ref[layer, 0:1, :]
    for frame in range(frames):
        unit, unused = unit_of(x_ref[frame * patches : (frame + 1) * patches, :])
        interleave(order, frame, frames, unit * gain + shift)
    for group in range(width // 128):
        order[group, count:, :] = jnp.zeros((rows - count, 128), FULL)
        normed_ref[:, group * 128 : (group + 1) * 128] = order[group].astype(HALF)
    normed_ref.flush()
    copies[0].wait()
    for column in range(0, 3 * width, TILE):
        part = slice(column, column + TILE)
        triple_ref[:, part] = dot(normed_ref[...], in_ref[:, part]).astype(HALF)
    triple_ref.flush()
    for begin, size in row_blocks(rows, step):
        own = slice(begin, begin + size)

        def load(part, pair):
            start = part * width + pair * 128
            return triple_ref[own, start : start + 128]

        def store(pair, mixed):
            order[pair, own, :] = mixed

        def store_total(totals):
            total_ref[own, :] = totals

        attend_forward(
            load, store, store_total, heads, width // heads, bias_ref[0:size, 0:size]
        )
    for frame in range(frames):
        plain[frame * patches : (frame + 1) * patches, :] = pick(order, frame, frames, patches)
    plain[count:, :] = jnp.zeros((rows - count, width), FULL)
    mixed_ref[...] = plain[...].astype(HALF)
    mixed_ref.flush()
    copies[1].wait()
    for column in range(0, width, TILE):
        part = slice(column, column + TILE)
        projected_ref[:, part] = dot(mixed_ref[...], out_ref[:, part]).astype(HALF)
    projected_ref.flush()
    copies[2].wait()
    for column in range(0, width, TILE):
        part = slice(column, column + TILE)
        after_ref[:, part] = x_ref[:, part] + dot(projected_ref[...], mix_ref[:, part])
    after_ref.flush()
    gain = gain_ref[layer, 1:2, :]
    shift = shift_ref[layer, 1:2, :]

    def norm(start, size):
        own = slice(start, start + size)
        unit, unused = unit_of(after_ref[own, :])
        plain[own, :] = unit * gain + shift

    over_rows(rows, 80, norm)
    send_blocks(plain, blocks, (send0, send1, send2, send3), place_ref[0], count // groups)
    class_ref[...] = plain[count:, :]


def send_blocks(plain, blocks, sends, place, size):
    groups = len(sends)
    rows = sends[0].shape[0]
    for group in range(groups):
        blocks[group, 0:size, :] = plain[group * size : (group + 1) * size, :]
        blocks[group, size:rows, :] = jnp.zeros((rows - size, plain.shape[1]), FULL)
    for away in range(groups):
        sends[away][...] = blocks[place ^ away][0:rows].astype(HALF)


def space_forward(dims, layer, place_ref, clip_ref, class_ref, piece0, piece1, piece2, piece3, in_hbm,
                  normed_ref, triple_ref, total_ref, send0, send1, send2, send3,
                  in_ref, plain, sems):
    frames, patches, width, heads, groups = dims
    own_frames = frames // groups
    seq = groups * patches
    rows = normed_ref.shape[0] // own_frames
    copies = fetch((in_hbm.at[layer],), (in_ref,), sems)
    yield
    pieces = [piece0, piece1, piece2, piece3]
    for away, piece in enumerate(pieces):
        values = piece[...].astype(FULL)
        for frame in range(own_frames):
            start = frame * rows + away * patches
            plain[start : start + patches, :] = values[frame * patches : (frame + 1) * patches]
    for frame in range(own_frames):
        start = frame * rows + seq
        plain[start : start + rows - seq, :] = jnp.zeros((rows - seq, width), FULL)
        clip = clip_ref[place_ref[0] * own_frames + frame]
        plain[start : start + 1, :] = class_ref[pl.ds(clip, 1), :]
    normed_ref[...] = plain[...].astype(HALF)
    normed_ref.flush()
    copies[0].wait()
    for column in range(0, 3 * width, TILE):
        part = slice(column, column + TILE)
        triple_ref[:, part] = dot(normed_ref[...], in_ref[:, part]).astype(HALF)
    triple_ref.flush()
    keys = lax.broadcasted_iota(jnp.int32, (1, rows), 1)
    bias = jnp.where(keys <= seq, 0.0, -1e30)

    for frame in range(own_frames):
        own = slice(frame * rows, (frame + 1) * rows)

        def load(part, pair):
            start = part * width + pair * 128
            return triple_ref[own, start : start + 128]

        def store(pair, mixed):
            plain[own, pair * 128 : (pair + 1) * 128] = mixed

        def store_total(totals):
            total_ref[own, :] = totals

        attend_forward(load, store, store_total, heads, width // heads, bias)
    return_pieces(plain, (send0, send1, send2, send3), own_frames, patches, rows)


def return_pieces(plain, sends, own_frames, patches, rows):
    seq = len(sends) * patches
    tail = []
    for frame in range(own_frames):
        row = plain[frame * rows + seq : frame * rows + seq + 1, :]
        high = row.astype(HALF).astype(FULL)
        tail += [high, row - high]
    size = own_frames * patches
    spare = sends[0].shape[0] - size - len(tail)
    tail.append(jnp.zeros((spare, plain.shape[1]), FULL))
    for away, send in enumerate(sends):
        kept = [
            plain[frame * rows + away * patches : frame * rows + (away + 1) * patches, :]
            for frame in range(own_frames)
        ]
        send[...] = jnp.concatenate(kept + tail, 0).astype(HALF)


def take_pieces(pieces, blocks, plain, frame_rows, place, size, own_frames):
    for away, piece in enumerate(pieces):
        blocks[place ^ away] = piece[...].astype(FULL)
    for group in range(len(pieces)):
        plain[group * size : (group + 1) * size, :] = blocks[group, 0:size, :]
        for frame in range(own_frames):
            start = size + 2 * frame
            frame_rows[group * own_frames + frame : group * own_frames + frame + 1, :] = (
                blocks[group, start : start + 1, :] + blocks[group, start + 1 : start + 2, :]
            )


def feed_forward(dims, layer, place_ref, piece0, piece1, piece2, piece3, share_ref, after_ref,
                 gain_ref, shift_ref, out_hbm,
                 up_hbm, down_hbm, peer_up, peer_down, peer2, peer3, peer4, peer5,
                 mixed_ref, rows_ref, normed_ref, active_ref, slope_ref, next_ref,
                 out_ref, up_ref, down_ref, plain, blocks, frame_rows, whole, out_sem, sems):
    frames, patches, width, heads, groups = dims
    count = frames * patches
    rows = after_ref.shape[0]
    size = count // groups
    place = place_ref[0]
    copies = fetch((out_hbm.at[layer],), (out_ref,), out_sem)
    own = (up_hbm.at[layer], peer_up.at[layer], down_hbm.at[layer], peer_down.at[layer])
    peers = (peer2, peer3, peer4, peer5)
    shards = start_shards(place_ref, own, peers, up_ref, down_ref, sems)
    yield
    take_pieces(
        (piece0, piece1, piece2, piece3), blocks, plain, frame_rows, place, size, frames // groups
    )
    plain[count:, :] = jnp.dot(
        share_ref[...], frame_rows[...], precision=HIGH, preferred_element_type=FULL
    )
    whole[...] = plain[...].astype(HALF)
    leader = jnp.where(place == 0, 1.0, 0.0).astype(FULL)
    kept = lax.broadcasted_iota(jnp.int32, (rows, 1), 0) < count
    kept = jnp.where(kept, 1.0, leader)
    mixed_ref[...] = (plain[...] * kept).astype(HALF)
    mixed_ref.flush()
    copies[0].wait()
    for column in range(0, width, TILE):
        part = slice(column, column + TILE)
        rows_ref[:, part] = after_ref[:, part] + dot(whole[...], out_ref[:, part])
    rows_ref.flush()
    gain = gain_ref[layer, 2:3, :]
    shift = shift_ref[layer, 2:3, :]

    def norm(start, size):
        own = slice(start, start + size)
        unit, unused = unit_of(rows_ref[own, :])
        plain[own, :] = unit * gain + shift

    over_rows(rows, 80, norm)
    whole[...] = plain[...].astype(HALF)
    normed_ref[...] = (plain[...] * kept).astype(HALF)
    normed_ref.flush()
    next_ref[...] = rows_ref[...]
    for away in range(groups):
        for copy in shards[away]:
            copy.wait()
        for column in range(0, width, TILE):
            part = slice(column, column + TILE)
            hidden = dot(whole[...], up_ref[away, :, part])
            below = 0.5 + 0.5 * lax.erf(hidden * ROOT_HALF)
            active = (hidden * below).astype(HALF)
            slope = below + hidden * (jnp.exp(hidden * hidden * -0.5) * DENSITY)
            start = away * width + column
            active_ref[:, start : start + TILE] = active
            slope_ref[:, start : start + TILE] = slope.astype(HALF)
        own = slice(away * width, (away + 1) * width)
        for column in range(0, width, TILE):
            part = slice(column, column + TILE)
            next_ref[:, part] += dot(active_ref[:, own], down_ref[away, :, part])
        end = count // 16 * 16
        active_ref[end:, own] = (active_ref[end:, own].astype(FULL) * kept[end:]).astype(HALF)
        active_ref.flush(own)
        slope_ref.flush(own)
    next_ref.flush()


def feed_backward(dims, layer, place_ref, clip_ref, grad_ref, slope_ref, rows_ref, share_ref, gain_ref,
                  out_hbm, up_hbm, down_hbm, peer_up, peer_down, peer2, peer3, peer4, peer5,
                  update_ref, hidden_ref, branch_ref, back_ref, norms_ref,
                  send0, send1, send2, send3, class_ref,
                  out_ref, up_ref, down_ref, total, plain, blocks, out_sem, sems):
    frames, patches, width, heads, groups = dims
    count = frames * patches
    rows = grad_ref.shape[0]
    place = place_ref[0]
    own_frames = frames // groups
    own = (up_hbm.at[layer], peer_up.at[layer], down_hbm.at[layer], peer_down.at[layer])
    peers = (peer2, peer3, peer4, peer5)
    shards = start_shards(place_ref, own, peers, up_ref, down_ref, sems)
    copies = fetch((out_hbm.at[layer],), (out_ref,), out_sem)
    yield
    update_ref[...] = grad_ref[...].astype(HALF)
    update_ref.flush()
    for away in range(groups):
        for copy in shards[away]:
            copy.wait()
        for column in range(0, width, TILE):
            part = slice(column, column + TILE)
            start = away * width + column
            grad_active = dot_back(update_ref[...], down_ref[away, part, :])
            slope = slope_ref[:, start : start + TILE].astype(FULL)
            grad_hidden = (grad_active * slope).astype(HALF)
            hidden_ref[:, start : start + TILE] = grad_hidden
        own = slice(away * width, (away + 1) * width)
        for column in range(0, width, TILE):
            part = slice(column, column + TILE)
            term = dot_back(hidden_ref[:, own], up_ref[away, part, :])
            if away == 0:
                total[:, part] = term
            else:
                total[:, part] += term
        hidden_ref.flush(own)
    gain = gain_ref[layer, 2:3, :]
    leader = jnp.where(place == 0, 1.0, 0.0).astype(FULL)
    norms_ref[...] = jnp.zeros(norms_ref.shape, FULL)
    def norm(start, size):
        own = slice(start, start + size)
        unit, inverse = unit_of(rows_ref[own, :])
        grad = total[own, :]
        back = grad_ref[own, :] + unit_back(grad, unit, inverse, gain)
        back_ref[own, :] = back
        branch_ref[own, :] = back.astype(HALF)
        kept = lax.broadcasted_iota(jnp.int32, (size, 1), 0) + start < count
        grad = jnp.where(kept, grad, grad * leader)
        norms_ref[0:1, :] += jnp.sum(grad * unit, 0, keepdims=True)
        norms_ref[1:2, :] += jnp.sum(grad, 0, keepdims=True)

    over_rows(rows, 80, norm)
    back_ref.flush()
    branch_ref.flush()
    copies[-1].wait()
    for column in range(0, width, TILE):
        part = slice(column, column + TILE)
        plain[:, part] = dot_back(branch_ref[...], out_ref[part, :])
    send_blocks(plain, blocks, (send0, send1, send2, send3), place, count // groups)
    for frame in range(own_frames):
        clip = clip_ref[place * own_frames + frame]
        class_ref[frame : frame + 1, :] = (
            plain[pl.ds(count + clip, 1), :] * share_ref[pl.ds(clip, 1), 0:1]
        )


def space_backward(dims, layer, piece0, piece1, piece2, piece3, class_ref, triple_ref, total_ref, in_hbm,
                   grad_ref, send0, send1, send2, send3,
                   in_ref, plain, mixed, sems):
    frames, patches, width, heads, groups = dims
    own_frames = frames // groups
    seq = groups * patches
    rows = triple_ref.shape[0] // own_frames
    copies = fetch((in_hbm.at[layer],), (in_ref,), sems)
    yield
    for away, piece in enumerate((piece0, piece1, piece2, piece3)):
        values = piece[...].astype(FULL)
        for frame in range(own_frames):
            start = frame * rows + away * patches
            plain[start : start + patches, :] = values[frame * patches : (frame + 1) * patches]
    for frame in range(own_frames):
        start = frame * rows + seq
        plain[start : start + rows - seq, :] = jnp.zeros((rows - seq, width), FULL)
        plain[start : start + 1, :] = class_ref[frame : frame + 1, :]
    mixed[...] = plain[...].astype(HALF)
    keys = lax.broadcasted_iota(jnp.int32, (rows, 1), 0)
    bias = jnp.where(keys <= seq, 0.0, -1e30)
    for frame in range(own_frames):
        own = slice(frame * rows, (frame + 1) * rows)

        def load(part, pair):
            start = part * width + pair * 128
            return triple_ref[own, start : start + 128]

        def load_grad(pair):
            return mixed[own, pair * 128 : (pair + 1) * 128]

        def store(part, pair, grad):
            start = part * width + pair * 128
            grad_ref[own, start : start + 128] = grad.astype(HALF)

        attend_backward(load, load_grad, total_ref[own, :], store, heads, width // heads, bias)
    grad_ref.flush()
    copies[0].wait()
    for column in range(0, width, TILE):
        part = slice(column, column + TILE)
        plain[:, part] = dot_back(grad_ref[...], in_ref[part, :])
    return_pieces(plain, (send0, send1, send2, send3), own_frames, patches, rows)


def time_backward(dims, layer, place_ref, piece0, piece1, piece2, piece3, member_ref, back_ref, after_ref, x_ref,
                  triple_ref, total_ref, bias_ref, gain_ref, in_hbm, out_hbm, mix_hbm,
                  branch_ref, projected_ref, grad_ref, next_ref, norms_ref,
                  in_ref, out_ref, mix_ref, order, plain, blocks, frame_rows, mixed, sems):
    frames, patches, width, heads, groups = dims
    count = frames * patches
    rows = x_ref.shape[0]
    step = bias_ref.shape[0]
    place = place_ref[0]
    copies = fetch(
        (mix_hbm.at[layer], out_hbm.at[layer], in_hbm.at[layer]), (mix_ref, out_ref, in_ref), sems
    )
    yield
    take_pieces(
        (piece0, piece1, piece2, piece3),
        blocks,
        plain,
        frame_rows,
        place,
        count // groups,
        frames // groups,
    )
    plain[count:, :] = jnp.dot(
        member_ref[...], frame_rows[...], precision=HIGH, preferred_element_type=FULL
    )
    leader = jnp.where(place == 0, 1.0, 0.0).astype(FULL)
    norms_ref[...] = jnp.zeros(norms_ref.shape, FULL)
    gain = gain_ref[layer, 1:2, :]

    def space_norm(start, size):
        own = slice(start, start + size)
        unit, inverse = unit_of(after_ref[own, :])
        grad = plain[own, :]
        back = back_ref[own, :] + unit_back(grad, unit, inverse, gain)
        next_ref[own, :] = back
        kept = lax.broadcasted_iota(jnp.int32, (size, 1), 0) + start < count
        branch_ref[own, :] = jnp.where(kept, back, 0.0).astype(HALF)
        grad = jnp.where(kept, grad, grad * leader)
        norms_ref[0:1, :] += jnp.sum(grad * unit, 0, keepdims=True)
        norms_ref[1:2, :] += jnp.sum(grad, 0, keepdims=True)

    over_rows(rows, 80, space_norm)
    branch_ref.flush()
    copies[0].wait()
    for column in range(0, width, TILE):
        part = slice(column, column + TILE)
        projected_ref[:, part] = dot_back(branch_ref[...], mix_ref[part, :]).astype(HALF)
    projected_ref.flush()
    copies[1].wait()
    for column in range(0, width, TILE):
        part = slice(column, column + TILE)
        plain[:, part] = dot_back(projected_ref[...], out_ref[part, :])
    for frame in range(frames):
        interleave(order, frame, frames, plain[frame * patches : (frame + 1) * patches, :])
    for group in range(width // 128):
        order[group, count:, :] = jnp.zeros((rows - count, 128), FULL)
        mixed[:, group * 128 : (group + 1) * 128] = order[group].astype(HALF)

    for begin, size in row_blocks(rows, step):
        own = slice(begin, begin + size)

        def load(part, pair):
            start = part * width + pair * 128
            return triple_ref[own, start : start + 128]

        def load_grad(pair):
            return mixed[own, pair * 128 : (pair + 1) * 128]

        def store(part, pair, grad):
            start = part * width + pair * 128
            grad_ref[own, start : start + 128] = grad.astype(HALF)

        attend_backward(
            load,
            load_grad,
            total_ref[own, :],
            store,
            heads,
            width // heads,
            bias_ref[0:size, 0:size],
        )
    grad_ref.flush()
    copies[2].wait()
    for column in range(0, width, TILE):
        part = slice(column, column + TILE)
        grad = dot_back(grad_ref[...], in_ref[part, :])
        for group in range(TILE // 128):
            order[column // 128 + group] = grad[:, group * 128 : (group + 1) * 128]
    gain = gain_ref[layer, 0:1, :]
    for frame in range(frames):
        own = slice(frame * patches, (frame + 1) * patches)
        grad = pick(order, frame, frames, patches)
        unit, inverse = unit_of(x_ref[own, :])
        next_ref[own, :] += unit_back(grad, unit, inverse, gain)
        norms_ref[2:3, :] += jnp.sum(grad * unit, 0, keepdims=True)
        norms_ref[3:4, :] += jnp.sum(grad, 0, keepdims=True)
    next_ref.flush()


def cost(micros):
    return pl.CostEstimate(flops=micros, bytes_accessed=micros, transcendentals=0)


class Fetched:
    def __init__(self, source, target, sem):
        self.target, self.shape = target, target.shape
        self.copy = pltpu.make_async_copy(source, target, sem)
        self.copy.start()

    def wait(self):
        if self.copy is not None:
            self.copy.wait()
            self.copy = None

    def __getitem__(self, index):
        self.wait()
        return self.target[index]


class Written:
    def __init__(self, source, target, sems):
        self.source, self.target, self.sems = source, target, sems
        self.shape = source.shape
        self.copies = []

    def __getitem__(self, index):
        return self.source[index]

    def __setitem__(self, index, values):
        self.source[index] = values

    def flush(self, columns=None):
        parts = (self.source, self.target)
        if columns is not None:
            parts = tuple(ref.at[:, columns] for ref in parts)
        copy = pltpu.make_async_copy(*parts, self.sems.at[len(self.copies)])
        copy.start()
        self.copies.append(copy)

    def wait(self):
        if not self.copies:
            self.flush()
        for copy in self.copies:
            copy.wait()


class Result:
    def __init__(self, index):
        self.index = index


def step_of(kernel, outs, scratch, specs, micros):
    return lambda *arrays: (kernel, outs, scratch, specs, micros, arrays)


def call(kernel, outs, scratch, specs, micros):
    return lambda *arrays: call_steps((kernel, outs, scratch, specs, micros, arrays))


def call_steps(*steps):
    outs = sum([list(step[1]) for step in steps], [])
    scratch = sum([list(step[2]) for step in steps], [])
    specs, arrays = [], []
    for step in steps:
        for kind, array in zip(step[3], step[5]):
            if not isinstance(array, Result):
                specs.append(kind)
                arrays.append(array)

    def kernel(*refs):
        ins = list(refs[: len(specs)])
        written = list(refs[len(specs) : len(specs) + len(outs)])
        rest = list(refs[len(specs) + len(outs) :])
        before = ()
        runs = []
        for unused, own_outs, own_scratch, unused, unused, own_arrays in steps:
            given = [before[a.index] if isinstance(a, Result) else ins.pop(0) for a in own_arrays]
            before = [written.pop(0) for out in own_outs]
            given += before + [rest.pop(0) for buffer in own_scratch]
            runs.append(given)
        runs = [step[0](*given) for step, given in zip(steps, runs)]
        for run in runs:
            next(run)
        for run in runs:
            for unused in run:
                pass

    results = call_arrays(kernel, outs, scratch, specs, sum(step[4] for step in steps))(*arrays)
    parts = []
    for step in steps:
        parts.append(results[: len(step[1])])
        results = results[len(step[1]) :]
    return parts[0] if len(steps) == 1 else parts


def call_arrays(kernel, outs, scratch, specs, micros):
    def run(*arrays):
        fetched = [index for index, kind in enumerate(specs) if kind == ROWS]
        count, results = len(specs), len(outs)

        def whole(*refs):
            ins, out_refs = list(refs[:count]), refs[count : count + results]
            rest = refs[count + results :]
            in_refs, rest = rest[: len(fetched)], rest[len(fetched) :]
            kept, rest = rest[:results], rest[results:]
            in_sems, out_sems = rest[0], rest[1]
            for place, index in enumerate(fetched):
                ins[index] = Fetched(ins[index], in_refs[place], in_sems.at[place])
            written = [
                Written(source, target, out_sems.at[index])
                for index, (source, target) in enumerate(zip(kept, out_refs))
            ]
            kernel(*ins, *written, *rest[2:])
            for index in fetched:
                ins[index].wait()
            for result in written:
                result.wait()

        return pl.pallas_call(
            whole,
            out_shape=[jax.ShapeDtypeStruct(shape, kind) for shape, kind in outs],
            in_specs=[SMEM if kind == SMALL else HBM for kind in specs],
            out_specs=[HBM] * results,
            scratch_shapes=[pltpu.VMEM(arrays[index].shape, arrays[index].dtype) for index in fetched]
            + [pltpu.VMEM(shape, kind) for shape, kind in outs]
            + [pltpu.SemaphoreType.DMA((len(fetched),)), pltpu.SemaphoreType.DMA((results, 4))]
            + scratch,
            compiler_params=pltpu.CompilerParams(vmem_limit_bytes=VMEM_BYTES),
            cost_estimate=cost(micros),
        )(*arrays)

    return run


def outer_group(place, pairs, groups, split, micros, whole=False):
    rows = pairs[0][0].shape[1]
    parts = 2 if split else groups
    inner = parts // 2
    sizes = [right.shape[1] // parts for left, right in pairs]
    total = sum(sizes)
    tiles = []
    for side in range(2):
        for index, size in enumerate(sizes):
            for shard in range(inner):
                for start in range(0, size, 768):
                    tiles.append((side, index, shard, start, min(768, size - start)))
    count = len(pairs)
    results = 1 if whole else 2

    def kernel(place_ref, *refs):
        lefts, rights = refs[:count], refs[count : 2 * count]
        outs = refs[2 * count : 2 * count + results]
        left_refs = refs[2 * count + results : 3 * count + results]
        right_refs, stage, left_sems, right_sems, out_sems = refs[3 * count + results :]
        arrivals = []
        lefts_here = []
        for number, (side, index, shard, start, size) in enumerate(tiles):
            if index == len(lefts_here):
                copy = pltpu.make_async_copy(lefts[index], left_refs[index], left_sems.at[index])
                copy.start()
                lefts_here.append(copy)
            if split:
                part = jnp.where(place_ref[0] % 2 == 0, 1 - side, side)
                begin = pl.multiple_of(part * sizes[index] + start, 128)
            else:
                begin = (2 * shard + 1 - side) * sizes[index] + start
            copy = pltpu.make_async_copy(
                rights[index].at[:, pl.ds(begin, size)],
                right_refs.at[number, pl.ds(0, rights[index].shape[0]), pl.ds(0, size)],
                right_sems.at[number],
            )
            copy.start()
            arrivals.append(copy)
        leaving = []
        waited = [False] * count
        for number, (side, index, shard, start, size) in enumerate(tiles):
            if not waited[index]:
                lefts_here[index].wait()
                waited[index] = True
            arrivals[number].wait()
            depth = lefts[index].shape[0]
            terms = dot_outer(left_refs[index][...], right_refs[number, 0:depth, 0:size])
            stage[number, :, 0:size] = terms.astype(HALF)
            column = sum(sizes[:index]) + start
            if whole:
                target = outs[0].at[(2 * shard + 1 - side) ^ place_ref[0]]
            else:
                target = outs[side] if split else outs[side].at[shard]
            copy = pltpu.make_async_copy(
                stage.at[number, :, pl.ds(0, size)],
                target.at[:, pl.ds(column, size)],
                out_sems.at[number],
            )
            copy.start()
            leaving.append(copy)
        for copy in leaving:
            copy.wait()

    shape = (rows, total) if split else (groups if whole else inner, rows, total)
    lefts, rights = zip(*pairs)
    width = max(tile[4] for tile in tiles)
    return pl.pallas_call(
        kernel,
        out_shape=[jax.ShapeDtypeStruct(shape, HALF)] * results,
        in_specs=[SMEM] + [HBM] * (2 * count),
        out_specs=[HBM] * results,
        scratch_shapes=[pltpu.VMEM(left.shape, HALF) for left in lefts]
        + [
            pltpu.VMEM((len(tiles), max(left.shape[0] for left in lefts), width), HALF),
            pltpu.VMEM((len(tiles), rows, width), HALF),
            pltpu.SemaphoreType.DMA((count,)),
            pltpu.SemaphoreType.DMA((len(tiles),)),
            pltpu.SemaphoreType.DMA((len(tiles),)),
        ],
        compiler_params=pltpu.CompilerParams(vmem_limit_bytes=VMEM_BYTES),
        cost_estimate=cost(micros),
    )(place, *lefts, *rights)


def exchange(axis, bit):
    return (axis, [(index, index ^ bit) for index in range(lax.axis_size(axis))])


def swap(values, axis, bit):
    return lax.ppermute(values, *exchange(axis, bit))


def reduce_group(groups, path):
    others = yield [(send, exchange(TENSOR, 1)) for send, keep in groups]
    sums = [keep + other for (send, keep), other in zip(groups, others)]
    values = sums[0] if len(sums) == 1 else jnp.concatenate(sums, -1)
    columns = values.shape[-1]
    blocks = lax.axis_size(DP)
    far = blocks // 2
    place = lax.axis_index(DP)
    bits = {"x": lax.axis_index(TENSOR) // 2, "y": place % 2, "u": place // 2 % 2, "w": place // 4}
    ways = {
        "x": exchange(TENSOR, 2),
        "y": exchange(DP, 1),
        "u": exchange(DP, 2),
        "w": exchange(DP, 4),
    }
    if values.ndim == 3:
        values = values.reshape(2, 2, 2, 2, -1, columns)
        dims = "xwuy"
        bits["x"] = 0
    else:
        values = values.reshape(2, 2, 2, 2, -1, columns)
        dims = "wuyx"

    def side(array, left, axis, mine):
        bit = bits[axis] if mine else 1 - bits[axis]
        return lax.dynamic_index_in_dim(array, bit, left.index(axis), False)

    if path == "both":
        middle = columns // 2 // 128 * 128
        tracks = [[values[..., :middle], "xy"], [values[..., middle:], "yx"]]
        left = [dims, dims]
        for step in range(2):
            others = yield [
                (side(array, rest, way[step], False), ways[way[step]])
                for (array, way), rest in zip(tracks, left)
            ]
            tracks = [
                [side(array, rest, way[step], True) + other, way]
                for (array, way), rest, other in zip(tracks, left, others)
            ]
            left = [rest.replace(way[step], "") for (array, way), rest in zip(tracks, left)]
        values = jnp.concatenate([array for array, way in tracks], -1)
        dims = left[0]
        path = "uw"
    for axis in path:
        other = yield [(side(values, dims, axis, False), ways[axis])]
        values = side(values, dims, axis, True) + other[0]
        dims = dims.replace(axis, "")
    return values


def reduce_norms(values):
    count = lax.axis_size(DP)
    for axis, bit in ((TENSOR, 1), (TENSOR, 2), (DP, 1), (DP, 2), (DP, 4)):
        other = yield [(values, exchange(axis, bit))]
        values = values + other[0]
    lanes = values.shape[1] // count
    return lax.dynamic_slice_in_dim(values, lax.axis_index(DP) * lanes, lanes, 1)


def reduce_attention(groups, path, sizes):
    values = yield from reduce_group(groups, path)
    other = yield [(values, exchange(TENSOR, 2))]
    values = in_order(values, other[0], 2, 0)
    other = yield [(values, exchange(TENSOR, 1))]
    matrices = []
    begin = 0
    for size in sizes:
        end = begin + size // 2
        matrices.append(in_order(values[:, begin:end], other[0][:, begin:end], 1, 1).astype(FULL))
        begin = end
    return matrices


def in_order(values, other, bit, dim):
    first = lax.axis_index(TENSOR) // bit % 2 == 0
    return jnp.where(
        first,
        jnp.concatenate([values, other], dim),
        jnp.concatenate([other, values], dim),
    )


def reduce_far(parts):
    send, keep = parts
    other = yield [(send, exchange(TENSOR, 1))]
    values = keep + other[0]
    other = yield [(values[1], exchange(TENSOR, 2))]
    values = values[0] + other[0]
    values = values.reshape(-1, values.shape[-1])
    return lax.psum_scatter(values, DP, scatter_dimension=0, tiled=True).astype(FULL)


def reduce_whole(pairs):
    totals = []
    for left, right in pairs:
        total = lax.psum(dot_outer(left, right).astype(HALF), TENSOR)
        total = lax.psum_scatter(total, DP, scatter_dimension=0, tiled=True)
        totals.append(total.astype(FULL))
    return totals


class Flights:
    def __init__(self):
        self.running = {}
        self.results = {}
        self.asked = {}

    def start(self, name, steps):
        self.asked[name] = (steps, next(steps))

    def leave(self, values, names=None):
        asked = {name: self.asked.pop(name) for name in list(names or self.asked) if name in self.asked}
        sends = [[send for send, way in entry[1]] for entry in asked.values()]
        values, sends = lax.optimization_barrier((values, sends))
        for (name, (steps, entry)), ready in zip(asked.items(), sends):
            self.running[name] = (
                steps,
                [lax.ppermute(send, *way) for send, (unused, way) in zip(ready, entry)],
            )
        return values

    def land(self, names, values):
        names = [name for name in names if name in self.running]
        held = [self.running[name][1] for name in names]
        values, held = lax.optimization_barrier((values, held))
        for name, arrived in zip(names, held):
            steps = self.running.pop(name)[0]
            try:
                self.asked[name] = (steps, steps.send(arrived))
            except StopIteration as stop:
                self.results[name] = stop.value
        return values

    def turn(self, names, values):
        return self.leave(self.land(names, values), names)


def spread(pieces):
    return [pieces[0]] + [swap(piece, TENSOR, away) for away, piece in enumerate(pieces) if away]


def pass_on(values, way):
    arrived = yield [(values, way)]
    return arrived[0]


def both_matrices(hidden_up, hidden_down, layer, near):
    half = hidden_up.shape[1] // 2
    return jnp.stack(
        [
            lax.dynamic_slice_in_dim(matrices[layer], near * half, half, 0)
            for matrices in (hidden_up, hidden_down)
        ]
    )


def body(
    patch_tokens,
    class_tokens,
    frame_counts,
    patch_cotangent,
    class_cotangent,
    temporal_in,
    temporal_out,
    temporal_mix,
    spatial_in,
    spatial_out,
    hidden_up,
    hidden_down,
    norm_gain,
    norm_shift,
):
    frames, patches, width = patch_tokens.shape
    clips = class_tokens.shape[0]
    layers = temporal_in.shape[0]
    groups = lax.axis_size(TENSOR)
    place = jnp.stack([lax.axis_index(TENSOR), lax.axis_index(DP) % 2]).astype(jnp.int32)
    blocks_dp = lax.axis_size(DP)
    dims = (frames, patches, width, HEADS, groups)
    count = frames * patches
    rows = up_to(count + up_to(clips, 8), 80)
    spare = rows - count
    own_frames = frames // groups
    seq = groups * patches
    frame_span = up_to(seq + 1, 16)
    span = own_frames * frame_span
    hidden = groups * hidden_up.shape[2]
    piece_rows = own_frames * patches
    back_rows = up_to(piece_rows + 2 * own_frames, 16)

    ends = jnp.cumsum(frame_counts[0])
    frame_index = jnp.arange(frames, dtype=jnp.int32)
    clip_of = jnp.sum((frame_index[:, None] >= ends[None, :]).astype(jnp.int32), 1)
    clip_index = jnp.arange(spare, dtype=jnp.int32)
    member = (clip_index[:, None] == clip_of[None, :]).astype(FULL)
    counts = jnp.concatenate([frame_counts[0].astype(FULL), jnp.ones((spare - clips,), FULL)])
    share = member / counts[:, None]
    inverse_counts = 1.0 / counts
    row_index = jnp.arange(128, dtype=jnp.int32)
    row_clip = jnp.sum(
        jnp.where(row_index[:, None] % frames == frame_index[None, :], clip_of[None, :], 0), 1
    )
    same = jnp.logical_and(
        row_index[:, None] // frames == row_index[None, :] // frames,
        row_clip[:, None] == row_clip[None, :],
    )
    bias = jnp.where(same, 0.0, -1e30)

    def rows_of(patch, per_clip):
        return jnp.concatenate(
            [
                patch.reshape(count, width),
                per_clip,
                jnp.zeros((spare - clips, width), patch.dtype),
            ],
            0,
        ).astype(FULL)

    flights = Flights()
    near = lax.axis_index(DP) % 2
    gathered = [None] * layers
    by_core, by_x, by_y = exchange(TENSOR, 1), exchange(TENSOR, 2), exchange(DP, 1)

    def send(name, values, way):
        flights.start(name, pass_on(values, way))

    def arrived_here(name):
        return flights.results.pop(name)

    send("x0", both_matrices(hidden_up, hidden_down, 0, near), by_x)
    send("up", hidden_up, by_core)
    send("down", hidden_down, by_core)
    patch_rows = flights.leave(rows_of(patch_tokens, class_tokens))
    pieces_out = [((up_to(piece_rows, 16), width), HALF)] * groups
    backs_out = [((back_rows, width), HALF)] * groups
    lane_buffer = pltpu.VMEM((width // 128, rows, 128), FULL)
    row_buffer = pltpu.VMEM((rows, width), FULL)
    square = pltpu.VMEM((width, width), HALF)
    wide = pltpu.VMEM((width, 3 * width), HALF)
    shards = pltpu.VMEM((groups, width, width), HALF)
    blocks = pltpu.VMEM((groups, back_rows, width), FULL)
    frame_rows = pltpu.VMEM((frames, width), FULL)
    def time_step(layer, patch_rows):
        return step_of(
            partial(time_forward, dims, layer),
            [
                ((rows, width), HALF),
                ((rows, 3 * width), HALF),
                ((rows, 128), FULL),
                ((rows, width), HALF),
                ((rows, width), HALF),
                ((rows, width), FULL),
            ]
            + pieces_out
            + [((spare, width), FULL)],
            [wide, square, square, lane_buffer, row_buffer, blocks, pltpu.SemaphoreType.DMA((3,))],
            [SMALL, ROWS, ROWS, ROWS, ROWS, FAR, FAR, FAR],
            14,
        )(place, patch_rows, bias, norm_gain, norm_shift, temporal_in, temporal_out, temporal_mix)

    def feed_step(layer, arrived, after):
        return step_of(
            partial(feed_forward, dims, layer),
            [
                ((rows, width), HALF),
                ((rows, width), FULL),
                ((rows, width), HALF),
                ((rows, hidden), HALF),
                ((rows, hidden), HALF),
                ((rows, width), FULL),
            ],
            [
                square,
                shards,
                shards,
                row_buffer,
                blocks,
                frame_rows,
                pltpu.VMEM((rows, width), HALF),
                pltpu.SemaphoreType.DMA((1,)),
                pltpu.SemaphoreType.DMA((12,)),
            ],
            [SMALL] + [ROWS] * groups + [ROWS] * 4 + [FAR] * 9,
            15,
        )(
            place, *arrived, share, after, norm_gain, norm_shift, spatial_out,
            hidden_up, hidden_down, *gathered[layer],
        )

    def feed_back_step(layer, grad_rows, slope, rows_in):
        return step_of(
            partial(feed_backward, dims, layer),
            [
                ((rows, width), HALF),
                ((rows, hidden), HALF),
                ((rows, width), HALF),
                ((rows, width), FULL),
                ((8, width), FULL),
            ]
            + pieces_out
            + [((8, width), FULL)],
            [
                square,
                shards,
                shards,
                row_buffer,
                row_buffer,
                blocks,
                pltpu.SemaphoreType.DMA((1,)),
                pltpu.SemaphoreType.DMA((12,)),
            ],
            [SMALL, SMALL] + [ROWS] * 5 + [FAR] * 9,
            23,
        )(
            place, clip_of, grad_rows, slope, rows_in,
            jnp.broadcast_to(inverse_counts[:, None], (spare, 128)), norm_gain, spatial_out,
            hidden_up, hidden_down, *gathered[layer],
        )

    def time_back_step(layer, arrived, back, time, start_rows):
        return step_of(
            partial(time_backward, dims, layer),
            [
                ((rows, width), HALF),
                ((rows, width), HALF),
                ((rows, 3 * width), HALF),
                ((rows, width), FULL),
                ((8, width), FULL),
            ],
            [
                wide,
                square,
                square,
                lane_buffer,
                row_buffer,
                blocks,
                frame_rows,
                pltpu.VMEM((rows, width), HALF),
                pltpu.SemaphoreType.DMA((3,)),
            ],
            [SMALL] + [ROWS] * groups + [ROWS] * 8 + [FAR] * 3,
            14,
        )(
            place, *arrived, member, back, time[5], start_rows, time[1], time[2], bias,
            norm_gain, temporal_in, temporal_out, temporal_mix,
        )

    saved = []
    time = call_steps(time_step(0, patch_rows))
    for layer in range(layers):
        pieces = time[6:10]
        if layer:
            pieces = flights.land(["x1"], pieces)
            first = arrived_here("x1")
            send("y1", first, by_y)
            pieces = flights.leave(pieces)
        arrived = spread(pieces)
        if layer == 0:
            arrived = flights.land(("x0", "up", "down"), arrived)
            core_shards = (arrived_here("up"), arrived_here("down"))
            first = arrived_here("x0")
            send("y0", first, by_y)
            arrived, later_near, cotangent = lax.optimization_barrier(
                (arrived, near, patch_cotangent)
            )
            send("x1", both_matrices(hidden_up, hidden_down, 1, later_near), by_x)
            grad_rows = rows_of(cotangent, class_cotangent)
        arrived = flights.leave(arrived)
        space = call(
            partial(space_forward, dims, layer),
            [((span, width), HALF), ((span, 3 * width), HALF), ((span, 128), FULL)] + backs_out,
            [wide, pltpu.VMEM((span, width), FULL), pltpu.SemaphoreType.DMA((1,))],
            [SMALL, SMALL, ROWS] + [ROWS] * groups + [FAR],
            9,
        )(place, clip_of, time[10], *arrived, spatial_in)
        arrived = spread(space[3:])
        arrived = flights.land([f"y{layer}"], arrived)
        second = arrived_here(f"y{layer}")
        send("first", first, by_core)
        send("second", second, by_core)
        arrived = flights.leave(arrived)
        arrived = flights.land(("first", "second"), arrived)
        gathered[layer] = (
            *core_shards,
            first,
            second,
            arrived_here("first"),
            arrived_here("second"),
        )
        step = feed_step(layer, arrived, time[5])
        if layer + 1 < layers:
            feed, later = call_steps(step, time_step(layer + 1, Result(5)))
        else:
            feed, later = call_steps(
                step, feed_back_step(layer, grad_rows, Result(4), Result(1))
            )
        saved.append((patch_rows, time, space, feed))
        patch_rows = feed[5]
        time = later
    feed_back = later
    patch_output = patch_rows[:count].reshape(frames, patches, width).astype(HALF)
    class_output = patch_rows[count : count + clips].astype(HALF)

    usual = blocks_dp == 2 * NEAR
    norms = [None] * layers

    def outer(pairs, split, micros):
        return outer_group(place, pairs, groups, split, micros)

    def start(name, pairs, path, split, micros, first=()):
        pairs = tuple(pairs)
        if split and not usual:
            flights.results[name] = reduce_whole([pair for early in first for pair in early[0]] + list(pairs))
            return
        parts = [early[1] for early in first] + [outer(pairs, split, micros)]
        if split:
            sizes = []
            for own in [early[0] for early in first] + [pairs]:
                sizes.append([right.shape[1] for left, right in own])
            flights.start(name, reduce_attention(parts, path, sum(sizes, [])))
        elif usual:
            flights.start(name, reduce_group(parts, path))
        else:
            flights.start(name, reduce_far(parts[0]))

    for layer in reversed(range(layers)):
        start_rows, time, space, feed = saved[layer]
        last = layer == 0
        update, grad_hidden, branch, back, feed_norms = feed_back[:5]
        arrived = spread(feed_back[5:9])
        pairs = ((feed[2], grad_hidden), (update, feed[3]))
        if last:
            pairs = flights.turn(["feed1"], pairs)
            time_pairs = lax.optimization_barrier((time_pairs, pairs))[0]
            start("attention1", time_pairs, "both", True, 9, [early])
            pairs = flights.leave(pairs, ["attention1"])
            start("feed0", pairs, "both", False, 10)
            arrived, feed_sum = lax.optimization_barrier((arrived, feed_sum))
            feed_sum = lax.psum_scatter(feed_sum, DP, scatter_dimension=0, tiled=True)
            arrived = flights.turn(["feed1", "attention1"], arrived)
        else:
            total = outer_group(place, pairs, groups, False, 10, True)[0]
            arrived, total = lax.optimization_barrier((arrived, total))
            total = total.reshape(-1, total.shape[-1])
            feed_sum = lax.psum_scatter(total, TENSOR, scatter_dimension=0, tiled=True)
        arrived = flights.leave(arrived)
        space_back = call(
            partial(space_backward, dims, layer),
            [((span, 3 * width), HALF)] + backs_out,
            [
                wide,
                pltpu.VMEM((span, width), FULL),
                pltpu.VMEM((span, width), HALF),
                pltpu.SemaphoreType.DMA((1,)),
            ],
            [ROWS] * groups + [ROWS] * 3 + [FAR],
            29,
        )(*arrived, feed_back[9], space[1], space[2], spatial_in)
        pieces = space_back[1:]
        if last:
            pieces = flights.land(["feed1", "feed0"], pieces)
        arrived = spread(pieces)
        pairs = ((space[0], space_back[0]), (feed[0], branch))
        if last:
            start("space0", pairs, "xyuw", True, 8)
            arrived = flights.land(["attention1"], arrived)
            arrived = flights.leave(arrived)
        else:
            pairs = flights.turn(["feed1"], pairs)
            if usual:
                early = (pairs, outer(pairs, True, 8))
                arrived, parts = lax.optimization_barrier((arrived, early[1]))
                early = (pairs, parts)
            else:
                early = (pairs, None)
        step = time_back_step(layer, arrived, back, time, start_rows)
        if last:
            time_back = call_steps(step)
        else:
            ahead = saved[layer - 1][3]
            time_back, later = call_steps(
                step, feed_back_step(layer - 1, Result(3), ahead[4], ahead[1])
            )
        grad_rows = time_back[3]
        norms[layer] = (time_back[4], feed_norms)
        pairs = ((time[0], time_back[2]), (time[3], time_back[1]), (time[4], time_back[0]))
        if last:
            ordered = [
                entry[at : at + 1]
                for part, at in ((0, 2), (0, 0), (1, 0), (0, 3), (0, 1), (1, 1))
                for entry in [norms[index][part] for index in range(layers)]
            ]
            ordered = jnp.concatenate(ordered, 0)
            if usual:
                flights.start("norms", reduce_norms(ordered))
            else:
                total = lax.psum(ordered, TENSOR)
                flights.results["norms"] = lax.psum_scatter(
                    total, DP, scatter_dimension=1, tiled=True
                )
            start("time0", pairs, "both", True, 9)
            token = grad_rows[count : count + clips]
            token = flights.leave(token, ["time0"])
            token, flights.results["feed1"] = lax.optimization_barrier((token, feed_sum))
        else:
            time_pairs = pairs
            feed_back = later
    for names in (
        ("attention1", "feed0", "space0"),
        ("attention1", "feed0", "time0", "norms"),
        ("space0", "time0", "norms"),
        ("attention1", "feed0"),
        ("space0", "time0", "norms"),
        ("attention1", "feed0"),
        ("space0", "time0", "norms"),
        ("attention1",),
        ("space0", "time0", "norms"),
        ("space0", "time0"),
    ):
        token = flights.turn(names, token)
    while flights.running:
        token = flights.turn(list(flights.running), token)
    results = flights.results
    lanes = width // blocks_dp

    norm_sums = results["norms"].reshape(2, 3, layers, lanes).transpose(0, 2, 1, 3)
    feeds = (results["feed0"], results["feed1"])
    late = results["attention1"]
    time_sums = (results["time0"], late[2:])
    space_sums = (results["space0"], late[:2])
    gradients = (
        *[jnp.stack([sums[index] for sums in time_sums]) for index in range(3)],
        *[jnp.stack([sums[index] for sums in space_sums]) for index in range(2)],
        jnp.stack([sums[:, :width].astype(FULL) for sums in feeds]),
        jnp.stack([sums[:, width:].T.astype(FULL) for sums in feeds]),
        norm_sums[0],
        norm_sums[1],
    )
    patch_grad = grad_rows[:count].reshape(frames, patches, width)
    class_grad = token
    return (patch_output, class_output, patch_grad, class_grad, *gradients)


def solution(mesh):
    placed = (
        P(DP, TENSOR, None),
        P(DP, None),
        P(DP, None),
        P(DP, TENSOR, None),
        P(DP, None),
        P(),
        P(),
        P(),
        P(),
        P(),
        P(None, None, TENSOR),
        P(None, TENSOR, None),
        P(),
        P(),
    )
    return jax.shard_map(
        body,
        mesh=mesh,
        in_specs=placed,
        out_specs=(
            P(DP, TENSOR, None),
            P(DP, None),
            P(DP, TENSOR, None),
            P(DP, None),
            P(None, DP, None),
            P(None, DP, None),
            P(None, DP, None),
            P(None, DP, None),
            P(None, DP, None),
            P(None, DP, TENSOR),
            P(None, TENSOR, DP),
            P(None, None, DP),
            P(None, None, DP),
        ),
        check_vma=False,
    )
```
